32 devices in a mesh: ctx: 8 (over z, core), fsdp: 4 (over y, x).
Axes of the slice: x: 2, y: 2, z: 4, core: 2. Of those that a mesh axis runs over, the one named last changes fastest.
Arguments:
- inputs: bfloat16 [2, 4, 1024, 1536], P(None, 'fsdp', 'ctx'), may hold values from -6 to 6
- cotangent: bfloat16 [2, 4, 1024, 1536], P(None, 'fsdp', 'ctx'), may hold values from -6 to 6
- lengths: int32 [2, 4, 4], P(None, 'fsdp'), may hold values from 1 to 512, 1024 in all within a row
- deal: int32 [2, 8], replicated, may hold values from 0 to 7, each once within a row
- norm1_gain: bfloat16 [1536], P(('ctx', 'fsdp')), may hold values from 0.5 to 1.5
- w_query: bfloat16 [1536, 1536], P(('ctx', 'fsdp')), may hold values from -0.15625 to 0.15625
- w_key: bfloat16 [1536, 1536], P(('ctx', 'fsdp')), may hold values from -0.15625 to 0.15625
- w_value: bfloat16 [1536, 1536], P(('ctx', 'fsdp')), may hold values from -0.15625 to 0.15625
- w_outgate: bfloat16 [1536, 1536], P(('ctx', 'fsdp')), may hold values from -0.15625 to 0.15625
- w_out: bfloat16 [1536, 1536], P(('ctx', 'fsdp')), may hold values from -1.25 to 1.25
- forget_weight: bfloat16 [1536, 24], P(('ctx', 'fsdp')), may hold values from -0.15625 to 0.15625
- forget_bias: float32 [24], replicated, may hold values from 2 to 9
- norm2_gain: bfloat16 [1536], P(('ctx', 'fsdp')), may hold values from 0.5 to 1.5
- w_gate: bfloat16 [1536, 4096], P(('ctx', 'fsdp')), may hold values from -0.15625 to 0.15625
- w_up: bfloat16 [1536, 4096], P(('ctx', 'fsdp')), may hold values from -0.15625 to 0.15625
- w_down: bfloat16 [4096, 1536], P(('ctx', 'fsdp')), may hold values from -0.09375 to 0.09375
Outputs:
- output: bfloat16 [2, 4, 1024, 1536], P(None, 'fsdp', 'ctx')
- grad_inputs: float32 [2, 4, 1024, 1536], P(None, 'fsdp', 'ctx')
- grad_norm1_gain: float32 [1536], P(('ctx', 'fsdp'))
- grad_w_query: float32 [1536, 1536], P(('ctx', 'fsdp'))
- grad_w_key: float32 [1536, 1536], P(('ctx', 'fsdp'))
- grad_w_value: float32 [1536, 1536], P(('ctx', 'fsdp'))
- grad_w_outgate: float32 [1536, 1536], P(('ctx', 'fsdp'))
- grad_w_out: float32 [1536, 1536], P(('ctx', 'fsdp'))
- grad_forget_weight: float32 [1536, 24], P(('ctx', 'fsdp'))
- grad_forget_bias: float32 [24], replicated
- grad_norm2_gain: float32 [1536], P(('ctx', 'fsdp'))
- grad_w_gate: float32 [1536, 4096], P(('ctx', 'fsdp'))
- grad_w_up: float32 [1536, 4096], P(('ctx', 'fsdp'))
- grad_w_down: float32 [4096, 1536], P(('ctx', 'fsdp'))
The draws below stay inside these ranges and needn't reach their ends.
Inputs may be any that keep to these rules, and one draw needn't show every extreme that they name: Each row of lengths holds the 4 document lengths of one stream, summing to 1024, the longest exactly 512. Each row of deal is a permutation of the block pairs.
All inputs are finite; a program needn't handle non-finite values.
Results may differ from the reference program's by a relative error of at most 0.025.
Values may be sent and summed in bfloat16 or wider, within the bound.
No kernel may reach another device: no remote copies, remote signals or barrier semaphores. Data moves between devices by JAX's collectives and lax.ppermute only.
A program may use at most 384 MiB of HBM per device.

```python
import math
import jax
import jax.numpy as jnp
import numpy as np
from jax import lax

D = 1536
H = 24
HD = 64
FF = 4096
MB = 2
NDOC = 4
KEY_TILE = 512
SEQ = 1024
GROUPS = 4
N_CTX = 8


def level_of(own_key, shape, split, low, top_value):
    level, own = 1.0, jax.random.fold_in(own_key, 6)
    for position, parts in split:
        heights = jnp.exp(jax.random.uniform(jax.random.fold_in(own, position), (parts,), jnp.float32, low / len(split), top_value / len(split)))
        level = level * jnp.repeat(heights, shape[position] // parts).reshape([-1 if axis == position else 1 for axis in range(len(shape))])
    return level


def profile(number_of, total, most, lean):
    weights = [(1 << 20) // math.isqrt(rank ** lean) + 1 for rank in range(2, number_of + 1)]
    spare, counts = total - most - (number_of - 1), [1] * (number_of - 1)
    while spare > 0:
        candidates = [i for i in range(number_of - 1) if counts[i] < most]
        mass, left = sum([weights[i] for i in candidates]), spare
        for i in candidates:
            more = min(most - counts[i], max(1, left * weights[i] // mass), spare)
            counts[i] = counts[i] + more
            spare = spare - more
    return np.array([most] + counts)


def uneven_parts(own_key, count, total, most, skew):
    if count == 2:
        one = jax.random.randint(own_key, (), max(1, total - most), min(most, total - 1) + 1)
        return jnp.stack([one, total - one])
    sizes = jnp.asarray(profile(count, total, most, skew), jnp.int32)
    twos = (count - 1) // 2
    source_of, taker = sizes[1:1 + 2 * twos:2], sizes[2:2 + 2 * twos:2]
    slack = jnp.minimum(source_of - 1, most - taker)
    moved = jax.random.randint(jax.random.fold_in(own_key, 1), (twos,), 0, 1 << 20) % (slack + 1)
    sizes = sizes.at[1:1 + 2 * twos:2].set(source_of - moved).at[2:2 + 2 * twos:2].set(taker + moved)
    return sizes[jax.random.permutation(jax.random.fold_in(own_key, 2), count)]


def scatter_about(own_key, extent, scale, reach, cuts=(), held_as=jnp.bfloat16):
    loudness = level_of(own_key, extent, cuts, -0.22, 0.18) if cuts else 1.0
    values = jax.random.normal(own_key, extent, jnp.float32) * scale * loudness
    return jnp.minimum(jnp.maximum(values, -reach), reach).astype(held_as)


def setup_inputs(seed: int = 0) -> dict:
    splits = jax.random.split(jax.random.key(seed), 17)
    inputs = scatter_about(splits[0], (MB, GROUPS, SEQ, D), 1.0, 6.0, ((1, 4), (2, 8)))
    cotangent = scatter_about(splits[1], (MB, GROUPS, SEQ, D), 1.0, 6.0, ((1, 4), (2, 8)))
    lengths = jax.vmap(lambda own: uneven_parts(own, NDOC, SEQ, SEQ // 2, 2))(jax.random.split(splits[2], MB * GROUPS)).reshape((MB, GROUPS, NDOC)).astype(jnp.int32)
    deal = jax.vmap(lambda own: jax.random.permutation(own, N_CTX))(jax.random.split(splits[3], MB)).reshape((MB, N_CTX)).astype(jnp.int32)
    norm1_gain = jnp.clip(1.0 + 0.1 * jax.random.normal(splits[4], (D,), jnp.float32), 0.5, 1.5).astype(jnp.bfloat16)
    w_query = scatter_about(splits[5], (D, D), D ** -0.5, 0.15625, ((0, 32),))
    w_key = scatter_about(splits[6], (D, D), D ** -0.5, 0.15625, ((0, 32),))
    w_value = scatter_about(splits[7], (D, D), D ** -0.5, 0.15625, ((0, 32),))
    w_outgate = scatter_about(splits[8], (D, D), D ** -0.5, 0.15625, ((0, 32),))
    w_out = scatter_about(splits[9], (D, D), (D // 64) ** -0.5, 1.25, ((0, 32),))
    forget_weight = scatter_about(splits[10], (D, H), D ** -0.5, 0.15625, ((0, 32),))
    forget_bias = jnp.clip(jax.random.uniform(splits[11], (H,), jnp.float32, 2.0, 9.0), 2.0, 9.0)
    norm2_gain = jnp.clip(1.0 + 0.1 * jax.random.normal(splits[12], (D,), jnp.float32), 0.5, 1.5).astype(jnp.bfloat16)
    w_gate = scatter_about(splits[13], (D, FF), D ** -0.5, 0.15625, ((0, 32),))
    w_up = scatter_about(splits[14], (D, FF), D ** -0.5, 0.15625, ((0, 32),))
    w_down = scatter_about(splits[15], (FF, D), FF ** -0.5, 0.09375, ((0, 32),))
    return dict(inputs=inputs, cotangent=cotangent, lengths=lengths, deal=deal, norm1_gain=norm1_gain, w_query=w_query, w_key=w_key, w_value=w_value, w_outgate=w_outgate, w_out=w_out, forget_weight=forget_weight, forget_bias=forget_bias, norm2_gain=norm2_gain, w_gate=w_gate, w_up=w_up, w_down=w_down)


@jax.custom_vjp
def low(v):
    return lax.optimization_barrier(v.astype(jnp.bfloat16)).astype(jnp.float32)

@jax.custom_vjp
def low_back(v):
    return v

def low_keep(v):
    return (low(v), None)

def low_pass(kept, grad):
    return (grad,)

def back_keep(v):
    return (v, None)

def back_low(kept, grad):
    return (low(grad),)
low.defvjp(low_keep, low_pass)
low_back.defvjp(back_keep, back_low)
norm_eps = 1e-06
very_low = -1e+30

def product(left, right):
    return jnp.dot(left, right, precision=lax.Precision.HIGHEST)

def doc_begins(lengths_row, total):
    ends = jnp.cumsum(lengths_row).astype(jnp.int32)
    begins = (ends - lengths_row).astype(jnp.int32)
    place = jnp.arange(total, dtype=jnp.int32)
    inside = (place[:, None] >= begins[None, :]) & (place[:, None] < ends[None, :])
    return lax.optimization_barrier(jnp.sum(jnp.where(inside, begins[None, :], 0), axis=1)).astype(jnp.int32)

def slot_order(deal_row, count):
    return jnp.stack([deal_row, 2 * count - 1 - deal_row], axis=1).reshape(-1).astype(jnp.int32)

def into_natural(array, order):
    count = order.shape[0]
    numbers = jnp.arange(count, dtype=jnp.int32)
    source = lax.optimization_barrier(jnp.sum(jnp.where(order[None, :] == numbers[:, None], numbers[None, :], 0), axis=1)).astype(jnp.int32)
    blocks = array.reshape((count, array.shape[0] // count) + array.shape[1:])
    return jnp.take(blocks, source, axis=0).reshape(array.shape)

def into_slots(array, order):
    count = order.shape[0]
    blocks = array.reshape((count, array.shape[0] // count) + array.shape[1:])
    return jnp.take(blocks, order, axis=0).reshape(array.shape)

def rms_norm(values, gain):
    return values * lax.rsqrt(lax.optimization_barrier(jnp.mean(values * values, axis=-1, keepdims=True)) + norm_eps) * gain

def attention(queries, keys, values, cumul, begins):
    total = queries.shape[0]
    place = jnp.arange(total, dtype=jnp.int32)
    scale = HD ** (-0.5)

    def one_tile(number):
        first = number * KEY_TILE
        tile_query = lax.dynamic_slice_in_dim(queries, first, KEY_TILE, 0)
        tile_cumul = lax.dynamic_slice_in_dim(cumul, first, KEY_TILE, 0)
        tile_place = lax.dynamic_slice_in_dim(place, first, KEY_TILE, 0)
        tile_begin = lax.dynamic_slice_in_dim(begins, first, KEY_TILE, 0)
        scores = jnp.einsum('rhd,thd->hrt', tile_query, keys, precision=lax.Precision.HIGHEST) * scale
        scores = scores + tile_cumul.T[:, :, None] - cumul.T[:, None, :]
        scores = low_back(scores)
        mask = (place[None, :] <= tile_place[:, None]) & (place[None, :] >= tile_begin[:, None])
        masked = jnp.where(mask[None], scores, very_low)
        peak = lax.optimization_barrier(jnp.max(masked, axis=2, keepdims=True))
        weights = jnp.exp(masked - peak)
        probs = low(weights / lax.optimization_barrier(jnp.sum(weights, axis=2, keepdims=True)))
        return jnp.einsum('hrt,thd->rhd', probs, values, precision=lax.Precision.HIGHEST)
    tiles = lax.map(jax.checkpoint(one_tile), jnp.arange(total // KEY_TILE, dtype=jnp.int32))
    return tiles.reshape(total, queries.shape[1] * queries.shape[2])

def stream_layer(stream_slots, lengths_row, deal_row, params):
    gain_one, w_query, w_key, w_value, w_outgate, w_out, forget_weight, forget_bias, gain_two, w_gate, w_up, w_down = params
    order = slot_order(deal_row, N_CTX)
    stream = into_natural(stream_slots, order)
    normed = low(rms_norm(stream, gain_one))
    queries = low_back(low(product(normed, w_query)))
    keys = low_back(low(product(normed, w_key)))
    values = low_back(low(product(normed, w_value)))
    outgate = low_back(product(normed, w_outgate))
    forget = low(jax.nn.log_sigmoid(product(normed, forget_weight) + forget_bias))
    cumul = jnp.cumsum(forget, axis=0)
    begins = doc_begins(lengths_row, SEQ)
    attended = attention(queries.reshape(SEQ, H, HD), keys.reshape(SEQ, H, HD), values.reshape(SEQ, H, HD), cumul, begins)
    attended = low_back(attended)
    gated = low(attended * jax.nn.sigmoid(outgate))
    middle = stream + low_back(product(gated, w_out))
    normed_two = low(rms_norm(middle, gain_two))
    gate_pre = low_back(product(normed_two, w_gate))
    up_pre = low_back(product(normed_two, w_up))
    activ = low(jax.nn.silu(gate_pre) * up_pre)
    result = middle + low_back(product(activ, w_down))
    return into_slots(result, order)

def reference(inputs, cotangent, lengths, deal, norm1_gain, w_query, w_key, w_value, w_outgate, w_out, forget_weight, forget_bias, norm2_gain, w_gate, w_up, w_down):
    params = tuple((item.astype(jnp.float32) for item in (norm1_gain, w_query, w_key, w_value, w_outgate, w_out, forget_weight, forget_bias, norm2_gain, w_gate, w_up, w_down)))
    count = MB * GROUPS
    streams = inputs.astype(jnp.float32).reshape(count, SEQ, D)
    lengths_all = lengths.reshape(count, NDOC).astype(jnp.int32)
    deals = jnp.repeat(deal, GROUPS, axis=0).astype(jnp.int32)
    layer_call = jax.checkpoint(stream_layer)

    def forward(streams_in, params_in):

        def one(carry, item):
            return (carry, layer_call(item[0], item[1], item[2], params_in))
        unused, results = lax.scan(one, jnp.zeros((), jnp.float32), (streams_in, lengths_all, deals))
        return results
    results, pullback = jax.vjp(forward, streams, params)
    stream_grads, grads = pullback(cotangent.astype(jnp.float32).reshape(count, SEQ, D))
    shape = (MB, GROUPS, SEQ, D)
    return (results.reshape(shape).astype(jnp.bfloat16), stream_grads.reshape(shape), grads[0], grads[1], grads[2], grads[3], grads[4], grads[5], grads[6], grads[7], grads[8], grads[9], grads[10], grads[11])
```

```python
import functools

import jax
import jax.numpy as jnp
from jax import lax
from jax.experimental import pallas as pl
from jax.experimental.pallas import tpu as pltpu
from jax.sharding import Mesh, PartitionSpec as P

EPS = 1e-06
LOW = -1e30
BQ = 256
F32 = jnp.float32
BF16 = jnp.bfloat16
VMEM_LIMIT = 56 * 1024 * 1024


def dot(left, right, contract=((1,), (0,)), out=F32):
    return lax.dot_general(left, right, (contract, ((), ())), preferred_element_type=out)


def xor_permute(x, axis, step):
    n = lax.axis_size(axis)
    return lax.ppermute(x, axis, [(i, i ^ step) for i in range(n)])


def pick(stacked, index):
    return lax.dynamic_index_in_dim(stacked, index, 0, keepdims=False)


def rows_to_group(x):
    np_, nz = lax.axis_size("p"), lax.axis_size("z")
    p, z = lax.axis_index("p"), lax.axis_index("z")
    micro, tokens, width = x.shape
    rp = tokens // np_
    parts = x.reshape(micro, np_, rp, width).transpose(1, 0, 2, 3)
    got = [pick(parts, p)]
    for k in range(1, np_):
        got.append(xor_permute(pick(parts, p ^ k), "p", k))
    got = jnp.stack(got).reshape(np_ * micro, rp, width)

    def for_layer(target):
        m, ps = target // np_, target % np_
        return pick(got, (p ^ ps) * micro + m)

    rows = [for_layer(z)]
    for k in range(1, nz):
        rows.append(xor_permute(for_layer(z ^ k), "z", k))
    return jnp.concatenate(rows, axis=0)


def rows_from_group(y, micro):
    np_, nz = lax.axis_size("p"), lax.axis_size("z")
    p, z = lax.axis_index("p"), lax.axis_index("z")
    width = y.shape[1]
    rp = y.shape[0] // nz
    parts = y.reshape(nz, rp, width)
    got = [parts[0]]
    for k in range(1, nz):
        got.append(xor_permute(parts[k], "z", k))
    got = jnp.stack(got)

    def for_place(target):
        return jnp.stack([pick(got, z ^ (m * np_ + target)) for m in range(micro)])

    back = [for_place(p)]
    for k in range(1, np_):
        back.append(xor_permute(for_place(p ^ k), "p", k))
    back = jnp.stack(back)
    return jnp.stack([pick(back, p ^ c) for c in range(np_)], axis=1).reshape(micro, np_ * rp, width)


def gather_heads(x):
    np_ = lax.axis_size("p")
    own = [x] + [xor_permute(x, "p", k) for k in range(1, np_)]
    other = [xor_permute(block, "core", 1) for block in own]
    return jnp.concatenate(own + other, axis=0)


def scatter_heads(partial):
    np_ = lax.axis_size("p")
    rows = partial.shape[0] // 2
    low = partial.astype(BF16)
    got = xor_permute(low[rows:], "core", 1)
    total = partial[:rows] + got.astype(F32)
    total = total.reshape(np_, rows // np_, -1)
    out = total[0]
    for k in range(1, np_):
        out = out + xor_permute(total[k].astype(BF16), "p", k).astype(F32)
    return out


def gather_plane(x):
    np_ = lax.axis_size("p")
    half = x.shape[0] // 2
    over_q = xor_permute(x, "q", 1)
    if np_ == 2:
        over_p = xor_permute(x, "p", 1)
        diagonal = [xor_permute(over_q[:half], "p", 1), xor_permute(over_p[half:], "q", 1)]
        own = [x, over_q, over_p, jnp.concatenate(diagonal, axis=0)]
    else:
        own = [x, over_q]
        for k in range(1, np_):
            own += [xor_permute(x, "p", k), xor_permute(over_q, "p", k)]
    other = [xor_permute(block, "core", 1) for block in own]
    return jnp.concatenate(own + other, axis=0)


def scatter_plane(partial):
    np_ = lax.axis_size("p")
    rows = partial.shape[0] // 2
    low = partial.astype(BF16)
    got = xor_permute(low[rows:], "core", 1)
    total = partial[:rows] + got.astype(F32)
    total = total.reshape(np_, 2, rows // np_ // 2, -1)
    if np_ == 2:
        half = total.shape[2] // 2
        diagonal = total[1, 1].astype(BF16)
        into_q = xor_permute(diagonal[:half], "p", 1)
        into_p = xor_permute(diagonal[half:], "q", 1)
        to_q = jnp.concatenate([total[0, 1, :half] + into_q.astype(F32), total[0, 1, half:]], axis=0)
        to_p = jnp.concatenate([total[1, 0, :half], total[1, 0, half:] + into_p.astype(F32)], axis=0)
        over_q = xor_permute(to_q.astype(BF16), "q", 1)
        over_p = xor_permute(to_p.astype(BF16), "p", 1)
        return total[0, 0] + over_q.astype(F32) + over_p.astype(F32)
    pair = total[0]
    for k in range(1, np_):
        pair = pair + xor_permute(total[k].astype(BF16), "p", k).astype(F32)
    return pair[0] + xor_permute(pair[1].astype(BF16), "q", 1).astype(F32)


def lanes_of(rows, width, head, depth):
    lane = lax.broadcasted_iota(jnp.int32, (rows, width), 1)
    return (lane >= head * depth) & (lane < (head + 1) * depth)


def log_sigmoid(z):
    return jnp.minimum(z, 0.0) - jnp.log(1.0 + jnp.exp(-jnp.abs(z)))


def to_natural(table, source, target, chunk):
    for n in range(target.shape[0] // chunk):
        place = pl.multiple_of(table[n] * chunk, chunk)
        target[pl.ds(n * chunk, chunk), :] = source[pl.ds(place, chunk), :].astype(target.dtype)


def from_natural(table, source, target, chunk):
    for n in range(source.shape[0] // chunk):
        place = pl.multiple_of(table[n] * chunk, chunk)
        target[pl.ds(place, chunk), :] = source[pl.ds(n * chunk, chunk), :].astype(target.dtype)


def attend_kernel(
    chunk, depth, table, q_ref, k_ref, v_ref, g_ref, z_ref, bias_ref, begin_ref,
    a_ref, b_ref, total_ref, cumul_ref,
    qn, kn, vn, an, cumul_rows,
):
    group = pl.program_id(0)
    total, width = q_ref.shape
    per_group = width // depth
    bq = min(BQ, total)
    window = total // 2

    @pl.when(group == 0)
    def _():
        logs = an
        lower = (
            lax.broadcasted_iota(jnp.int32, (bq, bq), 0) >= lax.broadcasted_iota(jnp.int32, (bq, bq), 1)
        ).astype(F32).astype(BF16)
        for n in range(total // chunk):
            place = pl.multiple_of(table[n] * chunk, chunk)
            logs[pl.ds(n * chunk, chunk), 0:128] = log_sigmoid(z_ref[pl.ds(place, chunk), :] + bias_ref[...])
        carry = jnp.zeros((1, 128), F32)
        for i in range(total // bq):
            part = dot(lower, logs[i * bq:(i + 1) * bq, 0:128].astype(BF16)) + carry
            cumul_ref[i * bq:(i + 1) * bq, :] = part
            carry = part[bq - 1:bq, :]
        cumul_rows[...] = jnp.transpose(cumul_ref[...])
        total_ref[...] = jnp.zeros_like(total_ref)

    to_natural(table, q_ref, qn, chunk)
    to_natural(table, k_ref, kn, chunk)
    to_natural(table, v_ref, vn, chunk)
    lane = lax.broadcasted_iota(jnp.int32, (bq, 128), 1)
    for i in range(total // bq):
        first = max(0, i * bq - window)
        span = (i + 1) * bq - first
        place = i * bq + lax.broadcasted_iota(jnp.int32, (bq, span), 0)
        other = first + lax.broadcasted_iota(jnp.int32, (bq, span), 1)
        begin = begin_ref[i * bq:(i + 1) * bq, :]
        bias = jnp.where((other <= place) & (other >= begin), 0.0, LOW)
        q_tile = qn[i * bq:(i + 1) * bq, :] * jnp.asarray(depth ** -0.5, BF16)
        keys = kn[first:first + span, :]
        values = jnp.concatenate([vn[first:first + span, :], jnp.ones((span, width), BF16)], axis=1)
        out = jnp.zeros((bq, width), F32)
        totals = total_ref[i * bq:(i + 1) * bq, :]
        for h in range(per_group):
            head = group * per_group + h
            mine = lanes_of(bq, width, h, depth)
            score = dot(jnp.where(mine, q_tile, jnp.zeros_like(q_tile)), keys, ((1,), (1,)))
            score = score - cumul_rows[pl.ds(head, 1), first:first + span] + bias
            peak = jnp.max(score, axis=1, keepdims=True)
            weight = jnp.exp(score - peak)
            both = dot(weight.astype(BF16), values)
            weight_sum = both[:, width:]
            out = jnp.where(mine, both[:, :width] / weight_sum, out)
            totals = jnp.where(lane == head, peak + jnp.log(weight_sum[:, 0:128]), totals)
        an[i * bq:(i + 1) * bq, 0:width] = out
        total_ref[i * bq:(i + 1) * bq, :] = totals
    for n in range(total // chunk):
        place = pl.multiple_of(table[n] * chunk, chunk)
        part = an[pl.ds(n * chunk, chunk), 0:width]
        a_ref[pl.ds(place, chunk), :] = part
        b_ref[pl.ds(place, chunk), :] = (part * jax.nn.sigmoid(g_ref[pl.ds(place, chunk), :])).astype(BF16)


def attend_back_kernel(
    chunk, depth, heads, table, q_ref, k_ref, v_ref, g_ref, a_ref, db_ref, total_ref, cumul_ref, z_ref,
    bias_ref, begin_ref,
    dq_ref, dk_ref, dv_ref, dg_ref, dz_ref, dbias_ref,
    qn, kn, vn, dan, delta, rows, total_rows, dqn, dkn, dvn, dcumul,
):
    group = pl.program_id(0)
    total, width = q_ref.shape
    per_group = width // depth
    bq = min(BQ, total)
    window = total // 2
    lane = lax.broadcasted_iota(jnp.int32, (bq, 128), 1)

    @pl.when(group == 0)
    def _():
        total_rows[...] = jnp.transpose(total_ref[...])
        dcumul[...] = jnp.zeros_like(dcumul)

    to_natural(table, q_ref, qn, chunk)
    to_natural(table, k_ref, kn, chunk)
    to_natural(table, v_ref, vn, chunk)
    small = lax.broadcasted_iota(jnp.int32, (chunk, 128), 1)
    for n in range(total // chunk):
        place = pl.multiple_of(table[n] * chunk, chunk)
        opened = jax.nn.sigmoid(g_ref[pl.ds(place, chunk), :])
        attended = a_ref[pl.ds(place, chunk), :]
        grad = db_ref[pl.ds(place, chunk), :]
        below = (grad * opened).astype(BF16)
        dan[pl.ds(n * chunk, chunk), :] = below
        dg_ref[pl.ds(place, chunk), :] = (grad * attended * opened * (1.0 - opened)).astype(BF16)
        both = below.astype(F32) * attended
        sums = jnp.zeros((chunk, 128), F32)
        for h in range(per_group):
            own = jnp.where(lanes_of(chunk, width, h, depth), both, 0.0)
            sums = jnp.where(small == h, jnp.sum(own, axis=1, keepdims=True), sums)
        delta[pl.ds(n * chunk, chunk), :] = sums
    rows[...] = jnp.transpose(delta[...])
    dkn[...] = jnp.zeros_like(dkn)
    dvn[...] = jnp.zeros_like(dvn)
    for i in range(total // bq):
        first = max(0, i * bq - window)
        span = (i + 1) * bq - first
        window_rows = pl.ds(first, span)
        place = i * bq + lax.broadcasted_iota(jnp.int32, (span, bq), 1)
        other = first + lax.broadcasted_iota(jnp.int32, (span, bq), 0)
        begin = begin_ref[:, i * bq:(i + 1) * bq]
        bias = jnp.where((other <= place) & (other >= begin), 0.0, LOW)
        q_tile = qn[i * bq:(i + 1) * bq, :] * jnp.asarray(depth ** -0.5, BF16)
        a_tile = dan[i * bq:(i + 1) * bq, :]
        keys = kn[window_rows, :]
        values = vn[window_rows, :]
        cumul = cumul_ref[window_rows, :]
        wide_lane = lax.broadcasted_iota(jnp.int32, (span, 128), 1)
        query_grad = jnp.zeros((bq, width + 128), F32)
        for h in range(per_group):
            head = group * per_group + h
            mine = lanes_of(bq, width, h, depth)
            q_mine = jnp.where(mine, q_tile, jnp.zeros_like(q_tile))
            a_mine = jnp.where(mine, a_tile, jnp.zeros_like(a_tile))
            column = jnp.sum(jnp.where(wide_lane == head, cumul, 0.0), axis=1, keepdims=True)
            score = dot(keys, q_mine, ((1,), (1,)))
            score = score - total_rows[pl.ds(head, 1), i * bq:(i + 1) * bq] - column + bias
            weight = jnp.exp(score)
            weight_grad = dot(values, a_mine, ((1,), (1,)))
            score_grad = (weight * (weight_grad - rows[h:h + 1, i * bq:(i + 1) * bq])).astype(BF16)
            mark = ((lane == head) | (lane == head + heads)).astype(F32).astype(BF16)
            mark_keys = ((wide_lane == head) | (wide_lane == head + heads)).astype(F32).astype(BF16)
            key_part = dot(score_grad, jnp.concatenate([q_mine, mark], axis=1))
            dvn[window_rows, :] += dot(weight.astype(BF16), a_mine)
            dkn[window_rows, :] += key_part[:, :width]
            dcumul[window_rows, :] -= key_part[:, width:]
            k_mine = jnp.where(lanes_of(span, width, h, depth), keys, jnp.zeros_like(keys))
            query_grad += dot(score_grad, jnp.concatenate([k_mine, mark_keys], axis=1), ((0,), (0,)))
        dqn[i * bq:(i + 1) * bq, :] = query_grad[:, :width] * depth ** -0.5
        dcumul[i * bq:(i + 1) * bq, :] += query_grad[:, width:]
    from_natural(table, dqn, dq_ref, chunk)
    from_natural(table, dkn, dk_ref, chunk)
    from_natural(table, dvn, dv_ref, chunk)

    @pl.when(group == pl.num_programs(0) - 1)
    def _():
        upper = (
            lax.broadcasted_iota(jnp.int32, (bq, bq), 0) <= lax.broadcasted_iota(jnp.int32, (bq, bq), 1)
        ).astype(F32)
        carry = jnp.zeros((1, 128), F32)
        for i in reversed(range(total // bq)):
            part = (
                jnp.dot(
                    upper, dcumul[i * bq:(i + 1) * bq, :], precision=lax.Precision.HIGHEST,
                    preferred_element_type=F32,
                )
                + carry
            )
            delta[i * bq:(i + 1) * bq, :] = part
            carry = part[0:1, :]
        sums = jnp.zeros((1, 128), F32)
        for n in range(total // chunk):
            place = pl.multiple_of(table[n] * chunk, chunk)
            logit = z_ref[pl.ds(place, chunk), :] + bias_ref[...]
            grad = delta[pl.ds(n * chunk, chunk), :] * jax.nn.sigmoid(-logit)
            sums = sums + jnp.sum(grad, axis=0, keepdims=True)
            high = grad.astype(BF16)
            rest = grad - high.astype(F32)
            dz_ref[pl.ds(place, chunk), :] = jnp.where(
                small < heads, high.astype(F32), jnp.where(small < 2 * heads, rest, 0.0)
            ).astype(BF16)
        dbias_ref[...] = jnp.broadcast_to(sums, dbias_ref.shape)


def group_width(columns):
    return 128 if columns % 128 == 0 else columns


def attend(table, qkv, gate, logit, bias, begin, chunk, depth):
    total = qkv[0].shape[0]
    columns = qkv[0].shape[1]
    width = group_width(columns)
    block = pl.BlockSpec((total, width), lambda g, t: (0, g))
    whole = pl.BlockSpec((total, 128), lambda g, t: (0, 0))
    wide = max(width, 128)
    return pl.pallas_call(
        functools.partial(attend_kernel, chunk, depth),
        grid_spec=pltpu.PrefetchScalarGridSpec(
            num_scalar_prefetch=1,
            grid=(columns // width,),
            in_specs=[
                block, block, block, block, whole,
                pl.BlockSpec((1, 128), lambda g, t: (0, 0)),
                pl.BlockSpec((total, 1), lambda g, t: (0, 0)),
            ],
            out_specs=[block, block, whole, whole],
            scratch_shapes=[
                pltpu.VMEM((total, width), BF16),
                pltpu.VMEM((total, width), BF16),
                pltpu.VMEM((total, width), BF16),
                pltpu.VMEM((total, wide), F32),
                pltpu.VMEM((128, total), F32),
            ],
        ),
        out_shape=[
            jax.ShapeDtypeStruct((total, columns), F32),
            jax.ShapeDtypeStruct((total, columns), BF16),
            jax.ShapeDtypeStruct((total, 128), F32),
            jax.ShapeDtypeStruct((total, 128), F32),
        ],
        compiler_params=pltpu.CompilerParams(vmem_limit_bytes=VMEM_LIMIT),
        name="attend",
    )(table, *qkv, gate, logit, bias, begin[:, None])


def attend_back(table, qkv, gate, attended, grad, totals, cumul, logit, bias, begin, chunk, depth):
    total = qkv[0].shape[0]
    columns = qkv[0].shape[1]
    width = group_width(columns)
    block = pl.BlockSpec((total, width), lambda g, t: (0, g))
    whole = pl.BlockSpec((total, 128), lambda g, t: (0, 0))
    low = jax.ShapeDtypeStruct((total, columns), BF16)
    return pl.pallas_call(
        functools.partial(attend_back_kernel, chunk, depth, columns // depth),
        grid_spec=pltpu.PrefetchScalarGridSpec(
            num_scalar_prefetch=1,
            grid=(columns // width,),
            in_specs=[
                block, block, block, block, block, block, whole, whole, whole,
                pl.BlockSpec((1, 128), lambda g, t: (0, 0)),
                pl.BlockSpec((1, total), lambda g, t: (0, 0)),
            ],
            out_specs=[block, block, block, block, whole, pl.BlockSpec((8, 128), lambda g, t: (0, 0))],
            scratch_shapes=[
                pltpu.VMEM((total, width), BF16),
                pltpu.VMEM((total, width), BF16),
                pltpu.VMEM((total, width), BF16),
                pltpu.VMEM((total, width), BF16),
                pltpu.VMEM((total, 128), F32),
                pltpu.VMEM((128, total), F32),
                pltpu.VMEM((128, total), F32),
                pltpu.VMEM((total, width), F32),
                pltpu.VMEM((total, width), F32),
                pltpu.VMEM((total, width), F32),
                pltpu.VMEM((total, 128), F32),
            ],
        ),
        out_shape=[
            low, low, low, low,
            jax.ShapeDtypeStruct((total, 128), BF16),
            jax.ShapeDtypeStruct((8, 128), F32),
        ],
        compiler_params=pltpu.CompilerParams(vmem_limit_bytes=VMEM_LIMIT),
        name="attend_back",
    )(table, *qkv, gate, attended, grad, totals, cumul, logit, bias, begin[None, :])


def doc_begins(lengths_row, total):
    ends = jnp.cumsum(lengths_row)
    begins = ends - lengths_row
    place = jnp.arange(total, dtype=jnp.int32)
    inside = (place[:, None] >= begins[None, :]) & (place[:, None] < ends[None, :])
    return jnp.sum(jnp.where(inside, begins[None, :], 0), axis=1)


def per_device(
    inputs, cotangent, lengths, deal, norm1_gain, w_query, w_key, w_value, w_outgate, w_out,
    forget_weight, forget_bias, norm2_gain, w_gate, w_up, w_down,
):
    nz, np_, nq = lax.axis_size("z"), lax.axis_size("p"), lax.axis_size("q")
    z, core, p, q = (lax.axis_index(name) for name in ("z", "core", "p", "q"))
    n_ctx = 2 * nz
    nt = 2 * np_
    plane = nt * nq
    micro, _, tokens, width = inputs.shape
    heads = forget_bias.shape[0]
    depth = width // heads
    own_heads = heads // nt
    columns = width // nt
    total = tokens * n_ctx
    chunk = tokens // np_
    block = tokens // 2
    hidden = w_gate.shape[1]
    slab = w_query.shape[0]
    everywhere = ("z", "core", "p", "q")
    member = core * np_ + p
    place = ((z * 2 + core) * np_ + p) * nq + q

    gains = lax.all_gather(jnp.stack([norm1_gain, norm2_gain]), everywhere, axis=0)
    gains = gains.transpose(1, 0, 2).reshape(2, width).astype(F32)
    gain_one, gain_two = gains[0:1], gains[1:2]

    forget = forget_weight.reshape(slab, nt, own_heads)
    spare = jnp.zeros((slab, nt, 128 - 2 * own_heads), BF16)
    packed = jnp.concatenate(
        [item.reshape(slab, nt, columns) for item in (w_query, w_key, w_value, w_outgate)]
        + [forget, forget, spare],
        axis=2,
    ).transpose(1, 0, 2)
    packed = lax.all_to_all(packed, ("core", "p"), split_axis=0, concat_axis=0, tiled=True)
    packed = lax.all_gather(packed, ("z", "q"), axis=0)
    packed = packed.reshape(nz, nq, nt, slab, -1).transpose(0, 2, 1, 3, 4).reshape(width, -1)
    w_qkv, w_gf = packed[:, :3 * columns], packed[:, 3 * columns:]

    piece = width // nz
    out_w = w_out.reshape(slab, nz, piece).transpose(1, 0, 2)
    out_w = lax.all_to_all(out_w, "z", split_axis=0, concat_axis=0, tiled=True)
    out_w = lax.all_to_all(out_w, ("core", "p"), split_axis=0, concat_axis=0, tiled=True)
    out_w = lax.all_gather(out_w, ("z", "q"), axis=0)
    out_w = out_w.reshape(nz, nq, nt, slab, piece).transpose(2, 1, 3, 0, 4).reshape(columns, width)

    unit = hidden // (nz * plane)
    share = nz * unit
    ffn_w = jnp.stack(
        [item.reshape(slab, nz, plane, unit).transpose(2, 0, 1, 3).reshape(plane, slab, share) for item in (w_gate, w_up)],
        axis=2,
    ).reshape(plane, slab, 2 * share)
    ffn_w = lax.all_to_all(ffn_w, ("core", "p", "q"), split_axis=0, concat_axis=0, tiled=True)
    ffn_w = lax.all_gather(ffn_w, "z", axis=0).reshape(width, 2 * share)
    down_w = lax.all_gather(w_down, "z", axis=0, tiled=True)

    stream_m, stream_p = z // np_, z % np_
    lengths_all = jnp.stack([lengths[:, 0]] + [xor_permute(lengths[:, 0], "p", k) for k in range(1, np_)])
    lengths_row = pick(pick(lengths_all, p ^ stream_p), stream_m)
    begin = doc_begins(lengths_row, total)
    number = jnp.arange(total // chunk, dtype=jnp.int32)
    from_core = core ^ (number // (np_ * nz))
    from_p = p ^ (number // nz % np_)
    from_z = z ^ (number % nz)
    dealt = jnp.take(pick(deal, stream_m), from_z * 2 + from_core)
    inside = from_p * chunk
    natural = jnp.where(inside < block, dealt, 2 * n_ctx - 1 - dealt) * block + inside % block
    natural = natural // chunk
    table = jnp.sum(jnp.where(natural[None, :] == number[:, None], number[None, :], 0), axis=1).astype(jnp.int32)
    bias_row = jnp.zeros((1, 128), F32)
    own_bias = lax.dynamic_slice_in_dim(forget_bias, member * own_heads, own_heads, 0)[None]
    bias_row = jnp.concatenate([own_bias, own_bias, jnp.zeros((1, 128 - 2 * own_heads), F32)], axis=1)

    stream = rows_to_group(inputs[:, 0]).astype(F32)
    norm_one = lax.rsqrt(jnp.mean(stream * stream, axis=-1, keepdims=True) + EPS)
    normed = gather_heads((stream * norm_one * gain_one).astype(BF16))
    qkv = dot(normed, w_qkv, out=BF16)
    gate_logit = dot(normed, w_gf)
    queries, keys, values = (qkv[:, i * columns:(i + 1) * columns] for i in range(3))
    gate, logit = gate_logit[:, :columns], gate_logit[:, columns:]
    attended, gated, totals, cumul = attend(
        table, (queries, keys, values), gate, logit, bias_row, begin, chunk, depth
    )
    middle = stream + scatter_heads(dot(gated, out_w))
    norm_two = lax.rsqrt(jnp.mean(middle * middle, axis=-1, keepdims=True) + EPS)
    normed_two = gather_plane((middle * norm_two * gain_two).astype(BF16))
    pre = dot(normed_two, ffn_w)
    gate_pre, up_pre = pre[:, :share], pre[:, share:]
    gate_sig = jax.nn.sigmoid(gate_pre)
    activ = (gate_pre * gate_sig * up_pre).astype(BF16)
    result = (middle + scatter_plane(dot(activ, down_w))).astype(BF16)
    output = rows_from_group(result, micro)

    upstream_own = rows_to_group(cotangent[:, 0])
    upstream = gather_plane(upstream_own)
    grad_activ = dot(upstream, down_w, ((1,), (1,)))
    gate_grad = (grad_activ * up_pre * (gate_sig * (1.0 + gate_pre * (1.0 - gate_sig)))).astype(BF16)
    up_grad = (grad_activ * gate_pre * gate_sig).astype(BF16)
    ffn_grad = jnp.concatenate([gate_grad, up_grad], axis=1)
    normed_two_grad = scatter_plane(dot(ffn_grad, ffn_w, ((1,), (1,))))
    grad_ffn_w = dot(normed_two, ffn_grad, ((0,), (0,)), BF16)
    grad_down = dot(activ, upstream, ((0,), (0,)), BF16)

    unit_two = middle * norm_two
    gain_two_sum = jnp.sum(normed_two_grad * unit_two, axis=0)
    scaled_two = normed_two_grad * gain_two
    middle_grad = upstream_own.astype(F32) + norm_two * (
        scaled_two - unit_two * jnp.mean(scaled_two * unit_two, axis=-1, keepdims=True)
    )
    branch_grad = gather_heads(middle_grad.astype(BF16))
    gated_grad = dot(branch_grad, out_w, ((1,), (1,)))
    grad_out = dot(gated, branch_grad, ((0,), (0,)), BF16)
    dq, dk, dv, dg, dz, dbias = attend_back(
        table, (queries, keys, values), gate, attended, gated_grad, totals, cumul, logit, bias_row, begin, chunk, depth
    )
    right = jnp.concatenate([dq, dk, dv, dg, dz], axis=1)
    normed_grad = scatter_heads(dot(right, packed, ((1,), (1,))))
    grad_packed = dot(normed, right, ((0,), (0,)), BF16)
    unit_one = stream * norm_one
    gain_one_sum = jnp.sum(normed_grad * unit_one, axis=0)
    scaled_one = normed_grad * gain_one
    stream_grad = middle_grad + norm_one * (
        scaled_one - unit_one * jnp.mean(scaled_one * unit_one, axis=-1, keepdims=True)
    )
    input_grad = rows_from_group(stream_grad.astype(BF16), micro).astype(F32)

    grad_ffn_w = lax.psum_scatter(grad_ffn_w, "z", scatter_dimension=0, tiled=True)
    grad_ffn_w = lax.all_to_all(
        grad_ffn_w.reshape(plane, slab, 2 * share), ("core", "p", "q"), split_axis=0, concat_axis=0, tiled=True
    ).astype(F32)
    grad_gate, grad_up = (
        item.reshape(plane, slab, nz, unit).transpose(1, 2, 0, 3).reshape(slab, hidden)
        for item in (grad_ffn_w[:, :, :share], grad_ffn_w[:, :, share:])
    )
    grad_down = lax.psum_scatter(grad_down, "z", scatter_dimension=0, tiled=True).astype(F32)

    grad_out = grad_out.reshape(nt, nq, slab, nz, piece).transpose(3, 1, 0, 2, 4).reshape(nz * nq, nt, slab, piece)
    grad_out = lax.psum_scatter(grad_out, ("z", "q"), scatter_dimension=0, tiled=True)[0]
    grad_out = lax.all_to_all(grad_out, ("core", "p"), split_axis=0, concat_axis=0, tiled=True)
    grad_out = lax.all_to_all(grad_out, "z", split_axis=0, concat_axis=0, tiled=True)
    grad_out = grad_out.transpose(1, 0, 2).reshape(slab, width).astype(F32)

    grad_packed = grad_packed.reshape(nz, nt, nq, slab, -1).transpose(0, 2, 1, 3, 4).reshape(nz * nq, nt, slab, -1)
    grad_packed = lax.psum_scatter(grad_packed, ("z", "q"), scatter_dimension=0, tiled=True)[0]
    grad_packed = lax.all_to_all(grad_packed, ("core", "p"), split_axis=0, concat_axis=0, tiled=True).astype(F32)
    grad_query, grad_key, grad_value, grad_outgate = (
        grad_packed[:, :, i * columns:(i + 1) * columns].transpose(1, 0, 2).reshape(slab, width) for i in range(4)
    )
    tail = grad_packed[:, :, 4 * columns:]
    grad_forget = (tail[:, :, :own_heads] + tail[:, :, own_heads:2 * own_heads]).transpose(1, 0, 2).reshape(slab, heads)

    bias_sum = lax.dynamic_update_slice_in_dim(
        jnp.zeros((width,), F32), dbias[0, :own_heads], member * own_heads, 0
    )
    sums = lax.psum(jnp.stack([gain_one_sum, gain_two_sum, bias_sum]), everywhere)
    grad_gain_one = lax.dynamic_slice_in_dim(sums[0], place * slab, slab, 0)
    grad_gain_two = lax.dynamic_slice_in_dim(sums[1], place * slab, slab, 0)
    return (
        output[:, None], input_grad[:, None], grad_gain_one, grad_query, grad_key, grad_value, grad_outgate,
        grad_out, grad_forget, sums[2, :heads], grad_gain_two, grad_gate, grad_up, grad_down,
    )


def solution(mesh):
    n_ctx, n_fsdp = mesh.shape["ctx"], mesh.shape["fsdp"]
    fine = Mesh(mesh.devices.reshape(n_ctx // 2, 2, n_fsdp // 2, 2), ("z", "core", "p", "q"))
    ctx, fsdp, every = ("z", "core"), ("p", "q"), ("z", "core", "p", "q")
    rows = P(None, fsdp, ctx, None)
    vector, matrix = P(every), P(every, None)
    return jax.shard_map(
        per_device,
        mesh=fine,
        in_specs=(
            rows, rows, P(None, fsdp, None), P(), vector, matrix, matrix, matrix, matrix, matrix, matrix, P(),
            vector, matrix, matrix, matrix,
        ),
        out_specs=(
            rows, rows, vector, matrix, matrix, matrix, matrix, matrix, matrix, P(), vector, matrix, matrix, matrix,
        ),
        check_vma=False,
    )
```

```python
import functools

import jax
import jax.numpy as jnp
from jax import lax
from jax.experimental import pallas as pl
from jax.experimental.pallas import tpu as pltpu
from jax.sharding import Mesh, PartitionSpec as P

EPS = 1e-06
LOW = -1e30
BQ = 256
F32 = jnp.float32
BF16 = jnp.bfloat16
VMEM_LIMIT = 56 * 1024 * 1024


def dot(left, right, contract=((1,), (0,)), out=F32):
    return lax.dot_general(left, right, (contract, ((), ())), preferred_element_type=out)


def xor_permute(x, axis, step):
    n = lax.axis_size(axis)
    return lax.ppermute(x, axis, [(i, i ^ step) for i in range(n)])


def pick(stacked, index):
    return lax.dynamic_index_in_dim(stacked, index, 0, keepdims=False)


def xor_plane(x, step):
    n = lax.axis_size("p") * lax.axis_size("q")
    return lax.ppermute(x, ("p", "q"), [(i, i ^ step) for i in range(n)])


def rows_to_plane(x):
    nf = lax.axis_size("p") * lax.axis_size("q")
    f = lax.axis_index(("p", "q"))
    micro, tokens, width = x.shape
    parts = x.reshape(micro, nf, tokens // nf, width).transpose(1, 0, 2, 3)
    return jnp.stack([pick(parts, f)] + [xor_plane(pick(parts, f ^ k), k) for k in range(1, nf)])


def rows_to_layer(got):
    nz = lax.axis_size("z")
    f, z = lax.axis_index(("p", "q")), lax.axis_index("z")
    return [pick(got, f ^ z)] + [xor_permute(pick(got, f ^ z ^ k), "z", k) for k in range(1, nz)]


def rows_from_layer(y):
    nz = lax.axis_size("z")
    micro, rows, width = y.shape
    rp = rows // nz
    return [y[:, :rp]] + [xor_permute(y[:, k * rp:(k + 1) * rp], "z", k) for k in range(1, nz)]


def rows_from_plane(got):
    nf = lax.axis_size("p") * lax.axis_size("q")
    f, z = lax.axis_index(("p", "q")), lax.axis_index("z")
    got = jnp.stack(got)
    back = [pick(got, z ^ f)] + [xor_plane(pick(got, z ^ f ^ k), k) for k in range(1, nf)]
    back = jnp.stack(back)
    return jnp.concatenate([pick(back, f ^ c) for c in range(nf)], axis=1)


def gather_first(x):
    np_ = lax.axis_size("p")
    return [x, xor_permute(x, "q", 1)] + [xor_permute(x, "p", k) for k in range(1, np_)]


def gather_rest(first):
    np_ = lax.axis_size("p")
    x, over_q = first[:2]
    half = x.shape[0] // 2
    if np_ == 2:
        over_p = first[2]
        own = [x, over_q, over_p, [xor_permute(over_q[:half], "p", 1), xor_permute(over_p[half:], "q", 1)]]
    else:
        own = [x, over_q]
        for k in range(1, np_):
            own += [first[1 + k], xor_permute(over_q, "p", k)]
    return own + jax.tree.map(lambda block: xor_permute(block, "core", 1), own)


def gather_plane(x):
    return gather_rest(gather_first(x))


def in_rows(blocks):
    return jnp.concatenate(jax.tree.leaves(blocks), axis=0)


def add_up(*parts):
    return sum(part.astype(F32) for part in parts)


def scatter_core(far, near):
    got = [xor_permute(item, "core", 1) for item in far]
    shape = (2 * lax.axis_size("p"), -1, near[0].shape[-1])
    near = [item.reshape(shape) for item in near]
    got = [item.reshape(shape) for item in got]
    return near, got, both_cores(near, got, shape[0] - 1).astype(BF16)


def both_cores(near, got, number):
    return jnp.concatenate([add_up(one[number], other[number]) for one, other in zip(near, got)], axis=0)


def scatter_diagonal(near, got, last, beside=None):
    np_ = lax.axis_size("p")
    near, got, last = lax.optimization_barrier((near, got, last))
    made = ()
    if np_ == 2:
        half = last.shape[0] // 2
        into_q = xor_permute(last[:half], "p", 1)
        into_p = xor_permute(last[half:], "q", 1)
        if beside is not None:
            into_q, into_p, made = lax.optimization_barrier((into_q, into_p, beside(last)))
        to_q, to_p = both_cores(near, got, 1), both_cores(near, got, 2)
        to_q = jnp.concatenate([add_up(to_q[:half], into_q), to_q[half:]], axis=0).astype(BF16)
        to_p = jnp.concatenate([to_p[:half], add_up(to_p[half:], into_p)], axis=0).astype(BF16)
        own = [side[0][0] if len(side) == 1 else jnp.concatenate([item[0] for item in side]) for side in (near, got)]
        return own, [(to_q, "q"), (to_p, "p")], made
    if beside is not None:
        made = beside(last)
    pair = [both_cores(near, got, 0), both_cores(near, got, 1)]
    for k in range(1, np_):
        for side in range(2):
            item = last if 2 * k + side == 2 * np_ - 1 else both_cores(near, got, 2 * k + side).astype(BF16)
            pair[side] = pair[side] + xor_permute(item, "p", k).astype(F32)
    return [pair[0]], [(pair[1].astype(BF16), "q")], made


def scatter_first(far, near, beside=None):
    return scatter_diagonal(*scatter_core(far, near), beside)


def sent(state):
    return [item for item, _ in state[1]]


def received(state, sends):
    return [xor_permute(item, axis, 1) for item, (_, axis) in zip(sends, state[1])]


def scatter_rest(state):
    return add_up(*state[0], *received(state, sent(state)))


def total_over(axis, x):
    step = 1
    while step < lax.axis_size(axis):
        x = x + xor_permute(x, axis, step)
        step *= 2
    return x


def log_sigmoid(z):
    return jnp.minimum(z, 0.0) - jnp.log(1.0 + jnp.exp(-jnp.abs(z)))


def window_of(i, bq, window):
    first = max(0, i * bq - window)
    return first, (i + 1) * bq - first


def pieces(members, rows, chunk):
    per = rows // chunk
    return [(j * per + k, j, k * chunk) for j in range(members) for k in range(per)]


def natural_rows(table, number, chunk):
    return pl.ds(pl.multiple_of(table[number] * chunk, chunk), chunk)


def spread_rows(table, source, far_ref, near_ref, chunk):
    half = near_ref.shape[0]
    for number, j, at in pieces(2 * half, near_ref.shape[1], chunk):
        target = near_ref if j < half else far_ref
        target[j % half, at:at + chunk, :] = source[natural_rows(table, number, chunk), :]


def attend_kernel(heads, depth, chunk, members, table, *refs):
    x_refs, refs = refs[:members], refs[members:]
    w_ref, bias_ref, begin_ref = refs[:3]
    h_ref, qkv_ref, g_ref, z_ref, a_ref, total_ref, cumul_ref, b_ref, gain_ref = refs[3:12]
    ka, va, rows, part = refs[12:]
    total = total_ref.shape[0]
    columns = heads * depth
    bq = min(BQ, total)
    window = total // 2
    scale = jnp.asarray(depth ** -0.5, BF16)
    for number, j, at in pieces(members, x_refs[0].shape[0], chunk):
        part[natural_rows(table, number, chunk), :] = x_refs[j][at:at + chunk, :]
    gains = jnp.transpose(w_ref[:, 0:128].astype(F32))[2 * heads:2 * heads + 2, :]
    gain_ref[...] = jnp.concatenate([gains, jnp.zeros((6, gains.shape[1]), F32)], axis=0)
    gain = gains[0:1, :]
    lower = (
        lax.broadcasted_iota(jnp.int32, (bq, bq), 0) >= lax.broadcasted_iota(jnp.int32, (bq, bq), 1)
    ).astype(F32).astype(BF16)
    carry = jnp.zeros((1, 128), F32)
    for i in range(total // bq):
        here = slice(i * bq, (i + 1) * bq)
        values = part[here, :].astype(F32)
        values = values * lax.rsqrt(jnp.mean(values * values, axis=1, keepdims=True) + EPS) * gain
        h_ref[here, :] = values.astype(BF16)
        tile = dot(h_ref[here, :], w_ref[...])
        logit = tile[:, 0:128] + bias_ref[...]
        z_ref[here, :] = logit
        cumul = dot(lower, log_sigmoid(logit).astype(BF16)) + carry
        cumul_ref[here, :] = cumul
        carry = cumul[bq - 1:bq, :]
        qkv_ref[here, :] = tile[:, 128:128 + 3 * columns].astype(BF16)
        g_ref[here, :] = tile[:, 128 + 3 * columns:]
        for h in range(heads):
            lo = 128 + columns + h * depth
            ka[h, here, :] = tile[:, lo:lo + depth].astype(BF16)
            lo += columns
            va[h, here, 0:depth] = tile[:, lo:lo + depth].astype(BF16)
            va[h, here, depth:] = jnp.ones((bq, 128 - depth), BF16)
    rows[...] = jnp.transpose(cumul_ref[...])
    lane = lax.broadcasted_iota(jnp.int32, (bq, 128), 1)
    for i in range(total // bq):
        first, span = window_of(i, bq, window)
        here = slice(i * bq, (i + 1) * bq)
        place = i * bq + lax.broadcasted_iota(jnp.int32, (bq, span), 0)
        other = first + lax.broadcasted_iota(jnp.int32, (bq, span), 1)
        mask = jnp.where((other <= place) & (other >= begin_ref[here, :]), 0.0, LOW)
        totals = jnp.zeros((bq, 128), F32)
        for h in range(heads):
            query = qkv_ref[here, h * depth:(h + 1) * depth] * scale
            score = dot(query, ka[h, first:first + span, :], ((1,), (1,)))
            score = score - rows[h:h + 1, first:first + span] + mask
            peak = jnp.max(score, axis=1, keepdims=True)
            weight = jnp.exp(score - peak)
            both = dot(weight.astype(BF16), va[h, first:first + span, :])
            a_ref[here, h * depth:(h + 1) * depth] = both[:, 0:depth] / both[:, depth:2 * depth]
            totals = jnp.where(lane == h, peak + jnp.log(both[:, depth:depth + 1]), totals)
        total_ref[here, :] = totals
        part[here, 0:columns] = (a_ref[here, :] * jax.nn.sigmoid(g_ref[here, :])).astype(BF16)
    for number, j, at in pieces(members, b_ref.shape[1], chunk):
        b_ref[j, at:at + chunk, :] = part[natural_rows(table, number, chunk), 0:columns]


def attend_back_kernel(heads, depth, chunk, members, streams, table, *refs):
    x_refs, refs = refs[:members], refs[members:]
    extra = members * max(0, streams - 1)
    other_refs, gated_refs, refs = refs[:extra], refs[extra:extra + streams], refs[extra + streams:]
    w_ref, o_ref, qkv_ref, g_ref, z_ref, a_ref, total_ref, cumul_ref, begin_ref = refs[:9]
    right_ref, far_ref, near_ref, dbias_ref = refs[9:13]
    part, below_grad, qa, ka, va, da, dkn, dvn, rows, deltas, dcumul = refs[-11:]
    if streams:
        out_grad = jnp.zeros(refs[13].shape, F32)
        for number, ref in enumerate(x_refs + other_refs):
            out_grad = out_grad + dot(gated_refs[number // members][number % members], ref[...], ((0,), (0,)))
        refs[13][...] = out_grad.astype(BF16)
    total = total_ref.shape[0]
    columns = heads * depth
    bq = min(BQ, total)
    window = total // 2
    scale = jnp.asarray(depth ** -0.5, BF16)
    lane = lax.broadcasted_iota(jnp.int32, (bq, 128), 1)
    per = x_refs[0].shape[0] // chunk
    for j in range(members):
        grad = dot(x_refs[j][...], o_ref[...], ((1,), (1,)))
        for k in range(per):
            below_grad[natural_rows(table, j * per + k, chunk), :] = grad[k * chunk:(k + 1) * chunk, :]
    dkn[...] = jnp.zeros_like(dkn)
    dvn[...] = jnp.zeros_like(dvn)
    for i in range(total // bq):
        here = slice(i * bq, (i + 1) * bq)
        grad = below_grad[here, :]
        opened = jax.nn.sigmoid(g_ref[here, :])
        attended = a_ref[here, :]
        below = (grad * opened).astype(BF16)
        right_ref[here, 128 + 3 * columns:] = (grad * attended * opened * (1.0 - opened)).astype(BF16)
        product = below.astype(F32) * attended
        delta = jnp.zeros((bq, 128), F32)
        for h in range(heads):
            da[h, here, :] = below[:, h * depth:(h + 1) * depth]
            delta = jnp.where(
                lane == h, jnp.sum(product[:, h * depth:(h + 1) * depth], axis=1, keepdims=True), delta
            )
            qa[h, here, 0:depth] = qkv_ref[here, h * depth:(h + 1) * depth] * scale
            qa[h, here, depth:] = jnp.ones((bq, 128 - depth), BF16)
            lo = columns + h * depth
            ka[h, here, 0:depth] = qkv_ref[here, lo:lo + depth]
            ka[h, here, depth:] = jnp.ones((bq, 128 - depth), BF16)
            lo += columns
            va[h, here, :] = qkv_ref[here, lo:lo + depth]
        dcumul[here, :] = delta
    deltas[...] = jnp.transpose(dcumul[...])
    rows[...] = jnp.transpose(total_ref[...])
    dcumul[...] = jnp.zeros_like(dcumul)
    for i in range(total // bq):
        first, span = window_of(i, bq, window)
        here, there = slice(i * bq, (i + 1) * bq), slice(first, first + span)
        place = i * bq + lax.broadcasted_iota(jnp.int32, (span, bq), 1)
        other = first + lax.broadcasted_iota(jnp.int32, (span, bq), 0)
        mask = jnp.where((other <= place) & (other >= begin_ref[:, here]), 0.0, LOW)
        for h in range(heads):
            query, below = qa[h, here, :], da[h, here, :]
            score = dot(ka[h, there, 0:depth], query[:, 0:depth], ((1,), (1,)))
            score = score - rows[h:h + 1, here] - cumul_ref[there, h:h + 1] + mask
            weight = jnp.exp(score)
            weight_grad = dot(va[h, there, :], below, ((1,), (1,))) - deltas[h:h + 1, here]
            score_grad = (weight * weight_grad).astype(BF16)
            dvn[h, there, :] += dot(weight.astype(BF16), below)
            dkn[h, there, :] += dot(score_grad, query)
            dq = dot(score_grad, ka[h, there, :], ((0,), (0,)))
            right_ref[here, 128 + h * depth:128 + (h + 1) * depth] = (dq[:, 0:depth] * depth ** -0.5).astype(BF16)
            mine = (lane == h) | (lane == h + heads)
            dcumul[here, :] += jnp.where(mine, dq[:, depth:depth + 1], 0.0)
    upper = (
        lax.broadcasted_iota(jnp.int32, (bq, bq), 0) <= lax.broadcasted_iota(jnp.int32, (bq, bq), 1)
    ).astype(F32)
    carry = jnp.zeros((1, 128), F32)
    sums = jnp.zeros((1, 128), F32)
    for i in reversed(range(total // bq)):
        here = slice(i * bq, (i + 1) * bq)
        change = dcumul[here, :]
        for h in range(heads):
            lo = 128 + columns + h * depth
            right_ref[here, lo:lo + depth] = dkn[h, here, 0:depth].astype(BF16)
            lo += columns
            right_ref[here, lo:lo + depth] = dvn[h, here, :].astype(BF16)
            mine = (lane == h) | (lane == h + heads)
            change = change - jnp.where(mine, dkn[h, here, depth:depth + 1], 0.0)
        summed = carry + jnp.dot(upper, change, precision=lax.Precision.HIGHEST, preferred_element_type=F32)
        carry = summed[0:1, :]
        grad = summed * jax.nn.sigmoid(-z_ref[here, :])
        sums = sums + jnp.sum(grad, axis=0, keepdims=True)
        high = grad.astype(BF16).astype(F32)
        pair = jnp.where(lane < heads, high, jnp.where(lane < 2 * heads, grad - high, 0.0))
        right_ref[here, 0:128] = pair.astype(BF16)
        part[here, :] = dot(right_ref[here, :], w_ref[...], ((1,), (1,))).astype(BF16)
    dbias_ref[...] = jnp.broadcast_to(sums, dbias_ref.shape)
    spread_rows(table, part, far_ref, near_ref, chunk)


def one_stream(blocks, m, streams):
    arrays, specs = [], []
    for block in blocks:
        array, place = (block[m], 0) if isinstance(block, list) else (block, m)
        rows, width = (array.shape[0] if isinstance(block, list) else array.shape[0] // streams), array.shape[1]
        arrays.append(array)
        specs.append(pl.BlockSpec((rows, width), lambda i, t, place=place: (place, 0), pipeline_mode=pl.Buffered(1)))
    return arrays, specs


def fixed(array):
    return pl.BlockSpec(array.shape, lambda i, t: (0,) * array.ndim, pipeline_mode=pl.Buffered(1))


def attend(table, blocks, m, streams, weights, bias, begin, heads, depth, chunk):
    arrays, specs = one_stream(blocks, m, streams)
    members, (rows, width) = len(arrays), specs[0].block_shape
    total = begin.shape[0]
    columns = heads * depth
    begin = begin[:, None]
    outs = [
        ((total, width), BF16), ((total, 3 * columns), BF16), ((total, columns), F32), ((total, 128), F32),
        ((total, columns), F32), ((total, 128), F32), ((total, 128), F32), ((members, rows, columns), BF16),
        ((8, width), F32),
    ]
    out_shape = [jax.ShapeDtypeStruct(shape, kind) for shape, kind in outs]
    return pl.pallas_call(
        functools.partial(attend_kernel, heads, depth, chunk, members),
        grid_spec=pltpu.PrefetchScalarGridSpec(
            num_scalar_prefetch=1,
            grid=(1,),
            in_specs=specs + [fixed(weights), fixed(bias), fixed(begin)],
            out_specs=[fixed(item) for item in out_shape],
            scratch_shapes=[
                pltpu.VMEM((heads, total, depth), BF16),
                pltpu.VMEM((heads, total, 128), BF16),
                pltpu.VMEM((128, total), F32),
                pltpu.VMEM((total, width), BF16),
            ],
        ),
        out_shape=out_shape,
        compiler_params=pltpu.CompilerParams(vmem_limit_bytes=VMEM_LIMIT),
        cost_estimate=pl.CostEstimate(flops=14 * 10 ** 9, bytes_accessed=10 ** 7, transcendentals=0),
        name="attend",
    )(table, *arrays, weights, bias, begin)


def attend_back(table, blocks, m, streams, weights, out_w, kept, begin, gated, heads, depth, chunk):
    arrays, specs = one_stream(blocks, m, streams)
    members, (rows, width) = len(arrays), specs[0].block_shape
    total = begin.shape[0]
    columns = heads * depth
    begin = begin[None, :]
    gated = [] if gated is None else gated
    for other in range(1, len(gated)):
        other_arrays, other_specs = one_stream(blocks, other, streams)
        arrays, specs = arrays + other_arrays, specs + other_specs
    outs = [
        ((total, 128 + 4 * columns), BF16), ((members // 2, rows, width), BF16), ((members // 2, rows, width), BF16),
        ((8, 128), F32),
    ] + [((columns, width), BF16)] * (len(gated) > 0)
    out_shape = [jax.ShapeDtypeStruct(shape, kind) for shape, kind in outs]
    return pl.pallas_call(
        functools.partial(attend_back_kernel, heads, depth, chunk, members, len(gated)),
        grid_spec=pltpu.PrefetchScalarGridSpec(
            num_scalar_prefetch=1,
            grid=(1,),
            in_specs=specs + [fixed(item) for item in (*gated, weights, out_w, *kept, begin)],
            out_specs=[fixed(item) for item in out_shape],
            scratch_shapes=[
                pltpu.VMEM((total, width), BF16),
                pltpu.VMEM((total, columns), F32),
                pltpu.VMEM((heads, total, 128), BF16),
                pltpu.VMEM((heads, total, 128), BF16),
                pltpu.VMEM((heads, total, depth), BF16),
                pltpu.VMEM((heads, total, depth), BF16),
                pltpu.VMEM((heads, total, 128), F32),
                pltpu.VMEM((heads, total, depth), F32),
                pltpu.VMEM((128, total), F32),
                pltpu.VMEM((128, total), F32),
                pltpu.VMEM((total, 128), F32),
            ],
        ),
        out_shape=out_shape,
        compiler_params=pltpu.CompilerParams(vmem_limit_bytes=VMEM_LIMIT),
        cost_estimate=pl.CostEstimate(flops=20 * 10 ** 9, bytes_accessed=10 ** 7, transcendentals=0),
        name="attend_back",
    )(table, *arrays, *gated, weights, out_w, *kept, begin)


def out_kernel(b_ref, o_ref, far_ref, near_ref):
    half = near_ref.shape[0]
    for j in range(2 * half):
        target = near_ref if j < half else far_ref
        target[j % half] = dot(b_ref[j], o_ref[...]).astype(BF16)


def out_product(gated, weights):
    members, rows, _ = gated.shape
    shape = jax.ShapeDtypeStruct((members // 2, rows, weights.shape[1]), BF16)
    return pl.pallas_call(
        out_kernel,
        out_shape=[shape, shape],
        compiler_params=pltpu.CompilerParams(vmem_limit_bytes=VMEM_LIMIT),
        name="out_product",
    )(gated, weights)


def ffn_kernel(h_ref, e_ref, w_ref, d_ref, *refs):
    m_ref, g_ref, part_ref = refs[-3:]
    down = d_ref[...].reshape(-1, d_ref.shape[-1])
    share = down.shape[0]
    pre = dot(h_ref[...], w_ref[...])
    gate, up = pre[:, :share], pre[:, share:]
    grad = dot(e_ref[...], down, ((1,), (1,)))
    opened = jax.nn.sigmoid(gate)
    silu = gate * opened
    m_ref[...] = (silu * up).astype(BF16)
    g_ref[:, :share] = (grad * up * (opened * (1.0 + gate * (1.0 - opened)))).astype(BF16)
    g_ref[:, share:] = (grad * silu).astype(BF16)
    part_ref[...] = dot(g_ref[...], w_ref[...], ((1,), (1,))).astype(BF16)


def ffn(normed, upstream, weights, down, unit, first, count, into):
    rows, width = normed.shape
    share = down.shape[0] * unit

    def blocks(lanes, shift):
        return pl.BlockSpec((BQ, lanes), lambda i: (i + shift, 0))

    def fixed(shape):
        return pl.BlockSpec(shape, lambda i: (0,) * len(shape), pipeline_mode=pl.Buffered(1))

    kept = [] if into is None else list(into)
    return pl.pallas_call(
        ffn_kernel,
        grid=(count,),
        in_specs=[blocks(width, first), blocks(width, first), fixed(weights.shape), fixed((down.shape[0], unit, width))]
        + [pl.BlockSpec(memory_space=pl.ANY)] * len(kept),
        out_specs=[blocks(share, first), blocks(2 * share, first), blocks(width, 0)],
        out_shape=[
            jax.ShapeDtypeStruct((rows, share), BF16),
            jax.ShapeDtypeStruct((rows, 2 * share), BF16),
            jax.ShapeDtypeStruct((count * BQ, width), BF16),
        ],
        input_output_aliases={4 + i: i for i in range(len(kept))},
        compiler_params=pltpu.CompilerParams(vmem_limit_bytes=VMEM_LIMIT),
        cost_estimate=pl.CostEstimate(
            flops=10 * count * BQ * width * share, bytes_accessed=count * BQ * width * 8, transcendentals=0
        ),
        name="ffn",
    )(normed, upstream, weights, down, *kept)


def layout(body, shapes, kind, *arrays):
    kinds = kind if isinstance(kind, list) else [kind] * len(shapes)
    out_shape = [jax.ShapeDtypeStruct(shape, own) for shape, own in zip(shapes, kinds)]
    return pl.pallas_call(body, out_shape=out_shape, name="layout")(*arrays)


def block_columns(block, columns, limit):
    return min(block * columns, limit), max(0, min((block + 1) * columns, limit) - min(block * columns, limit))


def pack_heads(forget, weights, nf, columns):
    slab, width = weights[0].shape
    plane = 2 * nf

    def body(f_ref, *refs):
        out = refs[-1]
        for t in range(plane):
            out[t, :, 0:128] = f_ref[:, t * 128:(t + 1) * 128]
            first, count = block_columns(t % nf * 2 + t // nf, columns, width)
            for number, ref in enumerate(refs[:-1]):
                lo = 128 + number * columns
                if count < columns:
                    out[t, :, lo:lo + columns] = jnp.zeros((slab, columns), BF16)
                if count:
                    out[t, :, lo:lo + count] = ref[:, first:first + count]

    return layout(body, [(plane, slab, 128 + 4 * columns)], BF16, forget, *weights)[0]


def unpack_heads(grads, weights, nf, columns):
    plane, slab, _ = grads.shape
    width = weights[0].shape[1]

    def body(x_ref, *refs):
        sums = jnp.zeros((slab, 1), F32)
        for number in range(4):
            weight, out = refs[number], refs[4 + number]
            for t in range(plane):
                first, count = block_columns(t % nf * 2 + t // nf, columns, width)
                lo = 128 + number * columns
                if count:
                    out[:, first:first + count] = x_ref[t, :, lo:lo + count].astype(F32)
            sums = sums + jnp.sum(weight[...].astype(F32) * out[...], axis=1, keepdims=True)
        refs[8][...] = sums

    return layout(body, [(slab, width)] * 4 + [(slab, 1)], F32, grads, *weights)


def pack_hidden(gate, up, nz, plane):
    slab, hidden = gate.shape
    unit = hidden // (nz * plane)

    def body(gate_ref, up_ref, out):
        for number, ref in enumerate((gate_ref, up_ref)):
            for t in range(plane):
                for z in range(nz):
                    lo = (number * nz + z) * unit
                    at = (z * plane + t) * unit
                    out[t, :, lo:lo + unit] = ref[:, at:at + unit]

    return layout(body, [(plane, slab, 2 * nz * unit)], BF16, gate, up)[0]


def unpack_hidden(grads, weights, nz):
    plane, slab, both = grads.shape
    unit = both // (2 * nz)

    def body(x_ref, *refs):
        sums = jnp.zeros((slab, 1), F32)
        for number in range(2):
            weight, out = refs[number], refs[2 + number]
            for t in range(plane):
                for z in range(nz):
                    lo = (number * nz + z) * unit
                    at = (z * plane + t) * unit
                    out[:, at:at + unit] = x_ref[t, :, lo:lo + unit].astype(F32)
            sums = sums + jnp.sum(weight[...].astype(F32) * out[...], axis=1, keepdims=True)
        refs[4][...] = sums

    return layout(body, [(slab, plane * nz * unit)] * 2 + [(slab, 1)], F32, grads, *weights)


def doc_begins(lengths_row, total):
    ends = jnp.cumsum(lengths_row)
    begins = ends - lengths_row
    place = jnp.arange(total, dtype=jnp.int32)
    inside = (place[:, None] >= begins[None, :]) & (place[:, None] < ends[None, :])
    return jnp.sum(jnp.where(inside, begins[None, :], 0), axis=1)


def all_to_all(x, axes):
    return lax.all_to_all(x, axes, split_axis=0, concat_axis=0, tiled=True)


def scatter_layers(grad):
    return lax.psum_scatter(grad, "z", scatter_dimension=0, tiled=True)


def join_grads(grad, down, nz):
    lanes, width = grad.shape[1], down.shape[1]
    grad, down = grad.reshape(nz, -1, lanes), down.reshape(nz, -1, width)
    parts = [grad] + [down[:, :, i * lanes:(i + 1) * lanes] for i in range(width // lanes)]
    rest = width % lanes
    if rest:
        count = lanes // rest
        rows = down.shape[1] // count
        over = down[:, :, width - rest:].reshape(nz, count, rows, rest)
        parts.append(jnp.concatenate([over[:, i] for i in range(count)], axis=2))
    return jnp.concatenate(parts, axis=1).reshape(-1, lanes)


def part_grads(joined, slabs, rows, width):
    lanes = joined.shape[1]
    grad, joined = joined[:slabs], joined[slabs:]
    whole = width // lanes
    parts = [joined[i * rows:(i + 1) * rows] for i in range(whole)]
    rest = width % lanes
    if rest:
        over = joined[whole * rows:]
        parts.append(jnp.concatenate([over[:, i * rest:(i + 1) * rest] for i in range(lanes // rest)], axis=0))
    return grad, jnp.concatenate(parts, axis=1)


def tie(*values):
    return lax.optimization_barrier(values)


def per_device(
    inputs, cotangent, lengths, deal, norm1_gain, w_query, w_key, w_value, w_outgate, w_out,
    forget_weight, forget_bias, norm2_gain, w_gate, w_up, w_down,
):
    nz, np_, nq = lax.axis_size("z"), lax.axis_size("p"), lax.axis_size("q")
    z, core, f = lax.axis_index("z"), lax.axis_index("core"), lax.axis_index(("p", "q"))
    nf = np_ * nq
    n_ctx = 2 * nz
    plane = 2 * nf
    devices = nz * plane
    everywhere, members = ("z", "core", "p", "q"), ("core", "p", "q")
    micro, _, tokens, width = inputs.shape
    heads = forget_bias.shape[0]
    depth = width // heads
    own_heads = -(-heads // plane)
    columns = own_heads * depth
    spare_heads = own_heads * plane - heads
    total = tokens * n_ctx
    chunk = tokens // nf
    block = tokens // 2
    hidden = w_gate.shape[1]
    slab = w_query.shape[0]
    unit = hidden // devices
    share = nz * unit
    own_block = f * 2 + core
    aligned = spare_heads == 0 and columns == nf * slab

    member_block = [t % nf * 2 + t // nf for t in range(plane)]
    head_of = jnp.arange(heads, dtype=jnp.int32)[:, None]
    lane_of = jnp.arange(plane * 128, dtype=jnp.int32)[None, :]
    lane_head = jnp.asarray(member_block, jnp.int32)[lane_of // 128] * own_heads + lane_of % 128 % own_heads
    select = ((lane_head == head_of) & (lane_of % 128 < 2 * own_heads)).astype(BF16)
    first_lanes = dot(forget_weight, select, out=BF16)
    for number, gain in enumerate((norm1_gain, norm2_gain)):
        first_lanes = jnp.where(lane_of % 128 == 2 * own_heads + number, gain[:, None], first_lanes)
    packed = pack_heads(first_lanes, (w_query, w_key, w_value, w_outgate), nf, columns)
    own = rows_to_layer(rows_to_plane(inputs[:, 0]))
    packed, own[1] = tie(packed, own[1])
    packed = all_to_all(packed, members)
    if aligned:
        out_w = jnp.stack([w_out] + [xor_permute(w_out, "z", k) for k in range(1, nz)])
        out_w = jnp.stack([pick(out_w, z ^ c) for c in range(nz)])
    else:
        out_w = jnp.pad(lax.all_gather(w_out, everywhere, axis=0, tiled=True), ((0, spare_heads * depth), (0, 0)))
        out_w = lax.dynamic_slice_in_dim(out_w, own_block * columns, columns, 0)
    own = jnp.concatenate(own, axis=1).reshape(-1, width)
    packed, own, out_w = tie(packed, own, out_w)
    packed = lax.all_gather(packed, "z", axis=0).reshape(width, -1)
    gathered = gather_first(own)
    ffn_send, gathered = tie(pack_hidden(w_gate, w_up, nz, plane), gathered)
    gathered = gather_rest(gathered)
    if aligned:
        out_w = all_to_all(out_w, ("p", "q")).reshape(columns, width)
    ffn_w = all_to_all(ffn_send, members)
    out_w, ffn_w, gathered, cotangent = tie(out_w, ffn_w, gathered, cotangent)
    upstream_own = rows_to_plane(cotangent[:, 0])
    packed, upstream_own = tie(packed, upstream_own)
    upstream_own = jnp.concatenate(rows_to_layer(upstream_own), axis=1).reshape(-1, width)

    lengths_own = lax.ppermute(
        lengths[:, 0], everywhere,
        [
            (((f_to * 2 + c) * nf) + z_to, ((z_to * 2 + c) * nf) + f_to)
            for z_to in range(nz) for c in range(2) for f_to in range(nf)
        ],
    )
    begins = [doc_begins(lengths_own[m], total) for m in range(micro)]
    number = jnp.arange(total // chunk, dtype=jnp.int32)
    from_core = core ^ (number // (nf * nz))
    from_f = f ^ (number // nz % nf)
    from_z = z ^ (number % nz)
    inside = from_f * chunk

    def natural_table(deal_row):
        dealt = jnp.take(deal_row, from_z * 2 + from_core)
        start = jnp.where(inside < block, dealt, 2 * n_ctx - 1 - dealt) * block + inside % block
        return (start // chunk).astype(jnp.int32)

    tables = [natural_table(deal[m]) for m in range(micro)]
    all_bias = jnp.pad(forget_bias, (0, spare_heads))
    own_bias = lax.dynamic_slice_in_dim(all_bias, own_block * own_heads, own_heads, 0)[None]
    bias_row = jnp.concatenate([own_bias, own_bias, jnp.zeros((1, 128 - 2 * own_heads), F32)], axis=1)

    def attend_stream(m, table):
        return attend(table, gathered, m, micro, packed, bias_row, begins[m], own_heads, depth, chunk)

    stream = own.astype(F32)
    attended = [attend_stream(0, tables[0])]
    gains = attended[0][8]
    gated = [attended[0][7]]
    parts = [out_product(gated[0], out_w)]
    table, upstream_own, gains, ffn_w, w_down = tie(tables[1], upstream_own, gains, ffn_w, w_down)
    ffn_w = lax.all_gather(ffn_w, "z", axis=0).reshape(width, 2 * share)
    down_w = lax.all_gather(w_down, "z", axis=0)
    attended.append(attend_stream(1, table))
    upstream = gather_first(upstream_own)
    last_gated, upstream = tie(attended[1][7], upstream)
    gated.append(last_gated)
    parts.append(out_product(gated[1], out_w))
    upstream = in_rows(gather_rest(upstream))
    gain_one, gain_two = gains[0:1], gains[1:2]
    middle = stream + scatter_rest(scatter_first([item[0] for item in parts], [item[1] for item in parts]))
    norm_two = lax.rsqrt(jnp.mean(middle * middle, axis=-1, keepdims=True) + EPS)
    normed_two = in_rows(gather_plane((middle * norm_two * gain_two).astype(BF16)))

    half_blocks = normed_two.shape[0] // BQ // 2
    weights = (normed_two, upstream, ffn_w, down_w, unit)
    activ, ffn_grad, far = ffn(*weights, half_blocks, half_blocks, None)
    activ, ffn_grad, near = ffn(*weights, 0, half_blocks, (activ, ffn_grad))
    def grad_of_ffn(hold):
        kept, _ = tie(normed_two, hold)
        return dot(kept, ffn_grad, ((0,), (0,)), BF16)

    state = scatter_first([far[None]], [near[None]], grad_of_ffn)
    grad_ffn_w = state[2]
    sends, held = tie(sent(state), activ)
    grad_down = dot(held, upstream, ((0,), (0,)), BF16)
    arrived, grad_ffn = tie(received(state, sends), join_grads(grad_ffn_w, grad_down, nz))
    grad_ffn = scatter_layers(grad_ffn)
    normed_two_grad = add_up(*state[0], *arrived)

    unit_two = middle * norm_two
    scaled_two = normed_two_grad * gain_two
    middle_grad = upstream_own.astype(F32) + norm_two * (
        scaled_two - unit_two * jnp.mean(scaled_two * unit_two, axis=-1, keepdims=True)
    )
    branch_own, held = tie(middle_grad.astype(BF16), activ)
    half = activ.shape[0] // 2
    down_rows = down_w.reshape(share, width)
    part_out = [dot(item, down_rows, out=BF16)[None] for item in (held[half:], held[:half])]
    branch_grad, part_out = tie(gather_first(branch_own), part_out)
    result = scatter_core(part_out[:1], part_out[1:])
    branch_grad = gather_rest(branch_grad)

    def back_stream(m, table, gated):
        return attend_back(
            table, branch_grad, m, micro, packed, out_w, attended[m][1:7], begins[m], gated, own_heads, depth, chunk
        )

    def first_back(hold):
        table, _ = tie(tables[0], hold)
        return back_stream(0, table, gated)

    result = scatter_diagonal(*result, first_back)
    backs = [result[2]]
    grad_packed = dot(attended[0][0], backs[0][0], ((0,), (0,)))
    grad_out = backs[0][4]
    if aligned:
        grad_out = all_to_all(grad_out.reshape(nf, slab, width), ("p", "q"))
    if aligned:
        grad_out = scatter_layers(grad_out.reshape(nf * slab, width))
    table, grad_packed, sends, grad_ffn = tie(tables[1], grad_packed, sent(result), grad_ffn)
    grad_ffn_w, grad_down = part_grads(grad_ffn, plane * slab, unit, width)
    arrived, last_back = tie(received(result, sends), back_stream(1, table, None))
    backs.append(last_back)
    result_base, far = tie(result[0], backs[1][1])
    result = (middle + add_up(*result_base, *arrived)).astype(BF16)
    output = rows_from_layer(result.reshape(micro, -1, width))
    bias_sum = sum(item[3][0] for item in backs)
    bias_all = lax.dynamic_update_slice_in_dim(
        jnp.zeros((own_heads * plane,), F32), bias_sum[:own_heads], own_block * own_heads, 0
    )[:heads]

    def grad_of_packed(hold):
        right, _ = tie(backs[1][0], hold)
        grad = (grad_packed + dot(attended[1][0], right, ((0,), (0,)))).astype(BF16)
        return grad, output, total_over("p", total_over("core", bias_all)), grad_down, grad_out

    state = scatter_first([backs[0][1], far], [item[2] for item in backs], grad_of_packed)
    grad_packed, output, bias_all, grad_down, grad_out = state[2]
    grad_packed = scatter_layers(grad_packed)
    sends, grad_ffn_w = tie(sent(state), grad_ffn_w)
    grad_ffn_w = all_to_all(grad_ffn_w.reshape(plane, slab, 2 * share), members)
    arrived, bias_all = tie(received(state, sends), total_over("q", bias_all))
    normed_grad = add_up(*state[0], *arrived)
    norm_one = lax.rsqrt(jnp.mean(stream * stream, axis=-1, keepdims=True) + EPS)
    unit_one = stream * norm_one
    scaled_one = normed_grad * gain_one
    stream_grad = middle_grad + norm_one * (
        scaled_one - unit_one * jnp.mean(scaled_one * unit_one, axis=-1, keepdims=True)
    )
    stream_grad, bias_all = tie(stream_grad.astype(BF16), bias_all)
    input_grad = rows_from_layer(stream_grad.reshape(micro, -1, width))
    input_grad, grad_packed, grad_ffn_w = tie(input_grad, grad_packed, grad_ffn_w)
    grad_packed = all_to_all(grad_packed.reshape(plane, slab, -1), members)
    grad_bias = total_over("z", bias_all)
    returned = rows_from_plane([jnp.concatenate(pair, axis=0) for pair in zip(output, input_grad)])
    output, input_grad = returned[:micro], returned[micro:].astype(F32)

    if not aligned:
        spread = jnp.zeros((own_heads * depth * plane, width), BF16)
        spread = lax.dynamic_update_slice_in_dim(spread, grad_out, own_block * columns, 0)
        grad_out = lax.psum_scatter(spread[:width], everywhere, scatter_dimension=0, tiled=True)
    grad_out = grad_out.astype(F32)
    grad_down = grad_down.astype(F32)
    grad_gate, grad_up, sums_two = unpack_hidden(grad_ffn_w, (w_gate, w_up), nz)
    grad_query, grad_key, grad_value, grad_outgate, sums_one = unpack_heads(
        grad_packed, (w_query, w_key, w_value, w_outgate), nf, columns
    )
    grad_forget = lax.dot_general(
        grad_packed[:, :, :128], select.reshape(heads, plane, 128), (((0, 2), (1, 2)), ((), ())),
        preferred_element_type=F32,
    )
    sums_one = sums_one[:, 0] + jnp.sum(forget_weight.astype(F32) * grad_forget, axis=1)
    grad_gain_one = sums_one / norm1_gain.astype(F32)
    grad_gain_two = sums_two[:, 0] / norm2_gain.astype(F32)
    return (
        output[:, None], input_grad[:, None], grad_gain_one, grad_query, grad_key, grad_value, grad_outgate,
        grad_out, grad_forget, grad_bias, grad_gain_two, grad_gate, grad_up, grad_down,
    )


def solution(mesh):
    n_ctx, n_fsdp = mesh.shape["ctx"], mesh.shape["fsdp"]
    fine = Mesh(mesh.devices.reshape(n_ctx // 2, 2, n_fsdp // 2, 2), ("z", "core", "p", "q"))
    ctx, fsdp, every = ("z", "core"), ("p", "q"), ("z", "core", "p", "q")
    rows = P(None, fsdp, ctx, None)
    vector, matrix = P(every), P(every, None)
    return jax.shard_map(
        per_device,
        mesh=fine,
        in_specs=(
            rows, rows, P(None, fsdp, None), P(), vector, matrix, matrix, matrix, matrix, matrix, matrix, P(),
            vector, matrix, matrix, matrix,
        ),
        out_specs=(
            rows, rows, vector, matrix, matrix, matrix, matrix, matrix, matrix, P(), vector, matrix, matrix, matrix,
        ),
        check_vma=False,
    )
```

```python
import functools

import jax
import jax.numpy as jnp
from jax import lax
from jax.experimental import pallas as pl
from jax.experimental.pallas import tpu as pltpu
from jax.sharding import Mesh, PartitionSpec as P

EPS = 1e-06
LOW = -1e30
BQ = 256
F32 = jnp.float32
BF16 = jnp.bfloat16
VMEM_LIMIT = 56 * 1024 * 1024


def dot(left, right, contract=((1,), (0,)), out=F32):
    return lax.dot_general(left, right, (contract, ((), ())), preferred_element_type=out)


def xor_permute(x, axis, step):
    n = lax.axis_size(axis)
    return lax.ppermute(x, axis, [(i, i ^ step) for i in range(n)])


def pick(stacked, index):
    return lax.dynamic_index_in_dim(stacked, index, 0, keepdims=False)


def xor_plane(x, step):
    n = lax.axis_size("p") * lax.axis_size("q")
    return lax.ppermute(x, ("p", "q"), [(i, i ^ step) for i in range(n)])


def rows_to_plane(x):
    nf = lax.axis_size("p") * lax.axis_size("q")
    f = lax.axis_index(("p", "q"))
    micro, tokens, width = x.shape
    parts = x.reshape(micro, nf, tokens // nf, width).transpose(1, 0, 2, 3)
    return jnp.stack([pick(parts, f)] + [xor_plane(pick(parts, f ^ k), k) for k in range(1, nf)])


def rows_to_layer(got):
    nz = lax.axis_size("z")
    f, z = lax.axis_index(("p", "q")), lax.axis_index("z")
    return [pick(got, f ^ z)] + [xor_permute(pick(got, f ^ z ^ k), "z", k) for k in range(1, nz)]


def rows_from_layer(y):
    nz = lax.axis_size("z")
    micro, rows, width = y.shape
    rp = rows // nz
    return [y[:, :rp]] + [xor_permute(y[:, k * rp:(k + 1) * rp], "z", k) for k in range(1, nz)]


def rows_from_plane(got):
    nf = lax.axis_size("p") * lax.axis_size("q")
    f, z = lax.axis_index(("p", "q")), lax.axis_index("z")
    got = jnp.stack(got)
    back = [pick(got, z ^ f)] + [xor_plane(pick(got, z ^ f ^ k), k) for k in range(1, nf)]
    back = jnp.stack(back)
    return jnp.concatenate([pick(back, f ^ c) for c in range(nf)], axis=1)


def gather_first(x):
    np_ = lax.axis_size("p")
    return [x, xor_permute(x, "q", 1)] + [xor_permute(x, "p", k) for k in range(1, np_)]


def gather_own_core(first):
    np_ = lax.axis_size("p")
    x, over_q = first[:2]
    half = x.shape[0] // 2
    if np_ == 2:
        over_p = first[2]
        own = [x, over_q, over_p, [xor_permute(over_q[:half], "p", 1), xor_permute(over_p[half:], "q", 1)]]
    else:
        own = [x, over_q]
        for k in range(1, np_):
            own += [first[1 + k], xor_permute(over_q, "p", k)]
    return own


def gather_both_cores(own):
    return own + jax.tree.map(lambda block: xor_permute(block, "core", 1), own)


def gather_rest(first):
    return gather_both_cores(gather_own_core(first))


def gather_plane(x):
    return gather_rest(gather_first(x))


def in_rows(blocks):
    return jnp.concatenate(jax.tree.leaves(blocks), axis=0)


def add_up(*parts):
    return sum(part.astype(F32) for part in parts)


def term(items, number=None):
    operands = []
    for item in items:
        if number is None:
            operands.append((item, pl.BlockSpec(item.shape, lambda i: (0, 0))))
        else:
            operands.append((item, pl.BlockSpec((None,) + item.shape[1:], lambda i: (number, 0, 0))))
    return operands


def read_term(refs):
    parts = [ref[...].astype(F32) for ref in refs]
    return parts[0] if len(parts) == 1 else jnp.concatenate(parts, axis=0)


def rows_kernel(body, terms, outs, name):
    counts = [len(item) for item in terms]
    operands = [pair for item in terms for pair in item]

    def kernel(*refs):
        values, at = [], 0
        for count in counts:
            values.append(read_term(refs[at:at + count]))
            at += count
        for ref, value in zip(refs[at:], body(*values)):
            ref[...] = value.astype(ref.dtype)

    return pl.pallas_call(
        kernel,
        grid=(1,),
        in_specs=[spec for _, spec in operands],
        out_specs=[pl.BlockSpec(shape, lambda i: (0, 0)) for shape, _ in outs],
        out_shape=[jax.ShapeDtypeStruct(shape, kind) for shape, kind in outs],
        compiler_params=pltpu.CompilerParams(vmem_limit_bytes=VMEM_LIMIT),
        name=name,
    )(*[array for array, _ in operands])


def scatter_core(far, near):
    got = [xor_permute(item, "core", 1) for item in far]
    last = 2 * lax.axis_size("p") - 1
    rows, width = sum(item.shape[1] for item in near), near[0].shape[2]
    half = rows // 2

    def body(one, other):
        total = one + other
        return total[:half], total[half:]

    return near, got, rows_kernel(body, [term(near, last), term(got, last)], [((half, width), BF16)] * 2, "sum_last")


def both_cores(near, got, number):
    return jnp.concatenate([add_up(one[number], other[number]) for one, other in zip(near, got)], axis=0)


def scatter_diagonal(near, got, last, beside=None):
    np_ = lax.axis_size("p")
    near, got, last = lax.optimization_barrier((near, got, last))
    made = ()
    if np_ == 2:
        into_q = xor_permute(last[0], "p", 1)
        into_p = xor_permute(last[1], "q", 1)
        if beside is not None:
            into_q, into_p, made = lax.optimization_barrier((into_q, into_p, beside(last)))
        half, width = last[0].shape

        def body(near_q, got_q, near_p, got_p, into_q, into_p):
            to_q, to_p = near_q + got_q, near_p + got_p
            to_q = jnp.concatenate([to_q[:half] + into_q, to_q[half:]], axis=0)
            return to_q, jnp.concatenate([to_p[:half], to_p[half:] + into_p], axis=0)

        to_q, to_p = rows_kernel(
            body, [term(near, 1), term(got, 1), term(near, 2), term(got, 2), term([into_q]), term([into_p])],
            [((2 * half, width), BF16)] * 2, "sum_next",
        )
        return [(near, 0), (got, 0)], [(to_q, "q"), (to_p, "p")], made
    if beside is not None:
        made = beside(last)
    last = jnp.concatenate(last, axis=0)
    pair = [both_cores(near, got, 0), both_cores(near, got, 1)]
    for k in range(1, np_):
        for side in range(2):
            item = last if 2 * k + side == 2 * np_ - 1 else both_cores(near, got, 2 * k + side).astype(BF16)
            pair[side] = pair[side] + xor_permute(item, "p", k).astype(F32)
    return [([pair[0]], None)], [(pair[1].astype(BF16), "q")], made


def scatter_first(far, near, beside=None):
    return scatter_diagonal(*scatter_core(far, near), beside)


def sent(state):
    return [item for item, _ in state[1]]


def received(state, sends):
    return [xor_permute(item, axis, 1) for item, (_, axis) in zip(sends, state[1])]


def sum_terms(parts, arrived):
    return [term(*part) for part in parts] + [term([item]) for item in arrived]


def normed_rows(x):
    return x * lax.rsqrt(jnp.mean(x * x, axis=-1, keepdims=True) + EPS)


def add_and_norm(parts, arrived, own, gain):
    terms = sum_terms(parts, arrived)

    def body(own, gain, *values):
        total = own + sum(values)
        return total, normed_rows(total) * gain

    return rows_kernel(body, [term([own]), term([gain])] + terms, [(own.shape, F32), (own.shape, BF16)], "add_norm")


def norm_back(parts, arrived, above, x, gain, kinds):
    terms = sum_terms(parts, arrived)

    def body(above, x, gain, *values):
        r = lax.rsqrt(jnp.mean(x * x, axis=-1, keepdims=True) + EPS)
        unit, scaled = x * r, sum(values) * gain
        total = above + r * (scaled - unit * jnp.mean(scaled * unit, axis=-1, keepdims=True))
        return [total] * len(kinds)

    return rows_kernel(
        body, [term([above]), term([x]), term([gain])] + terms, [(x.shape, kind) for kind in kinds], "norm_back"
    )


def add_rows(parts, arrived, own):
    return rows_kernel(
        lambda *values: [sum(values)], [term([own])] + sum_terms(parts, arrived), [(own.shape, BF16)], "add_rows"
    )[0]


def total_over(axis, x, step=1):
    while step < lax.axis_size(axis):
        x = x + xor_permute(x, axis, step)
        step *= 2
    return x


def log_sigmoid(z):
    return jnp.minimum(z, 0.0) - jnp.log(1.0 + jnp.exp(-jnp.abs(z)))


def window_of(i, bq, window):
    first = max(0, i * bq - window)
    return first, (i + 1) * bq - first


def pieces(members, rows, chunk):
    per = rows // chunk
    return [(j * per + k, j, k * chunk) for j in range(members) for k in range(per)]


def natural_rows(table, number, chunk):
    return pl.ds(pl.multiple_of(table[number] * chunk, chunk), chunk)


def spread_rows(table, source, far_ref, near_ref, chunk):
    half = near_ref.shape[0]
    for number, j, at in pieces(2 * half, near_ref.shape[1], chunk):
        target = near_ref if j < half else far_ref
        target[j % half, at:at + chunk, :] = source[natural_rows(table, number, chunk), :]


def attend_kernel(heads, depth, chunk, members, table, *refs):
    x_refs, refs = refs[:members], refs[members:]
    w_ref, bias_ref, begin_ref = refs[:3]
    h_ref, qkv_ref, g_ref, z_ref, a_ref, total_ref, cumul_ref, b_ref, gain_ref = refs[-13:-4]
    ka, va, rows, part = refs[-4:]
    total = total_ref.shape[0]
    columns = heads * depth
    bq = min(BQ, total)
    window = total // 2
    scale = jnp.asarray(depth ** -0.5, BF16)
    for number, j, at in pieces(members, x_refs[0].shape[0], chunk):
        part[natural_rows(table, number, chunk), :] = x_refs[j][at:at + chunk, :]
    gains = jnp.transpose(w_ref[:, 0:128].astype(F32))[2 * heads:2 * heads + 2, :]
    gain_ref[...] = jnp.concatenate([gains, jnp.zeros((6, gains.shape[1]), F32)], axis=0)
    gain = gains[0:1, :]
    lower = (
        lax.broadcasted_iota(jnp.int32, (bq, bq), 0) >= lax.broadcasted_iota(jnp.int32, (bq, bq), 1)
    ).astype(F32).astype(BF16)
    carry = jnp.zeros((1, 128), F32)
    for i in range(total // bq):
        here = slice(i * bq, (i + 1) * bq)
        values = part[here, :].astype(F32)
        values = values * lax.rsqrt(jnp.mean(values * values, axis=1, keepdims=True) + EPS) * gain
        h_ref[here, :] = values.astype(BF16)
        tile = dot(h_ref[here, :], w_ref[...])
        logit = tile[:, 0:128] + bias_ref[...]
        z_ref[here, :] = logit
        cumul = dot(lower, log_sigmoid(logit).astype(BF16)) + carry
        cumul_ref[here, :] = cumul
        carry = cumul[bq - 1:bq, :]
        qkv_ref[here, :] = tile[:, 128:128 + 3 * columns].astype(BF16)
        g_ref[here, :] = tile[:, 128 + 3 * columns:]
        for h in range(heads):
            lo = 128 + columns + h * depth
            ka[h, here, :] = tile[:, lo:lo + depth].astype(BF16)
            lo += columns
            va[h, here, 0:depth] = tile[:, lo:lo + depth].astype(BF16)
            va[h, here, depth:] = jnp.ones((bq, 128 - depth), BF16)
    rows[...] = jnp.transpose(cumul_ref[...])
    lane = lax.broadcasted_iota(jnp.int32, (bq, 128), 1)
    for i in range(total // bq):
        first, span = window_of(i, bq, window)
        here = slice(i * bq, (i + 1) * bq)
        place = i * bq + lax.broadcasted_iota(jnp.int32, (bq, span), 0)
        other = first + lax.broadcasted_iota(jnp.int32, (bq, span), 1)
        mask = jnp.where((other <= place) & (other >= begin_ref[here, :]), 0.0, LOW)
        totals = jnp.zeros((bq, 128), F32)
        for h in range(heads):
            query = qkv_ref[here, h * depth:(h + 1) * depth] * scale
            score = dot(query, ka[h, first:first + span, :], ((1,), (1,)))
            score = score - rows[h:h + 1, first:first + span] + mask
            peak = jnp.max(score, axis=1, keepdims=True)
            weight = jnp.exp(score - peak)
            both = dot(weight.astype(BF16), va[h, first:first + span, :])
            a_ref[here, h * depth:(h + 1) * depth] = both[:, 0:depth] / both[:, depth:2 * depth]
            totals = jnp.where(lane == h, peak + jnp.log(both[:, depth:depth + 1]), totals)
        total_ref[here, :] = totals
        part[here, 0:columns] = (a_ref[here, :] * jax.nn.sigmoid(g_ref[here, :])).astype(BF16)
    for number, j, at in pieces(members, b_ref.shape[1], chunk):
        b_ref[j, at:at + chunk, :] = part[natural_rows(table, number, chunk), 0:columns]


def attend_back_kernel(heads, depth, chunk, members, streams, held, table, *refs):
    x_refs, refs = refs[:members], refs[members:]
    extra = members * max(0, streams - 1)
    other_refs, gated_refs, refs = refs[:extra], refs[extra:extra + streams], refs[extra + streams:]
    w_ref, o_ref, qkv_ref, g_ref, z_ref, a_ref, total_ref, cumul_ref, begin_ref = refs[:9]
    refs = refs[held:]
    right_ref, far_ref, near_ref, dbias_ref = refs[9:13]
    part, below_grad, qa, ka, va, da, dkn, dvn, rows, deltas, dcumul = refs[-11:]
    if streams:
        out_grad = jnp.zeros(refs[13].shape, F32)
        for number, ref in enumerate(x_refs + other_refs):
            out_grad = out_grad + dot(gated_refs[number // members][number % members], ref[...], ((0,), (0,)))
        refs[13][...] = out_grad.astype(BF16)
    total = total_ref.shape[0]
    columns = heads * depth
    bq = min(BQ, total)
    window = total // 2
    scale = jnp.asarray(depth ** -0.5, BF16)
    lane = lax.broadcasted_iota(jnp.int32, (bq, 128), 1)
    per = x_refs[0].shape[0] // chunk
    for j in range(members):
        grad = dot(x_refs[j][...], o_ref[...], ((1,), (1,)))
        for k in range(per):
            below_grad[natural_rows(table, j * per + k, chunk), :] = grad[k * chunk:(k + 1) * chunk, :]
    dkn[...] = jnp.zeros_like(dkn)
    dvn[...] = jnp.zeros_like(dvn)
    for i in range(total // bq):
        here = slice(i * bq, (i + 1) * bq)
        grad = below_grad[here, :]
        opened = jax.nn.sigmoid(g_ref[here, :])
        attended = a_ref[here, :]
        below = (grad * opened).astype(BF16)
        right_ref[here, 128 + 3 * columns:] = (grad * attended * opened * (1.0 - opened)).astype(BF16)
        product = below.astype(F32) * attended
        delta = jnp.zeros((bq, 128), F32)
        for h in range(heads):
            da[h, here, :] = below[:, h * depth:(h + 1) * depth]
            delta = jnp.where(
                lane == h, jnp.sum(product[:, h * depth:(h + 1) * depth], axis=1, keepdims=True), delta
            )
            qa[h, here, 0:depth] = qkv_ref[here, h * depth:(h + 1) * depth] * scale
            qa[h, here, depth:] = jnp.ones((bq, 128 - depth), BF16)
            lo = columns + h * depth
            ka[h, here, 0:depth] = qkv_ref[here, lo:lo + depth]
            ka[h, here, depth:] = jnp.ones((bq, 128 - depth), BF16)
            lo += columns
            va[h, here, :] = qkv_ref[here, lo:lo + depth]
        dcumul[here, :] = delta
    deltas[...] = jnp.transpose(dcumul[...])
    rows[...] = jnp.transpose(total_ref[...])
    dcumul[...] = jnp.zeros_like(dcumul)
    for i in range(total // bq):
        first, span = window_of(i, bq, window)
        here, there = slice(i * bq, (i + 1) * bq), slice(first, first + span)
        place = i * bq + lax.broadcasted_iota(jnp.int32, (span, bq), 1)
        other = first + lax.broadcasted_iota(jnp.int32, (span, bq), 0)
        mask = jnp.where((other <= place) & (other >= begin_ref[:, here]), 0.0, LOW)
        for h in range(heads):
            query, below = qa[h, here, :], da[h, here, :]
            score = dot(ka[h, there, 0:depth], query[:, 0:depth], ((1,), (1,)))
            score = score - rows[h:h + 1, here] - cumul_ref[there, h:h + 1] + mask
            weight = jnp.exp(score)
            weight_grad = dot(va[h, there, :], below, ((1,), (1,))) - deltas[h:h + 1, here]
            score_grad = (weight * weight_grad).astype(BF16)
            dvn[h, there, :] += dot(weight.astype(BF16), below)
            dkn[h, there, :] += dot(score_grad, query)
            dq = dot(score_grad, ka[h, there, :], ((0,), (0,)))
            right_ref[here, 128 + h * depth:128 + (h + 1) * depth] = (dq[:, 0:depth] * depth ** -0.5).astype(BF16)
            mine = (lane == h) | (lane == h + heads)
            dcumul[here, :] += jnp.where(mine, dq[:, depth:depth + 1], 0.0)
    upper = (
        lax.broadcasted_iota(jnp.int32, (bq, bq), 0) <= lax.broadcasted_iota(jnp.int32, (bq, bq), 1)
    ).astype(F32)
    carry = jnp.zeros((1, 128), F32)
    sums = jnp.zeros((1, 128), F32)
    for i in reversed(range(total // bq)):
        here = slice(i * bq, (i + 1) * bq)
        change = dcumul[here, :]
        for h in range(heads):
            lo = 128 + columns + h * depth
            right_ref[here, lo:lo + depth] = dkn[h, here, 0:depth].astype(BF16)
            lo += columns
            right_ref[here, lo:lo + depth] = dvn[h, here, :].astype(BF16)
            mine = (lane == h) | (lane == h + heads)
            change = change - jnp.where(mine, dkn[h, here, depth:depth + 1], 0.0)
        summed = carry + jnp.dot(upper, change, precision=lax.Precision.HIGHEST, preferred_element_type=F32)
        carry = summed[0:1, :]
        grad = summed * jax.nn.sigmoid(-z_ref[here, :])
        sums = sums + jnp.sum(grad, axis=0, keepdims=True)
        high = grad.astype(BF16).astype(F32)
        pair = jnp.where(lane < heads, high, jnp.where(lane < 2 * heads, grad - high, 0.0))
        right_ref[here, 0:128] = pair.astype(BF16)
        part[here, :] = dot(right_ref[here, :], w_ref[...], ((1,), (1,))).astype(BF16)
    dbias_ref[...] = jnp.broadcast_to(sums, dbias_ref.shape)
    spread_rows(table, part, far_ref, near_ref, chunk)


def one_stream(blocks, m, streams):
    arrays, specs = [], []
    for block in blocks:
        array, place = (block[m], 0) if isinstance(block, list) else (block, m)
        rows, width = (array.shape[0] if isinstance(block, list) else array.shape[0] // streams), array.shape[1]
        arrays.append(array)
        specs.append(pl.BlockSpec((rows, width), lambda i, t, place=place: (place, 0), pipeline_mode=pl.Buffered(1)))
    return arrays, specs


def fixed(array):
    return pl.BlockSpec(array.shape, lambda i, t: (0,) * array.ndim, pipeline_mode=pl.Buffered(1))


def own_part(shape, m):
    return pl.BlockSpec(shape, lambda i, t: (m, 0), pipeline_mode=pl.Buffered(1))


def attend(table, blocks, m, streams, weights, bias, begin, into, heads, depth, chunk):
    arrays, specs = one_stream(blocks, m, streams)
    members, (rows, width) = len(arrays), specs[0].block_shape
    total = begin.shape[0]
    columns = heads * depth
    begin = begin[:, None]
    into = [] if into is None else [into]
    outs = [
        ((streams * total, width), BF16), ((total, 3 * columns), BF16), ((total, columns), F32), ((total, 128), F32),
        ((total, columns), F32), ((total, 128), F32), ((total, 128), F32), ((members, rows, columns), BF16),
        ((8, width), F32),
    ]
    out_shape = [jax.ShapeDtypeStruct(shape, kind) for shape, kind in outs]
    return pl.pallas_call(
        functools.partial(attend_kernel, heads, depth, chunk, members),
        grid_spec=pltpu.PrefetchScalarGridSpec(
            num_scalar_prefetch=1,
            grid=(1,),
            in_specs=specs + [fixed(weights), fixed(bias), fixed(begin)] + [pl.BlockSpec(memory_space=pl.ANY)] * len(into),
            out_specs=[own_part((total, width), m)] + [fixed(item) for item in out_shape[1:]],
            scratch_shapes=[
                pltpu.VMEM((heads, total, depth), BF16),
                pltpu.VMEM((heads, total, 128), BF16),
                pltpu.VMEM((128, total), F32),
                pltpu.VMEM((total, width), BF16),
            ],
        ),
        out_shape=out_shape,
        compiler_params=pltpu.CompilerParams(vmem_limit_bytes=VMEM_LIMIT),
        input_output_aliases={1 + members + 3: 0} if into else {},
        cost_estimate=pl.CostEstimate(flops=14 * 10 ** 9, bytes_accessed=10 ** 7, transcendentals=0),
        name="attend",
    )(table, *arrays, weights, bias, begin, *into)


def attend_back(table, blocks, m, streams, weights, out_w, kept, begin, gated, into, heads, depth, chunk):
    arrays, specs = one_stream(blocks, m, streams)
    members, (rows, width) = len(arrays), specs[0].block_shape
    total = begin.shape[0]
    columns = heads * depth
    begin = begin[None, :]
    gated = [] if gated is None else gated
    into = [] if into is None else [into]
    for other in range(1, len(gated)):
        other_arrays, other_specs = one_stream(blocks, other, streams)
        arrays, specs = arrays + other_arrays, specs + other_specs
    outs = [
        ((streams * total, 128 + 4 * columns), BF16), ((members // 2, rows, width), BF16), ((members // 2, rows, width), BF16),
        ((8, 128), F32),
    ] + [((columns, width), BF16)] * (len(gated) > 0)
    out_shape = [jax.ShapeDtypeStruct(shape, kind) for shape, kind in outs]
    return pl.pallas_call(
        functools.partial(attend_back_kernel, heads, depth, chunk, members, len(gated), len(into)),
        grid_spec=pltpu.PrefetchScalarGridSpec(
            num_scalar_prefetch=1,
            grid=(1,),
            in_specs=specs + [fixed(item) for item in (*gated, weights, out_w, *kept, begin)]
            + [pl.BlockSpec(memory_space=pl.ANY)] * len(into),
            out_specs=[own_part((total, 128 + 4 * columns), m)] + [fixed(item) for item in out_shape[1:]],
            scratch_shapes=[
                pltpu.VMEM((total, width), BF16),
                pltpu.VMEM((total, columns), F32),
                pltpu.VMEM((heads, total, 128), BF16),
                pltpu.VMEM((heads, total, 128), BF16),
                pltpu.VMEM((heads, total, depth), BF16),
                pltpu.VMEM((heads, total, depth), BF16),
                pltpu.VMEM((heads, total, 128), F32),
                pltpu.VMEM((heads, total, depth), F32),
                pltpu.VMEM((128, total), F32),
                pltpu.VMEM((128, total), F32),
                pltpu.VMEM((total, 128), F32),
            ],
        ),
        out_shape=out_shape,
        compiler_params=pltpu.CompilerParams(vmem_limit_bytes=VMEM_LIMIT),
        input_output_aliases={1 + len(arrays) + len(gated) + 3 + len(kept): 0} if into else {},
        cost_estimate=pl.CostEstimate(flops=20 * 10 ** 9, bytes_accessed=10 ** 7, transcendentals=0),
        name="attend_back",
    )(table, *arrays, *gated, weights, out_w, *kept, begin, *into)


def out_kernel(b_ref, o_ref, far_ref, near_ref):
    half = near_ref.shape[0]
    for j in range(2 * half):
        target = near_ref if j < half else far_ref
        target[j % half] = dot(b_ref[j], o_ref[...]).astype(BF16)


def out_product(gated, weights):
    members, rows, _ = gated.shape
    shape = jax.ShapeDtypeStruct((members // 2, rows, weights.shape[1]), BF16)
    return pl.pallas_call(
        out_kernel,
        out_shape=[shape, shape],
        compiler_params=pltpu.CompilerParams(vmem_limit_bytes=VMEM_LIMIT),
        name="out_product",
    )(gated, weights)


def ffn_kernel(h_ref, e_ref, w_ref, d_ref, *refs):
    m_ref, g_ref, part_ref = refs[-3:]
    down = d_ref[...].reshape(-1, d_ref.shape[-1])
    share = down.shape[0]
    pre = dot(h_ref[...], w_ref[...])
    gate, up = pre[:, :share], pre[:, share:]
    grad = dot(e_ref[...], down, ((1,), (1,)))
    opened = jax.nn.sigmoid(gate)
    silu = gate * opened
    m_ref[...] = (silu * up).astype(BF16)
    g_ref[:, :share] = (grad * up * (opened * (1.0 + gate * (1.0 - opened)))).astype(BF16)
    g_ref[:, share:] = (grad * silu).astype(BF16)
    part_ref[...] = dot(g_ref[...], w_ref[...], ((1,), (1,))).astype(BF16)


def ffn(normed, upstream, weights, down, unit, first, count, into):
    rows, width = normed.shape
    share = down.shape[0] * unit

    def blocks(lanes, shift):
        return pl.BlockSpec((BQ, lanes), lambda i: (i + shift, 0))

    def fixed(shape):
        return pl.BlockSpec(shape, lambda i: (0,) * len(shape), pipeline_mode=pl.Buffered(1))

    kept = [] if into is None else list(into)
    return pl.pallas_call(
        ffn_kernel,
        grid=(count,),
        in_specs=[blocks(width, first), blocks(width, first), fixed(weights.shape), fixed((down.shape[0], unit, width))]
        + [pl.BlockSpec(memory_space=pl.ANY)] * len(kept),
        out_specs=[
            blocks(share, first), blocks(2 * share, first), pl.BlockSpec((None, BQ, width), lambda i: (i, 0, 0)),
        ],
        out_shape=[
            jax.ShapeDtypeStruct((rows, share), BF16),
            jax.ShapeDtypeStruct((rows, 2 * share), BF16),
            jax.ShapeDtypeStruct((count, BQ, width), BF16),
        ],
        input_output_aliases={4 + i: i for i in range(len(kept))},
        compiler_params=pltpu.CompilerParams(vmem_limit_bytes=VMEM_LIMIT),
        cost_estimate=pl.CostEstimate(
            flops=10 * count * BQ * width * share, bytes_accessed=count * BQ * width * 8, transcendentals=0
        ),
        name="ffn",
    )(normed, upstream, weights, down, *kept)


def layout(body, shapes, kind, *arrays):
    kinds = kind if isinstance(kind, list) else [kind] * len(shapes)
    out_shape = [jax.ShapeDtypeStruct(shape, own) for shape, own in zip(shapes, kinds)]
    return pl.pallas_call(body, out_shape=out_shape, name="layout")(*arrays)


def block_columns(block, columns, limit):
    return min(block * columns, limit), max(0, min((block + 1) * columns, limit) - min(block * columns, limit))


def pack_heads(forget, weights, nf, columns):
    slab, width = weights[0].shape
    plane = 2 * nf

    def body(f_ref, *refs):
        out = refs[-1]
        for t in range(plane):
            out[t, :, 0:128] = f_ref[:, t * 128:(t + 1) * 128]
            first, count = block_columns(t % nf * 2 + t // nf, columns, width)
            for number, ref in enumerate(refs[:-1]):
                lo = 128 + number * columns
                if count < columns:
                    out[t, :, lo:lo + columns] = jnp.zeros((slab, columns), BF16)
                if count:
                    out[t, :, lo:lo + count] = ref[:, first:first + count]

    return layout(body, [(plane, slab, 128 + 4 * columns)], BF16, forget, *weights)[0]


def unpack_heads(grads, weights, nf, columns):
    plane, slab, _ = grads.shape
    width = weights[0].shape[1]

    def body(x_ref, *refs):
        sums = jnp.zeros((slab, 1), F32)
        for number in range(4):
            weight, out = refs[number], refs[4 + number]
            for t in range(plane):
                first, count = block_columns(t % nf * 2 + t // nf, columns, width)
                lo = 128 + number * columns
                if count:
                    out[:, first:first + count] = x_ref[t, :, lo:lo + count].astype(F32)
            sums = sums + jnp.sum(weight[...].astype(F32) * out[...], axis=1, keepdims=True)
        refs[8][...] = sums

    return layout(body, [(slab, width)] * 4 + [(slab, 1)], F32, grads, *weights)


def pack_hidden(gate, up, nz, plane):
    slab, hidden = gate.shape
    unit = hidden // (nz * plane)

    def body(gate_ref, up_ref, out):
        for number, ref in enumerate((gate_ref, up_ref)):
            for t in range(plane):
                for z in range(nz):
                    lo = (number * nz + z) * unit
                    at = (z * plane + t) * unit
                    out[t, :, lo:lo + unit] = ref[:, at:at + unit]

    return layout(body, [(plane, slab, 2 * nz * unit)], BF16, gate, up)[0]


def unpack_hidden(grads, weights, nz):
    plane, slab, both = grads.shape
    unit = both // (2 * nz)

    def body(x_ref, *refs):
        sums = jnp.zeros((slab, 1), F32)
        for number in range(2):
            weight, out = refs[number], refs[2 + number]
            for t in range(plane):
                for z in range(nz):
                    lo = (number * nz + z) * unit
                    at = (z * plane + t) * unit
                    out[:, at:at + unit] = x_ref[t, :, lo:lo + unit].astype(F32)
            sums = sums + jnp.sum(weight[...].astype(F32) * out[...], axis=1, keepdims=True)
        refs[4][...] = sums

    return layout(body, [(slab, plane * nz * unit)] * 2 + [(slab, 1)], F32, grads, *weights)


def doc_begins(lengths_row, total):
    ends = jnp.cumsum(lengths_row)
    begins = ends - lengths_row
    place = jnp.arange(total, dtype=jnp.int32)
    inside = (place[:, None] >= begins[None, :]) & (place[:, None] < ends[None, :])
    return jnp.sum(jnp.where(inside, begins[None, :], 0), axis=1)


def all_to_all(x, axes):
    return lax.all_to_all(x, axes, split_axis=0, concat_axis=0, tiled=True)


def scatter_layers(grad):
    return lax.psum_scatter(grad, "z", scatter_dimension=0, tiled=True)


def join_grads(grad, down, nz):
    lanes, width = grad.shape[1], down.shape[1]
    grad, down = grad.reshape(nz, -1, lanes), down.reshape(nz, -1, width)
    parts = [grad] + [down[:, :, i * lanes:(i + 1) * lanes] for i in range(width // lanes)]
    rest = width % lanes
    if rest:
        count = lanes // rest
        rows = down.shape[1] // count
        over = down[:, :, width - rest:].reshape(nz, count, rows, rest)
        parts.append(jnp.concatenate([over[:, i] for i in range(count)], axis=2))
    return jnp.concatenate(parts, axis=1).reshape(-1, lanes)


def part_grads(joined, slabs, rows, width):
    lanes = joined.shape[1]
    grad, joined = joined[:slabs], joined[slabs:]
    whole = width // lanes
    parts = [joined[i * rows:(i + 1) * rows] for i in range(whole)]
    rest = width % lanes
    if rest:
        over = joined[whole * rows:]
        parts.append(jnp.concatenate([over[:, i * rest:(i + 1) * rest] for i in range(lanes // rest)], axis=0))
    return grad, jnp.concatenate(parts, axis=1)


def tie(*values):
    return lax.optimization_barrier(values)


def per_device(
    inputs, cotangent, lengths, deal, norm1_gain, w_query, w_key, w_value, w_outgate, w_out,
    forget_weight, forget_bias, norm2_gain, w_gate, w_up, w_down,
):
    nz, np_, nq = lax.axis_size("z"), lax.axis_size("p"), lax.axis_size("q")
    z, core, f = lax.axis_index("z"), lax.axis_index("core"), lax.axis_index(("p", "q"))
    nf = np_ * nq
    n_ctx = 2 * nz
    plane = 2 * nf
    devices = nz * plane
    everywhere, members = ("z", "core", "p", "q"), ("core", "p", "q")
    micro, _, tokens, width = inputs.shape
    heads = forget_bias.shape[0]
    depth = width // heads
    own_heads = -(-heads // plane)
    columns = own_heads * depth
    spare_heads = own_heads * plane - heads
    total = tokens * n_ctx
    chunk = tokens // nf
    block = tokens // 2
    hidden = w_gate.shape[1]
    slab = w_query.shape[0]
    unit = hidden // devices
    share = nz * unit
    own_block = f * 2 + core
    aligned = spare_heads == 0 and columns == nf * slab

    member_block = [t % nf * 2 + t // nf for t in range(plane)]
    head_of = jnp.arange(heads, dtype=jnp.int32)[:, None]
    lane_of = jnp.arange(plane * 128, dtype=jnp.int32)[None, :]
    lane_head = jnp.asarray(member_block, jnp.int32)[lane_of // 128] * own_heads + lane_of % 128 % own_heads
    select = ((lane_head == head_of) & (lane_of % 128 < 2 * own_heads)).astype(BF16)
    first_lanes = dot(forget_weight, select, out=BF16)
    for number, gain in enumerate((norm1_gain, norm2_gain)):
        first_lanes = jnp.where(lane_of % 128 == 2 * own_heads + number, gain[:, None], first_lanes)
    packed = pack_heads(first_lanes, (w_query, w_key, w_value, w_outgate), nf, columns)
    own = rows_to_layer(rows_to_plane(inputs[:, 0]))
    packed, own[1] = tie(packed, own[1])
    packed = all_to_all(packed, members)
    if aligned:
        out_w = jnp.stack([w_out] + [xor_permute(w_out, "z", k) for k in range(1, nz)])
        out_w = jnp.stack([pick(out_w, z ^ c) for c in range(nz)])
    else:
        out_w = jnp.pad(lax.all_gather(w_out, everywhere, axis=0, tiled=True), ((0, spare_heads * depth), (0, 0)))
        out_w = lax.dynamic_slice_in_dim(out_w, own_block * columns, columns, 0)
    own = jnp.concatenate(own, axis=1).reshape(-1, width)
    packed, own, out_w = tie(packed, own, out_w)
    packed = lax.all_gather(packed, "z", axis=0).reshape(width, -1)
    gathered = gather_first(own)
    ffn_send, gathered = tie(pack_hidden(w_gate, w_up, nz, plane), gathered)
    gathered = gather_rest(gathered)
    if aligned:
        out_w = all_to_all(out_w, ("p", "q")).reshape(columns, width)
    ffn_w = all_to_all(ffn_send, members)
    out_w, ffn_w, gathered, cotangent = tie(out_w, ffn_w, gathered, cotangent)
    upstream_own = rows_to_plane(cotangent[:, 0])
    packed, upstream_own = tie(packed, upstream_own)
    upstream_own = jnp.concatenate(rows_to_layer(upstream_own), axis=1).reshape(-1, width)

    lengths_own = lax.ppermute(
        lengths[:, 0], everywhere,
        [
            (((f_to * 2 + c) * nf) + z_to, ((z_to * 2 + c) * nf) + f_to)
            for z_to in range(nz) for c in range(2) for f_to in range(nf)
        ],
    )
    begins = [doc_begins(lengths_own[m], total) for m in range(micro)]
    number = jnp.arange(total // chunk, dtype=jnp.int32)
    from_core = core ^ (number // (nf * nz))
    from_f = f ^ (number // nz % nf)
    from_z = z ^ (number % nz)
    inside = from_f * chunk

    def natural_table(deal_row):
        dealt = jnp.take(deal_row, from_z * 2 + from_core)
        start = jnp.where(inside < block, dealt, 2 * n_ctx - 1 - dealt) * block + inside % block
        return (start // chunk).astype(jnp.int32)

    tables = [natural_table(deal[m]) for m in range(micro)]
    all_bias = jnp.pad(forget_bias, (0, spare_heads))
    own_bias = lax.dynamic_slice_in_dim(all_bias, own_block * own_heads, own_heads, 0)[None]
    bias_row = jnp.concatenate([own_bias, own_bias, jnp.zeros((1, 128 - 2 * own_heads), F32)], axis=1)

    def attend_stream(m, table, into):
        return attend(table, gathered, m, micro, packed, bias_row, begins[m], into, own_heads, depth, chunk)

    attended = [attend_stream(0, tables[0], None)]
    gains = attended[0][8]
    gated = [attended[0][7]]
    parts = [out_product(gated[0], out_w)]
    table, upstream_own, gains, ffn_w, w_down = tie(tables[1], upstream_own, gains, ffn_w, w_down)
    ffn_w = lax.all_gather(ffn_w, "z", axis=0).reshape(width, 2 * share)
    down_w = lax.all_gather(w_down, "z", axis=0)
    attended.append(attend_stream(1, table, attended[0][0]))
    upstream = gather_first(upstream_own)
    last_gated, upstream = tie(attended[1][7], upstream)
    gated.append(last_gated)
    upstream, last_part = tie(gather_own_core(upstream), out_product(gated[1], out_w))
    parts.append(last_part)
    upstream = in_rows(gather_both_cores(upstream))
    gain_one, gain_two = gains[0:1], gains[1:2]
    state = scatter_first([item[0] for item in parts], [item[1] for item in parts])
    middle, normed_two = add_and_norm(state[0], received(state, sent(state)), own, gain_two)
    normed_two = in_rows(gather_plane(normed_two))

    half_blocks = normed_two.shape[0] // BQ // 2
    weights = (normed_two, upstream, ffn_w, down_w, unit)
    activ, ffn_grad, far = ffn(*weights, half_blocks, half_blocks, None)
    activ, ffn_grad, near = ffn(*weights, 0, half_blocks, (activ, ffn_grad))
    def grad_of_ffn(hold):
        kept, _ = tie(normed_two, hold)
        return dot(kept, ffn_grad, ((0,), (0,)), BF16)

    state = scatter_first([far], [near], grad_of_ffn)
    grad_ffn_w = state[2]
    sends, held = tie(sent(state), activ)
    grad_down = dot(held, upstream, ((0,), (0,)), BF16)
    arrived, grad_ffn = tie(received(state, sends), join_grads(grad_ffn_w, grad_down, nz))
    grad_ffn = scatter_layers(grad_ffn)
    middle_grad, branch_own = norm_back(state[0], arrived, upstream_own, middle, gain_two, (F32, BF16))
    branch_own, held = tie(branch_own, activ)
    half = activ.shape[0] // 2
    down_rows = down_w.reshape(share, width)
    part_out = [
        dot(item, down_rows, out=BF16).reshape(plane // 2, -1, width) for item in (held[half:], held[:half])
    ]
    branch_grad, part_out = tie(gather_first(branch_own), part_out)
    result = scatter_core(part_out[:1], part_out[1:])
    branch_grad = gather_rest(branch_grad)

    def back_stream(m, table, gated, into):
        return attend_back(
            table, branch_grad, m, micro, packed, out_w, attended[m][1:7], begins[m], gated, into, own_heads, depth, chunk
        )

    def first_back(hold):
        table, _ = tie(tables[0], hold)
        return back_stream(0, table, gated, None)

    result = scatter_diagonal(*result, first_back)
    backs = [result[2]]
    sends, table = tie(sent(result), tables[1])
    grad_out = backs[0][4]
    if aligned:
        grad_out = all_to_all(grad_out.reshape(nf, slab, width), ("p", "q"))
    arrived, grad_out, last_back = tie(received(result, sends), grad_out, back_stream(1, table, None, backs[0][0]))
    backs.append(last_back)
    grad_packed = dot(attended[1][0], backs[1][0], ((0,), (0,)), BF16)
    bias_sum = sum(item[3][0] for item in backs)
    bias_all = lax.dynamic_update_slice_in_dim(
        jnp.zeros((own_heads * plane,), F32), bias_sum[:own_heads], own_block * own_heads, 0
    )[:heads]

    def rows_of_output(hold):
        own_arrived, own_bias, _ = tie(arrived, bias_all, hold)
        rows = add_rows(result[0], own_arrived, middle)
        return rows, total_over("p", total_over("core", own_bias))

    near, got, last = scatter_core([item[1] for item in backs], [item[2] for item in backs])
    grad_packed, last, grad_ffn = tie(grad_packed, last, grad_ffn)
    grad_packed = scatter_layers(grad_packed)
    state = scatter_diagonal(near, got, last, rows_of_output)
    output, bias_all = state[2]
    output = rows_from_layer(output.reshape(micro, -1, width))
    sends, grad_ffn = tie(sent(state), grad_ffn)
    grad_ffn_w, grad_down = part_grads(grad_ffn, plane * slab, unit, width)
    grad_ffn_w = all_to_all(grad_ffn_w.reshape(plane, slab, 2 * share), members)
    arrived, bias_all = tie(received(state, sends), total_over("q", bias_all))
    (stream_grad,) = norm_back(state[0], arrived, middle_grad, own, gain_one, (BF16,))
    stream_grad, bias_all = tie(stream_grad, bias_all)
    input_grad = rows_from_layer(stream_grad.reshape(micro, -1, width))
    bias_all = bias_all + xor_permute(bias_all, "z", 1)
    input_grad, grad_packed, bias_all = tie(input_grad, grad_packed, bias_all)
    if aligned:
        grad_out, grad_packed = tie(grad_out, grad_packed)
        grad_out = scatter_layers(grad_out.reshape(nf * slab, width))
    grad_packed = all_to_all(grad_packed.reshape(plane, slab, -1), members)
    input_grad, grad_packed, bias_all = tie(input_grad, grad_packed, bias_all)
    grad_bias = total_over("z", bias_all, 2)
    returned = rows_from_plane([jnp.concatenate(pair, axis=0) for pair in zip(output, input_grad)])
    output, input_grad = returned[:micro], returned[micro:].astype(F32)

    grad_gate, grad_up, sums_two = unpack_hidden(grad_ffn_w, (w_gate, w_up), nz)
    if not aligned:
        spread = jnp.zeros((own_heads * depth * plane, width), BF16)
        spread = lax.dynamic_update_slice_in_dim(spread, grad_out, own_block * columns, 0)
        grad_out = lax.psum_scatter(spread[:width], everywhere, scatter_dimension=0, tiled=True)
    grad_out = grad_out.astype(F32)
    grad_down = grad_down.astype(F32)
    grad_query, grad_key, grad_value, grad_outgate, sums_one = unpack_heads(
        grad_packed, (w_query, w_key, w_value, w_outgate), nf, columns
    )
    grad_forget = lax.dot_general(
        grad_packed[:, :, :128], select.reshape(heads, plane, 128), (((0, 2), (1, 2)), ((), ())),
        preferred_element_type=F32,
    )
    sums_one = sums_one[:, 0] + jnp.sum(forget_weight.astype(F32) * grad_forget, axis=1)
    grad_gain_one = sums_one / norm1_gain.astype(F32)
    grad_gain_two = sums_two[:, 0] / norm2_gain.astype(F32)
    return (
        output[:, None], input_grad[:, None], grad_gain_one, grad_query, grad_key, grad_value, grad_outgate,
        grad_out, grad_forget, grad_bias, grad_gain_two, grad_gate, grad_up, grad_down,
    )


def solution(mesh):
    n_ctx, n_fsdp = mesh.shape["ctx"], mesh.shape["fsdp"]
    fine = Mesh(mesh.devices.reshape(n_ctx // 2, 2, n_fsdp // 2, 2), ("z", "core", "p", "q"))
    ctx, fsdp, every = ("z", "core"), ("p", "q"), ("z", "core", "p", "q")
    rows = P(None, fsdp, ctx, None)
    vector, matrix = P(every), P(every, None)
    return jax.shard_map(
        per_device,
        mesh=fine,
        in_specs=(
            rows, rows, P(None, fsdp, None), P(), vector, matrix, matrix, matrix, matrix, matrix, matrix, P(),
            vector, matrix, matrix, matrix,
        ),
        out_specs=(
            rows, rows, vector, matrix, matrix, matrix, matrix, matrix, matrix, P(), vector, matrix, matrix, matrix,
        ),
        check_vma=False,
    )
```

```python
import functools

import jax
import jax.numpy as jnp
from jax import lax
from jax.experimental import pallas as pl
from jax.experimental.pallas import tpu as pltpu
from jax.sharding import Mesh, PartitionSpec as P

EPS = 1e-06
LOW = -1e30
BQ = 256
F32 = jnp.float32
BF16 = jnp.bfloat16
VMEM_LIMIT = 56 * 1024 * 1024


def dot(left, right, contract=((1,), (0,)), out=F32):
    return lax.dot_general(left, right, (contract, ((), ())), preferred_element_type=out)


def xor_permute(x, axis, step):
    n = lax.axis_size(axis)
    return lax.ppermute(x, axis, [(i, i ^ step) for i in range(n)])


def pick(stacked, index):
    return lax.dynamic_index_in_dim(stacked, index, 0, keepdims=False)


def xor_plane(x, step):
    n = lax.axis_size("p") * lax.axis_size("q")
    return lax.ppermute(x, ("p", "q"), [(i, i ^ step) for i in range(n)])


def rows_to_plane(x):
    nf = lax.axis_size("p") * lax.axis_size("q")
    f = lax.axis_index(("p", "q"))
    micro, tokens, width = x.shape
    parts = x.reshape(micro, nf, tokens // nf, width).transpose(1, 0, 2, 3)
    return jnp.stack([pick(parts, f)] + [xor_plane(pick(parts, f ^ k), k) for k in range(1, nf)])


def rows_to_layer(got):
    nz = lax.axis_size("z")
    f, z = lax.axis_index(("p", "q")), lax.axis_index("z")
    return [pick(got, f ^ z)] + [xor_permute(pick(got, f ^ z ^ k), "z", k) for k in range(1, nz)]


def rows_from_layer(y):
    nz = lax.axis_size("z")
    micro, rows, width = y.shape
    rp = rows // nz
    return [y[:, :rp]] + [xor_permute(y[:, k * rp:(k + 1) * rp], "z", k) for k in range(1, nz)]


def rows_from_plane(got):
    nf = lax.axis_size("p") * lax.axis_size("q")
    f, z = lax.axis_index(("p", "q")), lax.axis_index("z")
    got = jnp.stack(got)
    back = [pick(got, z ^ f)] + [xor_plane(pick(got, z ^ f ^ k), k) for k in range(1, nf)]
    back = jnp.stack(back)
    return jnp.concatenate([pick(back, f ^ c) for c in range(nf)], axis=1)


def gather_first(x):
    np_ = lax.axis_size("p")
    return [x, xor_permute(x, "q", 1)] + [xor_permute(x, "p", k) for k in range(1, np_)]


def gather_own_core(first):
    np_ = lax.axis_size("p")
    x, over_q = first[:2]
    half = x.shape[0] // 2
    if np_ == 2:
        over_p = first[2]
        own = [x, over_q, over_p, [xor_permute(over_q[:half], "p", 1), xor_permute(over_p[half:], "q", 1)]]
    else:
        own = [x, over_q]
        for k in range(1, np_):
            own += [first[1 + k], xor_permute(over_q, "p", k)]
    return own


def gather_both_cores(own):
    return own + jax.tree.map(lambda block: xor_permute(block, "core", 1), own)


def gather_rest(first):
    return gather_both_cores(gather_own_core(first))


def gather_plane(x):
    return gather_rest(gather_first(x))


def in_rows(blocks):
    return jnp.concatenate(jax.tree.leaves(blocks), axis=0)


def add_up(*parts):
    return sum(part.astype(F32) for part in parts)


def term(items, number=None):
    operands = []
    for item in items:
        if number is None:
            operands.append((item, pl.BlockSpec(item.shape, lambda i: (0, 0))))
        else:
            operands.append((item, pl.BlockSpec((None,) + item.shape[1:], lambda i: (number, 0, 0))))
    return operands


def read_term(refs):
    parts = [ref[...].astype(F32) for ref in refs]
    return parts[0] if len(parts) == 1 else jnp.concatenate(parts, axis=0)


def rows_kernel(body, terms, outs, name):
    counts = [len(item) for item in terms]
    operands = [pair for item in terms for pair in item]

    def kernel(*refs):
        values, at = [], 0
        for count in counts:
            values.append(read_term(refs[at:at + count]))
            at += count
        for ref, value in zip(refs[at:], body(*values)):
            ref[...] = value.astype(ref.dtype)

    return pl.pallas_call(
        kernel,
        grid=(1,),
        in_specs=[spec for _, spec in operands],
        out_specs=[pl.BlockSpec(shape, lambda i: (0, 0)) for shape, _ in outs],
        out_shape=[jax.ShapeDtypeStruct(shape, kind) for shape, kind in outs],
        compiler_params=pltpu.CompilerParams(vmem_limit_bytes=VMEM_LIMIT),
        name=name,
    )(*[array for array, _ in operands])


def scatter_core(far, near):
    got = [xor_permute(item, "core", 1) for item in far]
    last = 2 * lax.axis_size("p") - 1
    rows, width = sum(item.shape[1] for item in near), near[0].shape[2]
    half = rows // 2

    def body(one, other):
        total = one + other
        return total[:half], total[half:]

    return near, got, rows_kernel(body, [term(near, last), term(got, last)], [((half, width), BF16)] * 2, "sum_last")


def both_cores(near, got, number):
    return jnp.concatenate([add_up(one[number], other[number]) for one, other in zip(near, got)], axis=0)


def scatter_diagonal(near, got, last, beside=None):
    np_ = lax.axis_size("p")
    near, got, last = lax.optimization_barrier((near, got, last))
    made = ()
    if np_ == 2:
        into_q = xor_permute(last[0], "p", 1)
        into_p = xor_permute(last[1], "q", 1)
        if beside is not None:
            into_q, into_p, made = lax.optimization_barrier((into_q, into_p, beside(last)))
        half, width = last[0].shape

        def body(near_q, got_q, near_p, got_p, into_q, into_p):
            to_q, to_p = near_q + got_q, near_p + got_p
            to_q = jnp.concatenate([to_q[:half] + into_q, to_q[half:]], axis=0)
            return to_q, jnp.concatenate([to_p[:half], to_p[half:] + into_p], axis=0)

        to_q, to_p = rows_kernel(
            body, [term(near, 1), term(got, 1), term(near, 2), term(got, 2), term([into_q]), term([into_p])],
            [((2 * half, width), BF16)] * 2, "sum_next",
        )
        return [(near, 0), (got, 0)], [(to_q, "q"), (to_p, "p")], made
    if beside is not None:
        made = beside(last)
    last = jnp.concatenate(last, axis=0)
    pair = [both_cores(near, got, 0), both_cores(near, got, 1)]
    for k in range(1, np_):
        for side in range(2):
            item = last if 2 * k + side == 2 * np_ - 1 else both_cores(near, got, 2 * k + side).astype(BF16)
            pair[side] = pair[side] + xor_permute(item, "p", k).astype(F32)
    return [([pair[0]], None)], [(pair[1].astype(BF16), "q")], made


def scatter_first(far, near, beside=None):
    return scatter_diagonal(*scatter_core(far, near), beside)


def sent(state):
    return [item for item, _ in state[1]]


def received(state, sends):
    return [xor_permute(item, axis, 1) for item, (_, axis) in zip(sends, state[1])]


def sum_terms(parts, arrived):
    return [term(*part) for part in parts] + [term([item]) for item in arrived]


def normed_rows(x):
    return x * lax.rsqrt(jnp.mean(x * x, axis=-1, keepdims=True) + EPS)


def add_and_norm(parts, arrived, own, gain):
    terms = sum_terms(parts, arrived)

    def body(own, gain, *values):
        total = own + sum(values)
        return total, normed_rows(total) * gain

    return rows_kernel(body, [term([own]), term([gain])] + terms, [(own.shape, F32), (own.shape, BF16)], "add_norm")


def norm_back(parts, arrived, above, x, gain, kinds):
    terms = sum_terms(parts, arrived)

    def body(above, x, gain, *values):
        r = lax.rsqrt(jnp.mean(x * x, axis=-1, keepdims=True) + EPS)
        unit, scaled = x * r, sum(values) * gain
        total = above + r * (scaled - unit * jnp.mean(scaled * unit, axis=-1, keepdims=True))
        return [total] * len(kinds)

    return rows_kernel(
        body, [term([above]), term([x]), term([gain])] + terms, [(x.shape, kind) for kind in kinds], "norm_back"
    )


def add_rows(parts, arrived, own):
    return rows_kernel(
        lambda *values: [sum(values)], [term([own])] + sum_terms(parts, arrived), [(own.shape, BF16)], "add_rows"
    )[0]


def total_over(axis, x, step=1):
    while step < lax.axis_size(axis):
        x = x + xor_permute(x, axis, step)
        step *= 2
    return x


def log_sigmoid(z):
    return jnp.minimum(z, 0.0) - jnp.log(1.0 + jnp.exp(-jnp.abs(z)))


def window_of(i, bq, window):
    first = max(0, i * bq - window)
    return first, (i + 1) * bq - first


def pieces(members, rows, chunk):
    per = rows // chunk
    return [(j * per + k, j, k * chunk) for j in range(members) for k in range(per)]


def natural_rows(table, number, chunk):
    return pl.ds(pl.multiple_of(table[number] * chunk, chunk), chunk)


def spread_rows(table, source, far_ref, near_ref, chunk):
    half = near_ref.shape[0]
    for number, j, at in pieces(2 * half, near_ref.shape[1], chunk):
        target = near_ref if j < half else far_ref
        target[j % half, at:at + chunk, :] = source[natural_rows(table, number, chunk), :]


def attend_kernel(heads, depth, chunk, members, table, *refs):
    x_refs, refs = refs[:members], refs[members:]
    w_ref, bias_ref, begin_ref = refs[:3]
    h_ref, qkv_ref, g_ref, z_ref, a_ref, total_ref, cumul_ref, b_ref, gain_ref = refs[-13:-4]
    ka, va, rows, part = refs[-4:]
    total = total_ref.shape[0]
    columns = heads * depth
    bq = min(BQ, total)
    window = total // 2
    scale = jnp.asarray(depth ** -0.5, BF16)
    for number, j, at in pieces(members, x_refs[0].shape[0], chunk):
        part[natural_rows(table, number, chunk), :] = x_refs[j][at:at + chunk, :]
    gains = jnp.transpose(w_ref[:, 0:128].astype(F32))[2 * heads:2 * heads + 2, :]
    gain_ref[...] = jnp.concatenate([gains, jnp.zeros((6, gains.shape[1]), F32)], axis=0)
    gain = gains[0:1, :]
    lower = (
        lax.broadcasted_iota(jnp.int32, (bq, bq), 0) >= lax.broadcasted_iota(jnp.int32, (bq, bq), 1)
    ).astype(F32).astype(BF16)
    carry = jnp.zeros((1, 128), F32)
    for i in range(total // bq):
        here = slice(i * bq, (i + 1) * bq)
        values = part[here, :].astype(F32)
        values = values * lax.rsqrt(jnp.mean(values * values, axis=1, keepdims=True) + EPS) * gain
        h_ref[here, :] = values.astype(BF16)
        tile = dot(h_ref[here, :], w_ref[...])
        logit = tile[:, 0:128] + bias_ref[...]
        z_ref[here, :] = logit
        cumul = dot(lower, log_sigmoid(logit).astype(BF16)) + carry
        cumul_ref[here, :] = cumul
        carry = cumul[bq - 1:bq, :]
        qkv_ref[here, :] = tile[:, 128:128 + 3 * columns].astype(BF16)
        g_ref[here, :] = tile[:, 128 + 3 * columns:]
        for h in range(heads):
            lo = 128 + columns + h * depth
            ka[h, here, :] = tile[:, lo:lo + depth].astype(BF16)
            lo += columns
            va[h, here, 0:depth] = tile[:, lo:lo + depth].astype(BF16)
            va[h, here, depth:] = jnp.ones((bq, 128 - depth), BF16)
    rows[...] = jnp.transpose(cumul_ref[...])
    lane = lax.broadcasted_iota(jnp.int32, (bq, 128), 1)
    for i in range(total // bq):
        first, span = window_of(i, bq, window)
        here = slice(i * bq, (i + 1) * bq)
        place = i * bq + lax.broadcasted_iota(jnp.int32, (bq, span), 0)
        other = first + lax.broadcasted_iota(jnp.int32, (bq, span), 1)
        mask = jnp.where((other <= place) & (other >= begin_ref[here, :]), 0.0, LOW)
        totals = jnp.zeros((bq, 128), F32)
        for h in range(heads):
            query = qkv_ref[here, h * depth:(h + 1) * depth] * scale
            score = dot(query, ka[h, first:first + span, :], ((1,), (1,)))
            score = score - rows[h:h + 1, first:first + span] + mask
            peak = jnp.max(score, axis=1, keepdims=True)
            weight = jnp.exp(score - peak)
            both = dot(weight.astype(BF16), va[h, first:first + span, :])
            a_ref[here, h * depth:(h + 1) * depth] = both[:, 0:depth] / both[:, depth:2 * depth]
            totals = jnp.where(lane == h, peak + jnp.log(both[:, depth:depth + 1]), totals)
        total_ref[here, :] = totals
        part[here, 0:columns] = (a_ref[here, :] * jax.nn.sigmoid(g_ref[here, :])).astype(BF16)
    for number, j, at in pieces(members, b_ref.shape[1], chunk):
        b_ref[j, at:at + chunk, :] = part[natural_rows(table, number, chunk), 0:columns]


def attend_back_kernel(heads, depth, chunk, members, streams, held, table, *refs):
    x_refs, refs = refs[:members], refs[members:]
    extra = members * max(0, streams - 1)
    other_refs, gated_refs, refs = refs[:extra], refs[extra:extra + streams], refs[extra + streams:]
    w_ref, o_ref, qkv_ref, g_ref, z_ref, a_ref, total_ref, cumul_ref, begin_ref = refs[:9]
    refs = refs[held:]
    right_ref, far_ref, near_ref, dbias_ref = refs[9:13]
    part, below_grad, qa, ka, va, da, dkn, dvn, rows, deltas, dcumul = refs[-11:]
    if streams:
        out_grad = jnp.zeros(refs[13].shape, F32)
        for number, ref in enumerate(x_refs + other_refs):
            out_grad = out_grad + dot(gated_refs[number // members][number % members], ref[...], ((0,), (0,)))
        refs[13][...] = out_grad.astype(BF16)
    total = total_ref.shape[0]
    columns = heads * depth
    bq = min(BQ, total)
    window = total // 2
    scale = jnp.asarray(depth ** -0.5, BF16)
    lane = lax.broadcasted_iota(jnp.int32, (bq, 128), 1)
    per = x_refs[0].shape[0] // chunk
    for j in range(members):
        grad = dot(x_refs[j][...], o_ref[...], ((1,), (1,)))
        for k in range(per):
            below_grad[natural_rows(table, j * per + k, chunk), :] = grad[k * chunk:(k + 1) * chunk, :]
    dkn[...] = jnp.zeros_like(dkn)
    dvn[...] = jnp.zeros_like(dvn)
    for i in range(total // bq):
        here = slice(i * bq, (i + 1) * bq)
        grad = below_grad[here, :]
        opened = jax.nn.sigmoid(g_ref[here, :])
        attended = a_ref[here, :]
        below = (grad * opened).astype(BF16)
        right_ref[here, 128 + 3 * columns:] = (grad * attended * opened * (1.0 - opened)).astype(BF16)
        product = below.astype(F32) * attended
        delta = jnp.zeros((bq, 128), F32)
        for h in range(heads):
            da[h, here, :] = below[:, h * depth:(h + 1) * depth]
            delta = jnp.where(
                lane == h, jnp.sum(product[:, h * depth:(h + 1) * depth], axis=1, keepdims=True), delta
            )
            qa[h, here, 0:depth] = qkv_ref[here, h * depth:(h + 1) * depth] * scale
            qa[h, here, depth:] = jnp.ones((bq, 128 - depth), BF16)
            lo = columns + h * depth
            ka[h, here, 0:depth] = qkv_ref[here, lo:lo + depth]
            ka[h, here, depth:] = jnp.ones((bq, 128 - depth), BF16)
            lo += columns
            va[h, here, :] = qkv_ref[here, lo:lo + depth]
        dcumul[here, :] = delta
    deltas[...] = jnp.transpose(dcumul[...])
    rows[...] = jnp.transpose(total_ref[...])
    dcumul[...] = jnp.zeros_like(dcumul)
    for i in range(total // bq):
        first, span = window_of(i, bq, window)
        here, there = slice(i * bq, (i + 1) * bq), slice(first, first + span)
        place = i * bq + lax.broadcasted_iota(jnp.int32, (span, bq), 1)
        other = first + lax.broadcasted_iota(jnp.int32, (span, bq), 0)
        mask = jnp.where((other <= place) & (other >= begin_ref[:, here]), 0.0, LOW)
        for h in range(heads):
            query, below = qa[h, here, :], da[h, here, :]
            score = dot(ka[h, there, 0:depth], query[:, 0:depth], ((1,), (1,)))
            score = score - rows[h:h + 1, here] - cumul_ref[there, h:h + 1] + mask
            weight = jnp.exp(score)
            weight_grad = dot(va[h, there, :], below, ((1,), (1,))) - deltas[h:h + 1, here]
            score_grad = (weight * weight_grad).astype(BF16)
            dvn[h, there, :] += dot(weight.astype(BF16), below)
            dkn[h, there, :] += dot(score_grad, query)
            dq = dot(score_grad, ka[h, there, :], ((0,), (0,)))
            right_ref[here, 128 + h * depth:128 + (h + 1) * depth] = (dq[:, 0:depth] * depth ** -0.5).astype(BF16)
            mine = (lane == h) | (lane == h + heads)
            dcumul[here, :] += jnp.where(mine, dq[:, depth:depth + 1], 0.0)
    upper = (
        lax.broadcasted_iota(jnp.int32, (bq, bq), 0) <= lax.broadcasted_iota(jnp.int32, (bq, bq), 1)
    ).astype(F32)
    carry = jnp.zeros((1, 128), F32)
    sums = jnp.zeros((1, 128), F32)
    for i in reversed(range(total // bq)):
        here = slice(i * bq, (i + 1) * bq)
        change = dcumul[here, :]
        for h in range(heads):
            lo = 128 + columns + h * depth
            right_ref[here, lo:lo + depth] = dkn[h, here, 0:depth].astype(BF16)
            lo += columns
            right_ref[here, lo:lo + depth] = dvn[h, here, :].astype(BF16)
            mine = (lane == h) | (lane == h + heads)
            change = change - jnp.where(mine, dkn[h, here, depth:depth + 1], 0.0)
        summed = carry + jnp.dot(upper, change, precision=lax.Precision.HIGHEST, preferred_element_type=F32)
        carry = summed[0:1, :]
        grad = summed * jax.nn.sigmoid(-z_ref[here, :])
        sums = sums + jnp.sum(grad, axis=0, keepdims=True)
        high = grad.astype(BF16).astype(F32)
        pair = jnp.where(lane < heads, high, jnp.where(lane < 2 * heads, grad - high, 0.0))
        right_ref[here, 0:128] = pair.astype(BF16)
        part[here, :] = dot(right_ref[here, :], w_ref[...], ((1,), (1,))).astype(BF16)
    dbias_ref[...] = jnp.broadcast_to(sums, dbias_ref.shape)
    spread_rows(table, part, far_ref, near_ref, chunk)


def one_stream(blocks, m, streams):
    arrays, specs = [], []
    for block in blocks:
        array, place = (block[m], 0) if isinstance(block, list) else (block, m)
        rows, width = (array.shape[0] if isinstance(block, list) else array.shape[0] // streams), array.shape[1]
        arrays.append(array)
        specs.append(pl.BlockSpec((rows, width), lambda i, t, place=place: (place, 0), pipeline_mode=pl.Buffered(1)))
    return arrays, specs


def fixed(array):
    return pl.BlockSpec(array.shape, lambda i, t: (0,) * array.ndim, pipeline_mode=pl.Buffered(1))


def own_part(shape, m):
    return pl.BlockSpec(shape, lambda i, t: (m, 0), pipeline_mode=pl.Buffered(1))


def attend(table, blocks, m, streams, weights, bias, begin, into, heads, depth, chunk):
    arrays, specs = one_stream(blocks, m, streams)
    members, (rows, width) = len(arrays), specs[0].block_shape
    total = begin.shape[0]
    columns = heads * depth
    begin = begin[:, None]
    into = [] if into is None else [into]
    outs = [
        ((streams * total, width), BF16), ((total, 3 * columns), BF16), ((total, columns), F32), ((total, 128), F32),
        ((total, columns), F32), ((total, 128), F32), ((total, 128), F32), ((members, rows, columns), BF16),
        ((8, width), F32),
    ]
    out_shape = [jax.ShapeDtypeStruct(shape, kind) for shape, kind in outs]
    return pl.pallas_call(
        functools.partial(attend_kernel, heads, depth, chunk, members),
        grid_spec=pltpu.PrefetchScalarGridSpec(
            num_scalar_prefetch=1,
            grid=(1,),
            in_specs=specs + [fixed(weights), fixed(bias), fixed(begin)] + [pl.BlockSpec(memory_space=pl.ANY)] * len(into),
            out_specs=[own_part((total, width), m)] + [fixed(item) for item in out_shape[1:]],
            scratch_shapes=[
                pltpu.VMEM((heads, total, depth), BF16),
                pltpu.VMEM((heads, total, 128), BF16),
                pltpu.VMEM((128, total), F32),
                pltpu.VMEM((total, width), BF16),
            ],
        ),
        out_shape=out_shape,
        compiler_params=pltpu.CompilerParams(vmem_limit_bytes=VMEM_LIMIT),
        input_output_aliases={1 + members + 3: 0} if into else {},
        cost_estimate=pl.CostEstimate(flops=14 * 10 ** 9, bytes_accessed=10 ** 7, transcendentals=0),
        name="attend",
    )(table, *arrays, weights, bias, begin, *into)


def attend_back(table, blocks, m, streams, weights, out_w, kept, begin, gated, into, heads, depth, chunk):
    arrays, specs = one_stream(blocks, m, streams)
    members, (rows, width) = len(arrays), specs[0].block_shape
    total = begin.shape[0]
    columns = heads * depth
    begin = begin[None, :]
    gated = [] if gated is None else gated
    into = [] if into is None else [into]
    for other in range(1, len(gated)):
        other_arrays, other_specs = one_stream(blocks, other, streams)
        arrays, specs = arrays + other_arrays, specs + other_specs
    outs = [
        ((streams * total, 128 + 4 * columns), BF16), ((members // 2, rows, width), BF16), ((members // 2, rows, width), BF16),
        ((8, 128), F32),
    ] + [((columns, width), BF16)] * (len(gated) > 0)
    out_shape = [jax.ShapeDtypeStruct(shape, kind) for shape, kind in outs]
    return pl.pallas_call(
        functools.partial(attend_back_kernel, heads, depth, chunk, members, len(gated), len(into)),
        grid_spec=pltpu.PrefetchScalarGridSpec(
            num_scalar_prefetch=1,
            grid=(1,),
            in_specs=specs + [fixed(item) for item in (*gated, weights, out_w, *kept, begin)]
            + [pl.BlockSpec(memory_space=pl.ANY)] * len(into),
            out_specs=[own_part((total, 128 + 4 * columns), m)] + [fixed(item) for item in out_shape[1:]],
            scratch_shapes=[
                pltpu.VMEM((total, width), BF16),
                pltpu.VMEM((total, columns), F32),
                pltpu.VMEM((heads, total, 128), BF16),
                pltpu.VMEM((heads, total, 128), BF16),
                pltpu.VMEM((heads, total, depth), BF16),
                pltpu.VMEM((heads, total, depth), BF16),
                pltpu.VMEM((heads, total, 128), F32),
                pltpu.VMEM((heads, total, depth), F32),
                pltpu.VMEM((128, total), F32),
                pltpu.VMEM((128, total), F32),
                pltpu.VMEM((total, 128), F32),
            ],
        ),
        out_shape=out_shape,
        compiler_params=pltpu.CompilerParams(vmem_limit_bytes=VMEM_LIMIT),
        input_output_aliases={1 + len(arrays) + len(gated) + 3 + len(kept): 0} if into else {},
        cost_estimate=pl.CostEstimate(flops=20 * 10 ** 9, bytes_accessed=10 ** 7, transcendentals=0),
        name="attend_back",
    )(table, *arrays, *gated, weights, out_w, *kept, begin, *into)


def out_kernel(b_ref, o_ref, far_ref, near_ref):
    half = near_ref.shape[0]
    for j in range(2 * half):
        target = near_ref if j < half else far_ref
        target[j % half] = dot(b_ref[j], o_ref[...]).astype(BF16)


def out_product(gated, weights):
    members, rows, _ = gated.shape
    shape = jax.ShapeDtypeStruct((members // 2, rows, weights.shape[1]), BF16)
    return pl.pallas_call(
        out_kernel,
        out_shape=[shape, shape],
        compiler_params=pltpu.CompilerParams(vmem_limit_bytes=VMEM_LIMIT),
        name="out_product",
    )(gated, weights)


def ffn_kernel(h_ref, e_ref, w_ref, d_ref, *refs):
    m_ref, g_ref, part_ref = refs[-3:]
    down = d_ref[...].reshape(-1, d_ref.shape[-1])
    share = down.shape[0]
    pre = dot(h_ref[...], w_ref[...])
    gate, up = pre[:, :share], pre[:, share:]
    grad = dot(e_ref[...], down, ((1,), (1,)))
    opened = jax.nn.sigmoid(gate)
    silu = gate * opened
    m_ref[...] = (silu * up).astype(BF16)
    g_ref[:, :share] = (grad * up * (opened * (1.0 + gate * (1.0 - opened)))).astype(BF16)
    g_ref[:, share:] = (grad * silu).astype(BF16)
    part_ref[...] = dot(g_ref[...], w_ref[...], ((1,), (1,))).astype(BF16)


def ffn(normed, upstream, weights, down, unit, first, count, into):
    rows, width = normed.shape
    share = down.shape[0] * unit

    def blocks(lanes, shift):
        return pl.BlockSpec((BQ, lanes), lambda i: (i + shift, 0))

    def fixed(shape):
        return pl.BlockSpec(shape, lambda i: (0,) * len(shape), pipeline_mode=pl.Buffered(1))

    kept = [] if into is None else list(into)
    return pl.pallas_call(
        ffn_kernel,
        grid=(count,),
        in_specs=[blocks(width, first), blocks(width, first), fixed(weights.shape), fixed((down.shape[0], unit, width))]
        + [pl.BlockSpec(memory_space=pl.ANY)] * len(kept),
        out_specs=[
            blocks(share, first), blocks(2 * share, first), pl.BlockSpec((None, BQ, width), lambda i: (i, 0, 0)),
        ],
        out_shape=[
            jax.ShapeDtypeStruct((rows, share), BF16),
            jax.ShapeDtypeStruct((rows, 2 * share), BF16),
            jax.ShapeDtypeStruct((count, BQ, width), BF16),
        ],
        input_output_aliases={4 + i: i for i in range(len(kept))},
        compiler_params=pltpu.CompilerParams(vmem_limit_bytes=VMEM_LIMIT),
        cost_estimate=pl.CostEstimate(
            flops=10 * count * BQ * width * share, bytes_accessed=count * BQ * width * 8, transcendentals=0
        ),
        name="ffn",
    )(normed, upstream, weights, down, *kept)


def layout(body, shapes, kind, *arrays):
    kinds = kind if isinstance(kind, list) else [kind] * len(shapes)
    out_shape = [jax.ShapeDtypeStruct(shape, own) for shape, own in zip(shapes, kinds)]
    return pl.pallas_call(body, out_shape=out_shape, name="layout")(*arrays)


def block_columns(block, columns, limit):
    return min(block * columns, limit), max(0, min((block + 1) * columns, limit) - min(block * columns, limit))


def pack_heads(forget, weights, nf, columns):
    slab, width = weights[0].shape
    plane = 2 * nf

    def body(f_ref, *refs):
        out = refs[-1]
        for t in range(plane):
            out[t, :, 0:128] = f_ref[:, t * 128:(t + 1) * 128]
            first, count = block_columns(t % nf * 2 + t // nf, columns, width)
            for number, ref in enumerate(refs[:-1]):
                lo = 128 + number * columns
                if count < columns:
                    out[t, :, lo:lo + columns] = jnp.zeros((slab, columns), BF16)
                if count:
                    out[t, :, lo:lo + count] = ref[:, first:first + count]

    return layout(body, [(plane, slab, 128 + 4 * columns)], BF16, forget, *weights)[0]


def unpack_heads(grads, weights, nf, columns):
    plane, slab, _ = grads.shape
    width = weights[0].shape[1]

    def body(x_ref, *refs):
        sums = jnp.zeros((slab, 1), F32)
        for number in range(4):
            weight, out = refs[number], refs[4 + number]
            for t in range(plane):
                first, count = block_columns(t % nf * 2 + t // nf, columns, width)
                lo = 128 + number * columns
                if count:
                    out[:, first:first + count] = x_ref[t, :, lo:lo + count].astype(F32)
            sums = sums + jnp.sum(weight[...].astype(F32) * out[...], axis=1, keepdims=True)
        refs[8][...] = sums

    return layout(body, [(slab, width)] * 4 + [(slab, 1)], F32, grads, *weights)


def pack_hidden(gate, up, nz, plane):
    slab, hidden = gate.shape
    unit = hidden // (nz * plane)

    def body(gate_ref, up_ref, out):
        for number, ref in enumerate((gate_ref, up_ref)):
            for t in range(plane):
                for z in range(nz):
                    lo = (number * nz + z) * unit
                    at = (z * plane + t) * unit
                    out[t, :, lo:lo + unit] = ref[:, at:at + unit]

    return layout(body, [(plane, slab, 2 * nz * unit)], BF16, gate, up)[0]


def unpack_hidden(grads, weights, nz):
    plane, slab, both = grads.shape
    unit = both // (2 * nz)

    def body(x_ref, *refs):
        sums = jnp.zeros((slab, 1), F32)
        for number in range(2):
            weight, out = refs[number], refs[2 + number]
            for t in range(plane):
                for z in range(nz):
                    lo = (number * nz + z) * unit
                    at = (z * plane + t) * unit
                    out[:, at:at + unit] = x_ref[t, :, lo:lo + unit].astype(F32)
            sums = sums + jnp.sum(weight[...].astype(F32) * out[...], axis=1, keepdims=True)
        refs[4][...] = sums

    return layout(body, [(slab, plane * nz * unit)] * 2 + [(slab, 1)], F32, grads, *weights)


def doc_begins(lengths_row, total):
    ends = jnp.cumsum(lengths_row)
    begins = ends - lengths_row
    place = jnp.arange(total, dtype=jnp.int32)
    inside = (place[:, None] >= begins[None, :]) & (place[:, None] < ends[None, :])
    return jnp.sum(jnp.where(inside, begins[None, :], 0), axis=1)


def all_to_all(x, axes):
    return lax.all_to_all(x, axes, split_axis=0, concat_axis=0, tiled=True)


def scatter_layers(grad):
    return lax.psum_scatter(grad, "z", scatter_dimension=0, tiled=True)


def join_grads(grad, down, nz):
    lanes, width = grad.shape[1], down.shape[1]
    grad, down = grad.reshape(nz, -1, lanes), down.reshape(nz, -1, width)
    parts = [grad] + [down[:, :, i * lanes:(i + 1) * lanes] for i in range(width // lanes)]
    rest = width % lanes
    if rest:
        count = lanes // rest
        rows = down.shape[1] // count
        over = down[:, :, width - rest:].reshape(nz, count, rows, rest)
        parts.append(jnp.concatenate([over[:, i] for i in range(count)], axis=2))
    return jnp.concatenate(parts, axis=1).reshape(-1, lanes)


def part_grads(joined, slabs, rows, width):
    lanes = joined.shape[1]
    grad, joined = joined[:slabs], joined[slabs:]
    whole = width // lanes
    parts = [joined[i * rows:(i + 1) * rows] for i in range(whole)]
    rest = width % lanes
    if rest:
        over = joined[whole * rows:]
        parts.append(jnp.concatenate([over[:, i * rest:(i + 1) * rest] for i in range(lanes // rest)], axis=0))
    return grad, jnp.concatenate(parts, axis=1)


def tie(*values):
    return lax.optimization_barrier(values)


def per_device(
    inputs, cotangent, lengths, deal, norm1_gain, w_query, w_key, w_value, w_outgate, w_out,
    forget_weight, forget_bias, norm2_gain, w_gate, w_up, w_down,
):
    nz, np_, nq = lax.axis_size("z"), lax.axis_size("p"), lax.axis_size("q")
    z, core, f = lax.axis_index("z"), lax.axis_index("core"), lax.axis_index(("p", "q"))
    nf = np_ * nq
    n_ctx = 2 * nz
    plane = 2 * nf
    devices = nz * plane
    everywhere, members = ("z", "core", "p", "q"), ("core", "p", "q")
    micro, _, tokens, width = inputs.shape
    heads = forget_bias.shape[0]
    depth = width // heads
    own_heads = -(-heads // plane)
    columns = own_heads * depth
    spare_heads = own_heads * plane - heads
    total = tokens * n_ctx
    chunk = tokens // nf
    block = tokens // 2
    hidden = w_gate.shape[1]
    slab = w_query.shape[0]
    unit = hidden // devices
    share = nz * unit
    own_block = f * 2 + core
    aligned = spare_heads == 0 and columns == nf * slab

    member_block = [t % nf * 2 + t // nf for t in range(plane)]
    head_of = jnp.arange(heads, dtype=jnp.int32)[:, None]
    lane_of = jnp.arange(plane * 128, dtype=jnp.int32)[None, :]
    lane_head = jnp.asarray(member_block, jnp.int32)[lane_of // 128] * own_heads + lane_of % 128 % own_heads
    select = ((lane_head == head_of) & (lane_of % 128 < 2 * own_heads)).astype(BF16)
    first_lanes = dot(forget_weight, select, out=BF16)
    for number, gain in enumerate((norm1_gain, norm2_gain)):
        first_lanes = jnp.where(lane_of % 128 == 2 * own_heads + number, gain[:, None], first_lanes)
    packed = pack_heads(first_lanes, (w_query, w_key, w_value, w_outgate), nf, columns)
    own = rows_to_layer(rows_to_plane(inputs[:, 0]))
    packed, own[1] = tie(packed, own[1])
    packed = all_to_all(packed, members)
    if aligned:
        out_w = jnp.stack([w_out] + [xor_permute(w_out, "z", k) for k in range(1, nz)])
        out_w = jnp.stack([pick(out_w, z ^ c) for c in range(nz)])
    else:
        out_w = jnp.pad(lax.all_gather(w_out, everywhere, axis=0, tiled=True), ((0, spare_heads * depth), (0, 0)))
        out_w = lax.dynamic_slice_in_dim(out_w, own_block * columns, columns, 0)
    own = jnp.concatenate(own, axis=1).reshape(-1, width)
    packed, own, out_w = tie(packed, own, out_w)
    packed = lax.all_gather(packed, "z", axis=0).reshape(width, -1)
    gathered = gather_first(own)
    ffn_send, gathered = tie(pack_hidden(w_gate, w_up, nz, plane), gathered)
    gathered = gather_rest(gathered)
    if aligned:
        out_w = all_to_all(out_w, ("p", "q")).reshape(columns, width)
    ffn_w = all_to_all(ffn_send, members)
    out_w, ffn_w, gathered, cotangent = tie(out_w, ffn_w, gathered, cotangent)
    upstream_own = rows_to_plane(cotangent[:, 0])
    packed, upstream_own = tie(packed, upstream_own)
    upstream_own = jnp.concatenate(rows_to_layer(upstream_own), axis=1).reshape(-1, width)

    lengths_own = lax.ppermute(
        lengths[:, 0], everywhere,
        [
            (((f_to * 2 + c) * nf) + z_to, ((z_to * 2 + c) * nf) + f_to)
            for z_to in range(nz) for c in range(2) for f_to in range(nf)
        ],
    )
    begins = [doc_begins(lengths_own[m], total) for m in range(micro)]
    number = jnp.arange(total // chunk, dtype=jnp.int32)
    from_core = core ^ (number // (nf * nz))
    from_f = f ^ (number // nz % nf)
    from_z = z ^ (number % nz)
    inside = from_f * chunk

    def natural_table(deal_row):
        dealt = jnp.take(deal_row, from_z * 2 + from_core)
        start = jnp.where(inside < block, dealt, 2 * n_ctx - 1 - dealt) * block + inside % block
        return (start // chunk).astype(jnp.int32)

    tables = [natural_table(deal[m]) for m in range(micro)]
    all_bias = jnp.pad(forget_bias, (0, spare_heads))
    own_bias = lax.dynamic_slice_in_dim(all_bias, own_block * own_heads, own_heads, 0)[None]
    bias_row = jnp.concatenate([own_bias, own_bias, jnp.zeros((1, 128 - 2 * own_heads), F32)], axis=1)

    def attend_stream(m, table, into):
        return attend(table, gathered, m, micro, packed, bias_row, begins[m], into, own_heads, depth, chunk)

    attended = [attend_stream(0, tables[0], None)]
    gains = attended[0][8]
    gated = [attended[0][7]]
    parts = [out_product(gated[0], out_w)]
    table, upstream_own, gains, ffn_w, w_down = tie(tables[1], upstream_own, gains, ffn_w, w_down)
    ffn_w = lax.all_gather(ffn_w, "z", axis=0).reshape(width, 2 * share)
    down_w = lax.all_gather(w_down, "z", axis=0)
    attended.append(attend_stream(1, table, attended[0][0]))
    upstream = gather_first(upstream_own)
    last_gated, upstream = tie(attended[1][7], upstream)
    gated.append(last_gated)
    upstream, last_part = tie(gather_own_core(upstream), out_product(gated[1], out_w))
    parts.append(last_part)
    upstream = in_rows(gather_both_cores(upstream))
    gain_one, gain_two = gains[0:1], gains[1:2]
    state = scatter_first([item[0] for item in parts], [item[1] for item in parts])
    middle, normed_two = add_and_norm(state[0], received(state, sent(state)), own, gain_two)
    normed_two = in_rows(gather_plane(normed_two))

    half_blocks = normed_two.shape[0] // BQ // 2
    weights = (normed_two, upstream, ffn_w, down_w, unit)
    activ, ffn_grad, far = ffn(*weights, half_blocks, half_blocks, None)
    activ, ffn_grad, near = ffn(*weights, 0, half_blocks, (activ, ffn_grad))
    def grad_of_ffn(hold):
        kept, _ = tie(normed_two, hold)
        return dot(kept, ffn_grad, ((0,), (0,)), BF16)

    state = scatter_first([far], [near], grad_of_ffn)
    grad_ffn_w = state[2]
    sends, held = tie(sent(state), activ)
    grad_down = dot(held, upstream, ((0,), (0,)), BF16)
    arrived, grad_ffn = tie(received(state, sends), join_grads(grad_ffn_w, grad_down, nz))
    grad_ffn = scatter_layers(grad_ffn)
    middle_grad, branch_own = norm_back(state[0], arrived, upstream_own, middle, gain_two, (F32, BF16))
    branch_own, held = tie(branch_own, activ)
    half = activ.shape[0] // 2
    down_rows = down_w.reshape(share, width)
    part_out = [
        dot(item, down_rows, out=BF16).reshape(plane // 2, -1, width) for item in (held[half:], held[:half])
    ]
    branch_grad, part_out = tie(gather_first(branch_own), part_out)
    result = scatter_core(part_out[:1], part_out[1:])
    branch_grad = gather_rest(branch_grad)

    def back_stream(m, table, gated, into):
        return attend_back(
            table, branch_grad, m, micro, packed, out_w, attended[m][1:7], begins[m], gated, into, own_heads, depth, chunk
        )

    def first_back(hold):
        table, _ = tie(tables[0], hold)
        return back_stream(0, table, gated, None)

    result = scatter_diagonal(*result, first_back)
    backs = [result[2]]
    sends, table = tie(sent(result), tables[1])
    grad_out = backs[0][4]
    if aligned:
        grad_out = all_to_all(grad_out.reshape(nf, slab, width), ("p", "q"))
    arrived, grad_out, last_back = tie(received(result, sends), grad_out, back_stream(1, table, None, backs[0][0]))
    backs.append(last_back)
    grad_packed = dot(attended[1][0], backs[1][0], ((0,), (0,)), BF16)
    bias_sum = sum(item[3][0] for item in backs)
    bias_all = lax.dynamic_update_slice_in_dim(
        jnp.zeros((own_heads * plane,), F32), bias_sum[:own_heads], own_block * own_heads, 0
    )[:heads]

    def rows_of_output(hold):
        own_arrived, own_bias, _ = tie(arrived, bias_all, hold)
        rows = add_rows(result[0], own_arrived, middle)
        own_bias = total_over("core", own_bias)
        return rows, own_bias + xor_permute(own_bias, "z", 1)

    near, got, last = scatter_core([item[1] for item in backs], [item[2] for item in backs])
    grad_packed, last, grad_ffn = tie(grad_packed, last, grad_ffn)
    grad_packed = scatter_layers(grad_packed)
    state = scatter_diagonal(near, got, last, rows_of_output)
    output, bias_all = state[2]
    sends, grad_ffn, grad_out = tie(sent(state), grad_ffn, grad_out)
    grad_ffn_w, grad_down = part_grads(grad_ffn, plane * slab, unit, width)
    grad_ffn_w = all_to_all(grad_ffn_w.reshape(plane, slab, 2 * share), members)
    arrived, bias_all = tie(received(state, sends), total_over("z", bias_all, 2))
    (stream_grad,) = norm_back(state[0], arrived, middle_grad, own, gain_one, (BF16,))
    stream_grad, bias_all = tie(stream_grad, bias_all)
    returned = jnp.concatenate([output, stream_grad], axis=0).reshape(2 * micro, -1, width)
    returned = rows_from_layer(returned)
    grad_bias = total_over("q", total_over("p", bias_all))
    returned, grad_packed, grad_bias, grad_out = tie(returned, grad_packed, grad_bias, grad_out)
    if aligned:
        grad_out = scatter_layers(grad_out.reshape(nf * slab, width))
    grad_packed = all_to_all(grad_packed.reshape(plane, slab, -1), members)
    returned, grad_packed = tie(rows_from_plane(returned), grad_packed)
    output, input_grad = returned[:micro], returned[micro:].astype(F32)

    grad_gate, grad_up, sums_two = unpack_hidden(grad_ffn_w, (w_gate, w_up), nz)
    if not aligned:
        spread = jnp.zeros((own_heads * depth * plane, width), BF16)
        spread = lax.dynamic_update_slice_in_dim(spread, grad_out, own_block * columns, 0)
        grad_out = lax.psum_scatter(spread[:width], everywhere, scatter_dimension=0, tiled=True)
    grad_out = grad_out.astype(F32)
    grad_down = grad_down.astype(F32)
    grad_query, grad_key, grad_value, grad_outgate, sums_one = unpack_heads(
        grad_packed, (w_query, w_key, w_value, w_outgate), nf, columns
    )
    grad_forget = lax.dot_general(
        grad_packed[:, :, :128], select.reshape(heads, plane, 128), (((0, 2), (1, 2)), ((), ())),
        preferred_element_type=F32,
    )
    sums_one = sums_one[:, 0] + jnp.sum(forget_weight.astype(F32) * grad_forget, axis=1)
    grad_gain_one = sums_one / norm1_gain.astype(F32)
    grad_gain_two = sums_two[:, 0] / norm2_gain.astype(F32)
    return (
        output[:, None], input_grad[:, None], grad_gain_one, grad_query, grad_key, grad_value, grad_outgate,
        grad_out, grad_forget, grad_bias, grad_gain_two, grad_gate, grad_up, grad_down,
    )


def solution(mesh):
    n_ctx, n_fsdp = mesh.shape["ctx"], mesh.shape["fsdp"]
    fine = Mesh(mesh.devices.reshape(n_ctx // 2, 2, n_fsdp // 2, 2), ("z", "core", "p", "q"))
    ctx, fsdp, every = ("z", "core"), ("p", "q"), ("z", "core", "p", "q")
    rows = P(None, fsdp, ctx, None)
    vector, matrix = P(every), P(every, None)
    return jax.shard_map(
        per_device,
        mesh=fine,
        in_specs=(
            rows, rows, P(None, fsdp, None), P(), vector, matrix, matrix, matrix, matrix, matrix, matrix, P(),
            vector, matrix, matrix, matrix,
        ),
        out_specs=(
            rows, rows, vector, matrix, matrix, matrix, matrix, matrix, matrix, P(), vector, matrix, matrix, matrix,
        ),
        check_vma=False,
    )
```

```python
import functools

import jax
import jax.numpy as jnp
from jax import lax
from jax.experimental import pallas as pl
from jax.experimental.pallas import tpu as pltpu
from jax.sharding import Mesh, PartitionSpec as P

EPS = 1e-06
LOW = -1e30
BQ = 256
F32 = jnp.float32
BF16 = jnp.bfloat16
VMEM_LIMIT = 56 * 1024 * 1024


def dot(left, right, contract=((1,), (0,)), out=F32):
    return lax.dot_general(left, right, (contract, ((), ())), preferred_element_type=out)


def xor_permute(x, axis, step):
    n = lax.axis_size(axis)
    return lax.ppermute(x, axis, [(i, i ^ step) for i in range(n)])


def pick(stacked, index):
    return lax.dynamic_index_in_dim(stacked, index, 0, keepdims=False)


def xor_plane(x, step):
    n = lax.axis_size("p") * lax.axis_size("q")
    return lax.ppermute(x, ("p", "q"), [(i, i ^ step) for i in range(n)])


def rows_to_plane(x):
    nf = lax.axis_size("p") * lax.axis_size("q")
    f = lax.axis_index(("p", "q"))
    micro, tokens, width = x.shape
    parts = x.reshape(micro, nf, tokens // nf, width).transpose(1, 0, 2, 3)
    return jnp.stack([pick(parts, f)] + [xor_plane(pick(parts, f ^ k), k) for k in range(1, nf)])


def rows_to_layer(got):
    nz = lax.axis_size("z")
    f, z = lax.axis_index(("p", "q")), lax.axis_index("z")
    return [pick(got, f ^ z)] + [xor_permute(pick(got, f ^ z ^ k), "z", k) for k in range(1, nz)]


def rows_from_layer(y):
    nz = lax.axis_size("z")
    micro, rows, width = y.shape
    rp = rows // nz
    return [y[:, :rp]] + [xor_permute(y[:, k * rp:(k + 1) * rp], "z", k) for k in range(1, nz)]


def rows_from_plane(got):
    nf = lax.axis_size("p") * lax.axis_size("q")
    f, z = lax.axis_index(("p", "q")), lax.axis_index("z")
    got = jnp.stack(got)
    back = [pick(got, z ^ f)] + [xor_plane(pick(got, z ^ f ^ k), k) for k in range(1, nf)]
    back = jnp.stack(back)
    return jnp.concatenate([pick(back, f ^ c) for c in range(nf)], axis=1)


def gather_first(x):
    np_ = lax.axis_size("p")
    return [x, xor_permute(x, "q", 1)] + [xor_permute(x, "p", k) for k in range(1, np_)]


def gather_own_core(first):
    np_ = lax.axis_size("p")
    x, over_q = first[:2]
    half = x.shape[0] // 2
    if np_ == 2:
        over_p = first[2]
        own = [x, over_q, over_p, [xor_permute(over_q[:half], "p", 1), xor_permute(over_p[half:], "q", 1)]]
    else:
        own = [x, over_q]
        for k in range(1, np_):
            own += [first[1 + k], xor_permute(over_q, "p", k)]
    return own


def gather_both_cores(own):
    return own + jax.tree.map(lambda block: xor_permute(block, "core", 1), own)


def gather_rest(first):
    return gather_both_cores(gather_own_core(first))


def gather_plane(x):
    return gather_rest(gather_first(x))


def in_rows(blocks):
    return jnp.concatenate(jax.tree.leaves(blocks), axis=0)


def add_up(*parts):
    return sum(part.astype(F32) for part in parts)


def term(items, number=None):
    operands = []
    for item in items:
        if number is None:
            operands.append((item, pl.BlockSpec(item.shape, lambda i: (0, 0))))
        else:
            operands.append((item, pl.BlockSpec((None,) + item.shape[1:], lambda i: (number, 0, 0))))
    return operands


def read_term(refs):
    parts = [ref[...].astype(F32) for ref in refs]
    return parts[0] if len(parts) == 1 else jnp.concatenate(parts, axis=0)


def rows_kernel(body, terms, outs, name):
    counts = [len(item) for item in terms]
    operands = [pair for item in terms for pair in item]

    def kernel(*refs):
        values, at = [], 0
        for count in counts:
            values.append(read_term(refs[at:at + count]))
            at += count
        for ref, value in zip(refs[at:], body(*values)):
            ref[...] = value.astype(ref.dtype)

    return pl.pallas_call(
        kernel,
        grid=(1,),
        in_specs=[spec for _, spec in operands],
        out_specs=[pl.BlockSpec(shape, lambda i: (0, 0)) for shape, _ in outs],
        out_shape=[jax.ShapeDtypeStruct(shape, kind) for shape, kind in outs],
        compiler_params=pltpu.CompilerParams(vmem_limit_bytes=VMEM_LIMIT),
        name=name,
    )(*[array for array, _ in operands])


def scatter_core(far, near):
    got = [xor_permute(item, "core", 1) for item in far]
    last = 2 * lax.axis_size("p") - 1
    rows, width = sum(item.shape[1] for item in near), near[0].shape[2]
    half = rows // 2

    def body(one, other):
        total = one + other
        return total[:half], total[half:]

    return near, got, rows_kernel(body, [term(near, last), term(got, last)], [((half, width), BF16)] * 2, "sum_last")


def both_cores(near, got, number):
    return jnp.concatenate([add_up(one[number], other[number]) for one, other in zip(near, got)], axis=0)


def scatter_diagonal(near, got, last, beside=None):
    np_ = lax.axis_size("p")
    near, got, last = lax.optimization_barrier((near, got, last))
    made = ()
    if np_ == 2:
        into_q = xor_permute(last[0], "p", 1)
        into_p = xor_permute(last[1], "q", 1)
        if beside is not None:
            into_q, into_p, made = lax.optimization_barrier((into_q, into_p, beside(last)))
        half, width = last[0].shape

        def body(near_q, got_q, near_p, got_p, into_q, into_p):
            to_q, to_p = near_q + got_q, near_p + got_p
            to_q = jnp.concatenate([to_q[:half] + into_q, to_q[half:]], axis=0)
            return to_q, jnp.concatenate([to_p[:half], to_p[half:] + into_p], axis=0)

        to_q, to_p = rows_kernel(
            body, [term(near, 1), term(got, 1), term(near, 2), term(got, 2), term([into_q]), term([into_p])],
            [((2 * half, width), BF16)] * 2, "sum_next",
        )
        return [(near, 0), (got, 0)], [(to_q, "q"), (to_p, "p")], made
    if beside is not None:
        made = beside(last)
    last = jnp.concatenate(last, axis=0)
    pair = [both_cores(near, got, 0), both_cores(near, got, 1)]
    for k in range(1, np_):
        for side in range(2):
            item = last if 2 * k + side == 2 * np_ - 1 else both_cores(near, got, 2 * k + side).astype(BF16)
            pair[side] = pair[side] + xor_permute(item, "p", k).astype(F32)
    return [([pair[0]], None)], [(pair[1].astype(BF16), "q")], made


def scatter_first(far, near, beside=None):
    return scatter_diagonal(*scatter_core(far, near), beside)


def sent(state):
    return [item for item, _ in state[1]]


def received(state, sends):
    return [xor_permute(item, axis, 1) for item, (_, axis) in zip(sends, state[1])]


def sum_terms(parts, arrived):
    return [term(*part) for part in parts] + [term([item]) for item in arrived]


def normed_rows(x):
    return x * lax.rsqrt(jnp.mean(x * x, axis=-1, keepdims=True) + EPS)


def add_and_norm(parts, arrived, own, gain):
    terms = sum_terms(parts, arrived)

    def body(own, gain, *values):
        total = own + sum(values)
        return total, normed_rows(total) * gain

    return rows_kernel(body, [term([own]), term([gain])] + terms, [(own.shape, F32), (own.shape, BF16)], "add_norm")


def norm_back(parts, arrived, above, x, gain, kinds):
    terms = sum_terms(parts, arrived)

    def body(above, x, gain, *values):
        r = lax.rsqrt(jnp.mean(x * x, axis=-1, keepdims=True) + EPS)
        unit, scaled = x * r, sum(values) * gain
        total = above + r * (scaled - unit * jnp.mean(scaled * unit, axis=-1, keepdims=True))
        return [total] * len(kinds)

    return rows_kernel(
        body, [term([above]), term([x]), term([gain])] + terms, [(x.shape, kind) for kind in kinds], "norm_back"
    )


def add_rows(parts, arrived, own):
    return rows_kernel(
        lambda *values: [sum(values)], [term([own])] + sum_terms(parts, arrived), [(own.shape, BF16)], "add_rows"
    )[0]


def total_over(axis, x, step=1):
    while step < lax.axis_size(axis):
        x = x + xor_permute(x, axis, step)
        step *= 2
    return x


def log_sigmoid(z):
    return jnp.minimum(z, 0.0) - jnp.log(1.0 + jnp.exp(-jnp.abs(z)))


def window_of(i, bq, window):
    first = max(0, i * bq - window)
    return first, (i + 1) * bq - first


def pieces(members, rows, chunk):
    per = rows // chunk
    return [(j * per + k, j, k * chunk) for j in range(members) for k in range(per)]


def natural_rows(table, number, chunk):
    return pl.ds(pl.multiple_of(table[number] * chunk, chunk), chunk)


def spread_rows(table, source, far_ref, near_ref, chunk):
    half = near_ref.shape[0]
    for number, j, at in pieces(2 * half, near_ref.shape[1], chunk):
        target = near_ref if j < half else far_ref
        target[j % half, at:at + chunk, :] = source[natural_rows(table, number, chunk), :]


def attend_kernel(heads, depth, chunk, members, table, *refs):
    x_refs, refs = refs[:members], refs[members:]
    w_ref, bias_ref, begin_ref = refs[:3]
    h_ref, qkv_ref, g_ref, z_ref, a_ref, total_ref, cumul_ref, b_ref, gain_ref = refs[-13:-4]
    ka, va, rows, part = refs[-4:]
    total = total_ref.shape[0]
    columns = heads * depth
    bq = min(BQ, total)
    window = total // 2
    scale = jnp.asarray(depth ** -0.5, BF16)
    for number, j, at in pieces(members, x_refs[0].shape[0], chunk):
        part[natural_rows(table, number, chunk), :] = x_refs[j][at:at + chunk, :]
    gains = jnp.transpose(w_ref[:, 0:128].astype(F32))[2 * heads:2 * heads + 2, :]
    gain_ref[...] = jnp.concatenate([gains, jnp.zeros((6, gains.shape[1]), F32)], axis=0)
    gain = gains[0:1, :]
    lower = (
        lax.broadcasted_iota(jnp.int32, (bq, bq), 0) >= lax.broadcasted_iota(jnp.int32, (bq, bq), 1)
    ).astype(F32).astype(BF16)
    carry = jnp.zeros((1, 128), F32)
    for i in range(total // bq):
        here = slice(i * bq, (i + 1) * bq)
        values = part[here, :].astype(F32)
        values = values * lax.rsqrt(jnp.mean(values * values, axis=1, keepdims=True) + EPS) * gain
        h_ref[here, :] = values.astype(BF16)
        tile = dot(h_ref[here, :], w_ref[...])
        logit = tile[:, 0:128] + bias_ref[...]
        z_ref[here, :] = logit
        cumul = dot(lower, log_sigmoid(logit).astype(BF16)) + carry
        cumul_ref[here, :] = cumul
        carry = cumul[bq - 1:bq, :]
        qkv_ref[here, :] = tile[:, 128:128 + 3 * columns].astype(BF16)
        g_ref[here, :] = tile[:, 128 + 3 * columns:]
        for h in range(heads):
            lo = 128 + columns + h * depth
            ka[h, here, :] = tile[:, lo:lo + depth].astype(BF16)
            lo += columns
            va[h, here, 0:depth] = tile[:, lo:lo + depth].astype(BF16)
            va[h, here, depth:] = jnp.ones((bq, 128 - depth), BF16)
    rows[...] = jnp.transpose(cumul_ref[...])
    lane = lax.broadcasted_iota(jnp.int32, (bq, 128), 1)
    for i in range(total // bq):
        first, span = window_of(i, bq, window)
        here = slice(i * bq, (i + 1) * bq)
        place = i * bq + lax.broadcasted_iota(jnp.int32, (bq, span), 0)
        other = first + lax.broadcasted_iota(jnp.int32, (bq, span), 1)
        mask = jnp.where((other <= place) & (other >= begin_ref[here, :]), 0.0, LOW)
        totals = jnp.zeros((bq, 128), F32)
        for h in range(heads):
            query = qkv_ref[here, h * depth:(h + 1) * depth] * scale
            score = dot(query, ka[h, first:first + span, :], ((1,), (1,)))
            score = score - rows[h:h + 1, first:first + span] + mask
            peak = jnp.max(score, axis=1, keepdims=True)
            weight = jnp.exp(score - peak)
            both = dot(weight.astype(BF16), va[h, first:first + span, :])
            a_ref[here, h * depth:(h + 1) * depth] = both[:, 0:depth] / both[:, depth:2 * depth]
            totals = jnp.where(lane == h, peak + jnp.log(both[:, depth:depth + 1]), totals)
        total_ref[here, :] = totals
        part[here, 0:columns] = (a_ref[here, :] * jax.nn.sigmoid(g_ref[here, :])).astype(BF16)
    for number, j, at in pieces(members, b_ref.shape[1], chunk):
        b_ref[j, at:at + chunk, :] = part[natural_rows(table, number, chunk), 0:columns]


def attend_back_kernel(heads, depth, chunk, members, streams, held, table, *refs):
    x_refs, refs = refs[:members], refs[members:]
    extra = members * max(0, streams - 1)
    other_refs, gated_refs, refs = refs[:extra], refs[extra:extra + streams], refs[extra + streams:]
    w_ref, o_ref, qkv_ref, g_ref, z_ref, a_ref, total_ref, cumul_ref, begin_ref = refs[:9]
    refs = refs[held:]
    right_ref, far_ref, near_ref, dbias_ref = refs[9:13]
    part, below_grad, qa, ka, va, da, dkn, dvn, rows, deltas, dcumul = refs[-11:]
    if streams:
        out_grad = jnp.zeros(refs[13].shape, F32)
        for number, ref in enumerate(x_refs + other_refs):
            out_grad = out_grad + dot(gated_refs[number // members][number % members], ref[...], ((0,), (0,)))
        refs[13][...] = out_grad.astype(BF16)
    total = total_ref.shape[0]
    columns = heads * depth
    bq = min(BQ, total)
    window = total // 2
    scale = jnp.asarray(depth ** -0.5, BF16)
    lane = lax.broadcasted_iota(jnp.int32, (bq, 128), 1)
    per = x_refs[0].shape[0] // chunk
    for j in range(members):
        grad = dot(x_refs[j][...], o_ref[...], ((1,), (1,)))
        for k in range(per):
            below_grad[natural_rows(table, j * per + k, chunk), :] = grad[k * chunk:(k + 1) * chunk, :]
    dkn[...] = jnp.zeros_like(dkn)
    dvn[...] = jnp.zeros_like(dvn)
    for i in range(total // bq):
        here = slice(i * bq, (i + 1) * bq)
        grad = below_grad[here, :]
        opened = jax.nn.sigmoid(g_ref[here, :])
        attended = a_ref[here, :]
        below = (grad * opened).astype(BF16)
        right_ref[here, 128 + 3 * columns:] = (grad * attended * opened * (1.0 - opened)).astype(BF16)
        product = below.astype(F32) * attended
        delta = jnp.zeros((bq, 128), F32)
        for h in range(heads):
            da[h, here, :] = below[:, h * depth:(h + 1) * depth]
            delta = jnp.where(
                lane == h, jnp.sum(product[:, h * depth:(h + 1) * depth], axis=1, keepdims=True), delta
            )
            qa[h, here, 0:depth] = qkv_ref[here, h * depth:(h + 1) * depth] * scale
            qa[h, here, depth:] = jnp.ones((bq, 128 - depth), BF16)
            lo = columns + h * depth
            ka[h, here, 0:depth] = qkv_ref[here, lo:lo + depth]
            ka[h, here, depth:] = jnp.ones((bq, 128 - depth), BF16)
            lo += columns
            va[h, here, :] = qkv_ref[here, lo:lo + depth]
        dcumul[here, :] = delta
    deltas[...] = jnp.transpose(dcumul[...])
    rows[...] = jnp.transpose(total_ref[...])
    dcumul[...] = jnp.zeros_like(dcumul)
    for i in range(total // bq):
        first, span = window_of(i, bq, window)
        here, there = slice(i * bq, (i + 1) * bq), slice(first, first + span)
        place = i * bq + lax.broadcasted_iota(jnp.int32, (span, bq), 1)
        other = first + lax.broadcasted_iota(jnp.int32, (span, bq), 0)
        mask = jnp.where((other <= place) & (other >= begin_ref[:, here]), 0.0, LOW)
        for h in range(heads):
            query, below = qa[h, here, :], da[h, here, :]
            score = dot(ka[h, there, 0:depth], query[:, 0:depth], ((1,), (1,)))
            score = score - rows[h:h + 1, here] - cumul_ref[there, h:h + 1] + mask
            weight = jnp.exp(score)
            weight_grad = dot(va[h, there, :], below, ((1,), (1,))) - deltas[h:h + 1, here]
            score_grad = (weight * weight_grad).astype(BF16)
            dvn[h, there, :] += dot(weight.astype(BF16), below)
            dkn[h, there, :] += dot(score_grad, query)
            dq = dot(score_grad, ka[h, there, :], ((0,), (0,)))
            right_ref[here, 128 + h * depth:128 + (h + 1) * depth] = (dq[:, 0:depth] * depth ** -0.5).astype(BF16)
            mine = (lane == h) | (lane == h + heads)
            dcumul[here, :] += jnp.where(mine, dq[:, depth:depth + 1], 0.0)
    upper = (
        lax.broadcasted_iota(jnp.int32, (bq, bq), 0) <= lax.broadcasted_iota(jnp.int32, (bq, bq), 1)
    ).astype(F32)
    carry = jnp.zeros((1, 128), F32)
    sums = jnp.zeros((1, 128), F32)
    for i in reversed(range(total // bq)):
        here = slice(i * bq, (i + 1) * bq)
        change = dcumul[here, :]
        for h in range(heads):
            lo = 128 + columns + h * depth
            right_ref[here, lo:lo + depth] = dkn[h, here, 0:depth].astype(BF16)
            lo += columns
            right_ref[here, lo:lo + depth] = dvn[h, here, :].astype(BF16)
            mine = (lane == h) | (lane == h + heads)
            change = change - jnp.where(mine, dkn[h, here, depth:depth + 1], 0.0)
        summed = carry + jnp.dot(upper, change, precision=lax.Precision.HIGHEST, preferred_element_type=F32)
        carry = summed[0:1, :]
        grad = summed * jax.nn.sigmoid(-z_ref[here, :])
        sums = sums + jnp.sum(grad, axis=0, keepdims=True)
        high = grad.astype(BF16).astype(F32)
        pair = jnp.where(lane < heads, high, jnp.where(lane < 2 * heads, grad - high, 0.0))
        right_ref[here, 0:128] = pair.astype(BF16)
        part[here, :] = dot(right_ref[here, :], w_ref[...], ((1,), (1,))).astype(BF16)
    dbias_ref[...] = jnp.broadcast_to(sums, dbias_ref.shape)
    spread_rows(table, part, far_ref, near_ref, chunk)


def one_stream(blocks, m, streams):
    arrays, specs = [], []
    for block in blocks:
        array, place = (block[m], 0) if isinstance(block, list) else (block, m)
        rows, width = (array.shape[0] if isinstance(block, list) else array.shape[0] // streams), array.shape[1]
        arrays.append(array)
        specs.append(pl.BlockSpec((rows, width), lambda i, t, place=place: (place, 0), pipeline_mode=pl.Buffered(1)))
    return arrays, specs


def fixed(array):
    return pl.BlockSpec(array.shape, lambda i, t: (0,) * array.ndim, pipeline_mode=pl.Buffered(1))


def own_part(shape, m):
    return pl.BlockSpec(shape, lambda i, t: (m, 0), pipeline_mode=pl.Buffered(1))


def attend(table, blocks, m, streams, weights, bias, begin, into, heads, depth, chunk):
    arrays, specs = one_stream(blocks, m, streams)
    members, (rows, width) = len(arrays), specs[0].block_shape
    total = begin.shape[0]
    columns = heads * depth
    begin = begin[:, None]
    into = [] if into is None else [into]
    outs = [
        ((streams * total, width), BF16), ((total, 3 * columns), BF16), ((total, columns), F32), ((total, 128), F32),
        ((total, columns), F32), ((total, 128), F32), ((total, 128), F32), ((members, rows, columns), BF16),
        ((8, width), F32),
    ]
    out_shape = [jax.ShapeDtypeStruct(shape, kind) for shape, kind in outs]
    return pl.pallas_call(
        functools.partial(attend_kernel, heads, depth, chunk, members),
        grid_spec=pltpu.PrefetchScalarGridSpec(
            num_scalar_prefetch=1,
            grid=(1,),
            in_specs=specs + [fixed(weights), fixed(bias), fixed(begin)] + [pl.BlockSpec(memory_space=pl.ANY)] * len(into),
            out_specs=[own_part((total, width), m)] + [fixed(item) for item in out_shape[1:]],
            scratch_shapes=[
                pltpu.VMEM((heads, total, depth), BF16),
                pltpu.VMEM((heads, total, 128), BF16),
                pltpu.VMEM((128, total), F32),
                pltpu.VMEM((total, width), BF16),
            ],
        ),
        out_shape=out_shape,
        compiler_params=pltpu.CompilerParams(vmem_limit_bytes=VMEM_LIMIT),
        input_output_aliases={1 + members + 3: 0} if into else {},
        cost_estimate=pl.CostEstimate(flops=14 * 10 ** 9, bytes_accessed=10 ** 7, transcendentals=0),
        name="attend",
    )(table, *arrays, weights, bias, begin, *into)


def attend_back(table, blocks, m, streams, weights, out_w, kept, begin, gated, into, heads, depth, chunk):
    arrays, specs = one_stream(blocks, m, streams)
    members, (rows, width) = len(arrays), specs[0].block_shape
    total = begin.shape[0]
    columns = heads * depth
    begin = begin[None, :]
    gated = [] if gated is None else gated
    into = [] if into is None else [into]
    for other in range(1, len(gated)):
        other_arrays, other_specs = one_stream(blocks, other, streams)
        arrays, specs = arrays + other_arrays, specs + other_specs
    outs = [
        ((streams * total, 128 + 4 * columns), BF16), ((members // 2, rows, width), BF16), ((members // 2, rows, width), BF16),
        ((8, 128), F32),
    ] + [((columns, width), BF16)] * (len(gated) > 0)
    out_shape = [jax.ShapeDtypeStruct(shape, kind) for shape, kind in outs]
    return pl.pallas_call(
        functools.partial(attend_back_kernel, heads, depth, chunk, members, len(gated), len(into)),
        grid_spec=pltpu.PrefetchScalarGridSpec(
            num_scalar_prefetch=1,
            grid=(1,),
            in_specs=specs + [fixed(item) for item in (*gated, weights, out_w, *kept, begin)]
            + [pl.BlockSpec(memory_space=pl.ANY)] * len(into),
            out_specs=[own_part((total, 128 + 4 * columns), m)] + [fixed(item) for item in out_shape[1:]],
            scratch_shapes=[
                pltpu.VMEM((total, width), BF16),
                pltpu.VMEM((total, columns), F32),
                pltpu.VMEM((heads, total, 128), BF16),
                pltpu.VMEM((heads, total, 128), BF16),
                pltpu.VMEM((heads, total, depth), BF16),
                pltpu.VMEM((heads, total, depth), BF16),
                pltpu.VMEM((heads, total, 128), F32),
                pltpu.VMEM((heads, total, depth), F32),
                pltpu.VMEM((128, total), F32),
                pltpu.VMEM((128, total), F32),
                pltpu.VMEM((total, 128), F32),
            ],
        ),
        out_shape=out_shape,
        compiler_params=pltpu.CompilerParams(vmem_limit_bytes=VMEM_LIMIT),
        input_output_aliases={1 + len(arrays) + len(gated) + 3 + len(kept): 0} if into else {},
        cost_estimate=pl.CostEstimate(flops=20 * 10 ** 9, bytes_accessed=10 ** 7, transcendentals=0),
        name="attend_back",
    )(table, *arrays, *gated, weights, out_w, *kept, begin, *into)


def out_kernel(b_ref, o_ref, far_ref, near_ref):
    half = near_ref.shape[0]
    for j in range(2 * half):
        target = near_ref if j < half else far_ref
        target[j % half] = dot(b_ref[j], o_ref[...]).astype(BF16)


def out_product(gated, weights):
    members, rows, _ = gated.shape
    shape = jax.ShapeDtypeStruct((members // 2, rows, weights.shape[1]), BF16)
    return pl.pallas_call(
        out_kernel,
        out_shape=[shape, shape],
        compiler_params=pltpu.CompilerParams(vmem_limit_bytes=VMEM_LIMIT),
        name="out_product",
    )(gated, weights)


def ffn_kernel(h_ref, e_ref, w_ref, d_ref, *refs):
    m_ref, g_ref, part_ref = refs[-3:]
    down = d_ref[...].reshape(-1, d_ref.shape[-1])
    share = down.shape[0]
    pre = dot(h_ref[...], w_ref[...])
    gate, up = pre[:, :share], pre[:, share:]
    grad = dot(e_ref[...], down, ((1,), (1,)))
    opened = jax.nn.sigmoid(gate)
    silu = gate * opened
    m_ref[...] = (silu * up).astype(BF16)
    g_ref[:, :share] = (grad * up * (opened * (1.0 + gate * (1.0 - opened)))).astype(BF16)
    g_ref[:, share:] = (grad * silu).astype(BF16)
    part_ref[...] = dot(g_ref[...], w_ref[...], ((1,), (1,))).astype(BF16)


def ffn(normed, upstream, weights, down, unit, first, count, into):
    rows, width = normed.shape
    share = down.shape[0] * unit

    def blocks(lanes, shift):
        return pl.BlockSpec((BQ, lanes), lambda i: (i + shift, 0))

    def fixed(shape):
        return pl.BlockSpec(shape, lambda i: (0,) * len(shape), pipeline_mode=pl.Buffered(1))

    kept = [] if into is None else list(into)
    return pl.pallas_call(
        ffn_kernel,
        grid=(count,),
        in_specs=[blocks(width, first), blocks(width, first), fixed(weights.shape), fixed((down.shape[0], unit, width))]
        + [pl.BlockSpec(memory_space=pl.ANY)] * len(kept),
        out_specs=[
            blocks(share, first), blocks(2 * share, first), pl.BlockSpec((None, BQ, width), lambda i: (i, 0, 0)),
        ],
        out_shape=[
            jax.ShapeDtypeStruct((rows, share), BF16),
            jax.ShapeDtypeStruct((rows, 2 * share), BF16),
            jax.ShapeDtypeStruct((count, BQ, width), BF16),
        ],
        input_output_aliases={4 + i: i for i in range(len(kept))},
        compiler_params=pltpu.CompilerParams(vmem_limit_bytes=VMEM_LIMIT),
        cost_estimate=pl.CostEstimate(
            flops=10 * count * BQ * width * share, bytes_accessed=count * BQ * width * 8, transcendentals=0
        ),
        name="ffn",
    )(normed, upstream, weights, down, *kept)


def layout(body, shapes, kind, *arrays):
    kinds = kind if isinstance(kind, list) else [kind] * len(shapes)
    out_shape = [jax.ShapeDtypeStruct(shape, own) for shape, own in zip(shapes, kinds)]
    return pl.pallas_call(body, out_shape=out_shape, name="layout")(*arrays)


def block_columns(block, columns, limit):
    return min(block * columns, limit), max(0, min((block + 1) * columns, limit) - min(block * columns, limit))


def pack_heads(forget, weights, nf, columns):
    slab, width = weights[0].shape
    plane = 2 * nf

    def body(f_ref, *refs):
        out = refs[-1]
        for t in range(plane):
            out[t, :, 0:128] = f_ref[:, t * 128:(t + 1) * 128]
            first, count = block_columns(t % nf * 2 + t // nf, columns, width)
            for number, ref in enumerate(refs[:-1]):
                lo = 128 + number * columns
                if count < columns:
                    out[t, :, lo:lo + columns] = jnp.zeros((slab, columns), BF16)
                if count:
                    out[t, :, lo:lo + count] = ref[:, first:first + count]

    return layout(body, [(plane, slab, 128 + 4 * columns)], BF16, forget, *weights)[0]


def unpack_heads(grads, weights, nf, columns):
    plane, slab, _ = grads.shape
    width = weights[0].shape[1]

    def body(x_ref, *refs):
        sums = jnp.zeros((slab, 1), F32)
        for number in range(4):
            weight, out = refs[number], refs[4 + number]
            for t in range(plane):
                first, count = block_columns(t % nf * 2 + t // nf, columns, width)
                lo = 128 + number * columns
                if count:
                    out[:, first:first + count] = x_ref[t, :, lo:lo + count].astype(F32)
            sums = sums + jnp.sum(weight[...].astype(F32) * out[...], axis=1, keepdims=True)
        refs[8][...] = sums

    return layout(body, [(slab, width)] * 4 + [(slab, 1)], F32, grads, *weights)


def pack_hidden(gate, up, nz, plane):
    slab, hidden = gate.shape
    unit = hidden // (nz * plane)

    def body(gate_ref, up_ref, out):
        for number, ref in enumerate((gate_ref, up_ref)):
            for t in range(plane):
                for z in range(nz):
                    lo = (number * nz + z) * unit
                    at = (z * plane + t) * unit
                    out[t, :, lo:lo + unit] = ref[:, at:at + unit]

    return layout(body, [(plane, slab, 2 * nz * unit)], BF16, gate, up)[0]


def unpack_hidden(grads, weights, nz):
    plane, slab, both = grads.shape
    unit = both // (2 * nz)

    def body(x_ref, *refs):
        sums = jnp.zeros((slab, 1), F32)
        for number in range(2):
            weight, out = refs[number], refs[2 + number]
            for t in range(plane):
                for z in range(nz):
                    lo = (number * nz + z) * unit
                    at = (z * plane + t) * unit
                    out[:, at:at + unit] = x_ref[t, :, lo:lo + unit].astype(F32)
            sums = sums + jnp.sum(weight[...].astype(F32) * out[...], axis=1, keepdims=True)
        refs[4][...] = sums

    return layout(body, [(slab, plane * nz * unit)] * 2 + [(slab, 1)], F32, grads, *weights)


def doc_begins(lengths_row, total):
    ends = jnp.cumsum(lengths_row)
    begins = ends - lengths_row
    place = jnp.arange(total, dtype=jnp.int32)
    inside = (place[:, None] >= begins[None, :]) & (place[:, None] < ends[None, :])
    return jnp.sum(jnp.where(inside, begins[None, :], 0), axis=1)


def all_to_all(x, axes):
    return lax.all_to_all(x, axes, split_axis=0, concat_axis=0, tiled=True)


def scatter_layers(grad):
    return lax.psum_scatter(grad, "z", scatter_dimension=0, tiled=True)


def join_grads(grad, down, nz):
    lanes, width = grad.shape[1], down.shape[1]
    grad, down = grad.reshape(nz, -1, lanes), down.reshape(nz, -1, width)
    parts = [grad] + [down[:, :, i * lanes:(i + 1) * lanes] for i in range(width // lanes)]
    rest = width % lanes
    if rest:
        count = lanes // rest
        rows = down.shape[1] // count
        over = down[:, :, width - rest:].reshape(nz, count, rows, rest)
        parts.append(jnp.concatenate([over[:, i] for i in range(count)], axis=2))
    return jnp.concatenate(parts, axis=1).reshape(-1, lanes)


def part_grads(joined, slabs, rows, width):
    lanes = joined.shape[1]
    grad, joined = joined[:slabs], joined[slabs:]
    whole = width // lanes
    parts = [joined[i * rows:(i + 1) * rows] for i in range(whole)]
    rest = width % lanes
    if rest:
        over = joined[whole * rows:]
        parts.append(jnp.concatenate([over[:, i * rest:(i + 1) * rest] for i in range(lanes // rest)], axis=0))
    return grad, jnp.concatenate(parts, axis=1)


def tie(*values):
    return lax.optimization_barrier(values)


def per_device(
    inputs, cotangent, lengths, deal, norm1_gain, w_query, w_key, w_value, w_outgate, w_out,
    forget_weight, forget_bias, norm2_gain, w_gate, w_up, w_down,
):
    nz, np_, nq = lax.axis_size("z"), lax.axis_size("p"), lax.axis_size("q")
    z, core, f = lax.axis_index("z"), lax.axis_index("core"), lax.axis_index(("p", "q"))
    nf = np_ * nq
    n_ctx = 2 * nz
    plane = 2 * nf
    devices = nz * plane
    everywhere, members = ("z", "core", "p", "q"), ("core", "p", "q")
    micro, _, tokens, width = inputs.shape
    heads = forget_bias.shape[0]
    depth = width // heads
    own_heads = -(-heads // plane)
    columns = own_heads * depth
    spare_heads = own_heads * plane - heads
    total = tokens * n_ctx
    chunk = tokens // nf
    block = tokens // 2
    hidden = w_gate.shape[1]
    slab = w_query.shape[0]
    unit = hidden // devices
    share = nz * unit
    own_block = f * 2 + core
    aligned = spare_heads == 0 and columns == nf * slab

    member_block = [t % nf * 2 + t // nf for t in range(plane)]
    head_of = jnp.arange(heads, dtype=jnp.int32)[:, None]
    lane_of = jnp.arange(plane * 128, dtype=jnp.int32)[None, :]
    lane_head = jnp.asarray(member_block, jnp.int32)[lane_of // 128] * own_heads + lane_of % 128 % own_heads
    select = ((lane_head == head_of) & (lane_of % 128 < 2 * own_heads)).astype(BF16)
    first_lanes = dot(forget_weight, select, out=BF16)
    for number, gain in enumerate((norm1_gain, norm2_gain)):
        first_lanes = jnp.where(lane_of % 128 == 2 * own_heads + number, gain[:, None], first_lanes)
    packed = pack_heads(first_lanes, (w_query, w_key, w_value, w_outgate), nf, columns)
    own = rows_to_layer(rows_to_plane(inputs[:, 0]))
    packed, own[1] = tie(packed, own[1])
    packed = all_to_all(packed, members)
    if aligned:
        out_w = jnp.stack([w_out] + [xor_permute(w_out, "z", k) for k in range(1, nz)])
        out_w = jnp.stack([pick(out_w, z ^ c) for c in range(nz)])
    else:
        out_w = jnp.pad(lax.all_gather(w_out, everywhere, axis=0, tiled=True), ((0, spare_heads * depth), (0, 0)))
        out_w = lax.dynamic_slice_in_dim(out_w, own_block * columns, columns, 0)
    own = jnp.concatenate(own, axis=1).reshape(-1, width)
    packed, own, out_w = tie(packed, own, out_w)
    packed = lax.all_gather(packed, "z", axis=0).reshape(width, -1)
    gathered = gather_first(own)
    ffn_send, gathered = tie(pack_hidden(w_gate, w_up, nz, plane), gathered)
    gathered = gather_rest(gathered)
    if aligned:
        out_w = all_to_all(out_w, ("p", "q")).reshape(columns, width)
    ffn_w = all_to_all(ffn_send, members)
    out_w, ffn_w, gathered, cotangent = tie(out_w, ffn_w, gathered, cotangent)
    upstream_own = rows_to_plane(cotangent[:, 0])
    packed, upstream_own = tie(packed, upstream_own)
    upstream_own = jnp.concatenate(rows_to_layer(upstream_own), axis=1).reshape(-1, width)

    lengths_own = lax.ppermute(
        lengths[:, 0], everywhere,
        [
            (((f_to * 2 + c) * nf) + z_to, ((z_to * 2 + c) * nf) + f_to)
            for z_to in range(nz) for c in range(2) for f_to in range(nf)
        ],
    )
    begins = [doc_begins(lengths_own[m], total) for m in range(micro)]
    number = jnp.arange(total // chunk, dtype=jnp.int32)
    from_core = core ^ (number // (nf * nz))
    from_f = f ^ (number // nz % nf)
    from_z = z ^ (number % nz)
    inside = from_f * chunk

    def natural_table(deal_row):
        dealt = jnp.take(deal_row, from_z * 2 + from_core)
        start = jnp.where(inside < block, dealt, 2 * n_ctx - 1 - dealt) * block + inside % block
        return (start // chunk).astype(jnp.int32)

    tables = [natural_table(deal[m]) for m in range(micro)]
    all_bias = jnp.pad(forget_bias, (0, spare_heads))
    own_bias = lax.dynamic_slice_in_dim(all_bias, own_block * own_heads, own_heads, 0)[None]
    bias_row = jnp.concatenate([own_bias, own_bias, jnp.zeros((1, 128 - 2 * own_heads), F32)], axis=1)

    def attend_stream(m, table, into):
        return attend(table, gathered, m, micro, packed, bias_row, begins[m], into, own_heads, depth, chunk)

    attended = [attend_stream(0, tables[0], None)]
    gains = attended[0][8]
    gated = [attended[0][7]]
    parts = [out_product(gated[0], out_w)]
    table, upstream_own, gains, ffn_w, w_down = tie(tables[1], upstream_own, gains, ffn_w, w_down)
    ffn_w = lax.all_gather(ffn_w, "z", axis=0).reshape(width, 2 * share)
    down_w = lax.all_gather(w_down, "z", axis=0)
    attended.append(attend_stream(1, table, attended[0][0]))
    upstream = gather_first(upstream_own)
    last_gated, upstream = tie(attended[1][7], upstream)
    gated.append(last_gated)
    upstream, last_part = tie(gather_own_core(upstream), out_product(gated[1], out_w))
    parts.append(last_part)
    upstream = in_rows(gather_both_cores(upstream))
    gain_one, gain_two = gains[0:1], gains[1:2]
    state = scatter_first([item[0] for item in parts], [item[1] for item in parts])
    middle, normed_two = add_and_norm(state[0], received(state, sent(state)), own, gain_two)
    normed_two = in_rows(gather_plane(normed_two))

    half_blocks = normed_two.shape[0] // BQ // 2
    weights = (normed_two, upstream, ffn_w, down_w, unit)
    activ, ffn_grad, far = ffn(*weights, half_blocks, half_blocks, None)
    activ, ffn_grad, near = ffn(*weights, 0, half_blocks, (activ, ffn_grad))
    def grad_of_ffn(hold):
        kept, _ = tie(normed_two, hold)
        return dot(kept, ffn_grad, ((0,), (0,)), BF16)

    state = scatter_first([far], [near], grad_of_ffn)
    grad_ffn_w = state[2]
    sends, held = tie(sent(state), activ)
    grad_down = dot(held, upstream, ((0,), (0,)), BF16)
    arrived, grad_ffn = tie(received(state, sends), join_grads(grad_ffn_w, grad_down, nz))
    grad_ffn = scatter_layers(grad_ffn)
    middle_grad, branch_own = norm_back(state[0], arrived, upstream_own, middle, gain_two, (F32, BF16))
    branch_own, held = tie(branch_own, activ)
    half = activ.shape[0] // 2
    down_rows = down_w.reshape(share, width)
    part_out = [
        dot(item, down_rows, out=BF16).reshape(plane // 2, -1, width) for item in (held[half:], held[:half])
    ]
    branch_grad, part_out = tie(gather_first(branch_own), part_out)
    result = scatter_core(part_out[:1], part_out[1:])
    branch_grad = gather_rest(branch_grad)

    def back_stream(m, table, gated, into):
        return attend_back(
            table, branch_grad, m, micro, packed, out_w, attended[m][1:7], begins[m], gated, into, own_heads, depth, chunk
        )

    def first_back(hold):
        table, _ = tie(tables[0], hold)
        return back_stream(0, table, gated, None)

    result = scatter_diagonal(*result, first_back)
    backs = [result[2]]
    sends, table = tie(sent(result), tables[1])
    grad_out = backs[0][4]
    if aligned:
        grad_out = all_to_all(grad_out.reshape(nf, slab, width), ("p", "q"))
    arrived, grad_out, last_back = tie(received(result, sends), grad_out, back_stream(1, table, None, backs[0][0]))
    backs.append(last_back)
    grad_packed = dot(attended[1][0], backs[1][0], ((0,), (0,)), BF16)
    bias_sum = sum(item[3][0] for item in backs)
    bias_all = lax.dynamic_update_slice_in_dim(
        jnp.zeros((own_heads * plane,), F32), bias_sum[:own_heads], own_block * own_heads, 0
    )[:heads]

    def rows_of_output(hold):
        own_arrived, own_bias, _ = tie(arrived, bias_all, hold)
        rows = add_rows(result[0], own_arrived, middle)
        own_bias = total_over("core", own_bias)
        return rows, own_bias + xor_permute(own_bias, "z", 1)

    near, got, last = scatter_core([item[1] for item in backs], [item[2] for item in backs])
    grad_packed, last, grad_ffn = tie(grad_packed, last, grad_ffn)
    grad_packed = scatter_layers(grad_packed)
    state = scatter_diagonal(near, got, last, rows_of_output)
    output, bias_all = state[2]
    sends, grad_ffn, grad_out = tie(sent(state), grad_ffn, grad_out)
    grad_ffn_w, grad_down = part_grads(grad_ffn, plane * slab, unit, width)
    grad_ffn_w = all_to_all(grad_ffn_w.reshape(plane, slab, 2 * share), members)
    arrived, bias_all = tie(received(state, sends), total_over("z", bias_all, 2))
    (stream_grad,) = norm_back(state[0], arrived, middle_grad, own, gain_one, (BF16,))
    stream_grad, bias_all = tie(stream_grad, bias_all)
    returned = jnp.concatenate([output, stream_grad], axis=0).reshape(2 * micro, -1, width)
    returned = rows_from_layer(returned)
    grad_bias = total_over("q", total_over("p", bias_all))
    returned, grad_packed, grad_bias = tie(returned, grad_packed, grad_bias)
    if aligned:
        grad_out = scatter_layers(grad_out.reshape(nf * slab, width))
    grad_packed = all_to_all(grad_packed.reshape(plane, slab, -1), members)
    returned, grad_packed = tie(returned, grad_packed)
    returned, grad_out = tie(rows_from_plane(returned), grad_out)
    output, input_grad = returned[:micro], returned[micro:].astype(F32)

    grad_gate, grad_up, sums_two = unpack_hidden(grad_ffn_w, (w_gate, w_up), nz)
    if not aligned:
        spread = jnp.zeros((own_heads * depth * plane, width), BF16)
        spread = lax.dynamic_update_slice_in_dim(spread, grad_out, own_block * columns, 0)
        grad_out = lax.psum_scatter(spread[:width], everywhere, scatter_dimension=0, tiled=True)
    grad_out = grad_out.astype(F32)
    grad_down = grad_down.astype(F32)
    grad_query, grad_key, grad_value, grad_outgate, sums_one = unpack_heads(
        grad_packed, (w_query, w_key, w_value, w_outgate), nf, columns
    )
    grad_forget = lax.dot_general(
        grad_packed[:, :, :128], select.reshape(heads, plane, 128), (((0, 2), (1, 2)), ((), ())),
        preferred_element_type=F32,
    )
    sums_one = sums_one[:, 0] + jnp.sum(forget_weight.astype(F32) * grad_forget, axis=1)
    grad_gain_one = sums_one / norm1_gain.astype(F32)
    grad_gain_two = sums_two[:, 0] / norm2_gain.astype(F32)
    return (
        output[:, None], input_grad[:, None], grad_gain_one, grad_query, grad_key, grad_value, grad_outgate,
        grad_out, grad_forget, grad_bias, grad_gain_two, grad_gate, grad_up, grad_down,
    )


def solution(mesh):
    n_ctx, n_fsdp = mesh.shape["ctx"], mesh.shape["fsdp"]
    fine = Mesh(mesh.devices.reshape(n_ctx // 2, 2, n_fsdp // 2, 2), ("z", "core", "p", "q"))
    ctx, fsdp, every = ("z", "core"), ("p", "q"), ("z", "core", "p", "q")
    rows = P(None, fsdp, ctx, None)
    vector, matrix = P(every), P(every, None)
    return jax.shard_map(
        per_device,
        mesh=fine,
        in_specs=(
            rows, rows, P(None, fsdp, None), P(), vector, matrix, matrix, matrix, matrix, matrix, matrix, P(),
            vector, matrix, matrix, matrix,
        ),
        out_specs=(
            rows, rows, vector, matrix, matrix, matrix, matrix, matrix, matrix, P(), vector, matrix, matrix, matrix,
        ),
        check_vma=False,
    )
```

```python
import functools

import jax
import jax.numpy as jnp
from jax import lax
from jax.experimental import pallas as pl
from jax.experimental.pallas import tpu as pltpu
from jax.sharding import Mesh, PartitionSpec as P

EPS = 1e-06
LOW = -1e30
BQ = 256
F32 = jnp.float32
BF16 = jnp.bfloat16
VMEM_LIMIT = 56 * 1024 * 1024


def dot(left, right, contract=((1,), (0,)), out=F32):
    return lax.dot_general(left, right, (contract, ((), ())), preferred_element_type=out)


def xor_permute(x, axis, step):
    n = lax.axis_size(axis)
    return lax.ppermute(x, axis, [(i, i ^ step) for i in range(n)])


def pick(stacked, index):
    return lax.dynamic_index_in_dim(stacked, index, 0, keepdims=False)


def xor_plane(x, step):
    n = lax.axis_size("p") * lax.axis_size("q")
    return lax.ppermute(x, ("p", "q"), [(i, i ^ step) for i in range(n)])


def rows_to_plane(x):
    nf = lax.axis_size("p") * lax.axis_size("q")
    f = lax.axis_index(("p", "q"))
    micro, tokens, width = x.shape
    parts = x.reshape(micro, nf, tokens // nf, width).transpose(1, 0, 2, 3)
    return jnp.stack([pick(parts, f)] + [xor_plane(pick(parts, f ^ k), k) for k in range(1, nf)])


def rows_to_layer(got):
    nz = lax.axis_size("z")
    f, z = lax.axis_index(("p", "q")), lax.axis_index("z")
    return [pick(got, f ^ z)] + [xor_permute(pick(got, f ^ z ^ k), "z", k) for k in range(1, nz)]


def rows_from_layer(y):
    nz = lax.axis_size("z")
    micro, rows, width = y.shape
    rp = rows // nz
    return [y[:, :rp]] + [xor_permute(y[:, k * rp:(k + 1) * rp], "z", k) for k in range(1, nz)]


def rows_from_plane(got):
    nf = lax.axis_size("p") * lax.axis_size("q")
    f, z = lax.axis_index(("p", "q")), lax.axis_index("z")
    got = jnp.stack(got)
    back = [pick(got, z ^ f)] + [xor_plane(pick(got, z ^ f ^ k), k) for k in range(1, nf)]
    back = jnp.stack(back)
    return jnp.concatenate([pick(back, f ^ c) for c in range(nf)], axis=1)


def gather_first(x):
    np_ = lax.axis_size("p")
    return [x, xor_permute(x, "q", 1)] + [xor_permute(x, "p", k) for k in range(1, np_)]


def gather_own_core(first):
    np_ = lax.axis_size("p")
    x, over_q = first[:2]
    half = x.shape[0] // 2
    if np_ == 2:
        over_p = first[2]
        own = [x, over_q, over_p, [xor_permute(over_q[:half], "p", 1), xor_permute(over_p[half:], "q", 1)]]
    else:
        own = [x, over_q]
        for k in range(1, np_):
            own += [first[1 + k], xor_permute(over_q, "p", k)]
    return own


def gather_both_cores(own):
    return own + jax.tree.map(lambda block: xor_permute(block, "core", 1), own)


def gather_rest(first):
    return gather_both_cores(gather_own_core(first))


def gather_plane(x):
    return gather_rest(gather_first(x))


def in_rows(blocks):
    return jnp.concatenate(jax.tree.leaves(blocks), axis=0)


def add_up(*parts):
    return sum(part.astype(F32) for part in parts)


def term(items, number=None):
    operands = []
    for item in items:
        if number is None:
            operands.append((item, pl.BlockSpec(item.shape, lambda i: (0, 0))))
        else:
            operands.append((item, pl.BlockSpec((None,) + item.shape[1:], lambda i: (number, 0, 0))))
    return operands


def read_term(refs):
    parts = [ref[...].astype(F32) for ref in refs]
    return parts[0] if len(parts) == 1 else jnp.concatenate(parts, axis=0)


def rows_kernel(body, terms, outs, name):
    counts = [len(item) for item in terms]
    operands = [pair for item in terms for pair in item]

    def kernel(*refs):
        values, at = [], 0
        for count in counts:
            values.append(read_term(refs[at:at + count]))
            at += count
        for ref, value in zip(refs[at:], body(*values)):
            ref[...] = value.astype(ref.dtype)

    return pl.pallas_call(
        kernel,
        grid=(1,),
        in_specs=[spec for _, spec in operands],
        out_specs=[pl.BlockSpec(shape, lambda i: (0, 0)) for shape, _ in outs],
        out_shape=[jax.ShapeDtypeStruct(shape, kind) for shape, kind in outs],
        compiler_params=pltpu.CompilerParams(vmem_limit_bytes=VMEM_LIMIT),
        name=name,
    )(*[array for array, _ in operands])


def scatter_core(far, near):
    got = [xor_permute(item, "core", 1) for item in far]
    last = 2 * lax.axis_size("p") - 1
    rows, width = sum(item.shape[1] for item in near), near[0].shape[2]
    half = rows // 2

    def body(one, other):
        total = one + other
        return total[:half], total[half:]

    return near, got, rows_kernel(body, [term(near, last), term(got, last)], [((half, width), BF16)] * 2, "sum_last")


def both_cores(near, got, number):
    return jnp.concatenate([add_up(one[number], other[number]) for one, other in zip(near, got)], axis=0)


def scatter_diagonal(near, got, last, beside=None):
    np_ = lax.axis_size("p")
    near, got, last = lax.optimization_barrier((near, got, last))
    made = ()
    if np_ == 2:
        into_q = xor_permute(last[0], "p", 1)
        into_p = xor_permute(last[1], "q", 1)
        if beside is not None:
            into_q, into_p, made = lax.optimization_barrier((into_q, into_p, beside(last)))
        half, width = last[0].shape

        def body(near_q, got_q, near_p, got_p, into_q, into_p):
            to_q, to_p = near_q + got_q, near_p + got_p
            to_q = jnp.concatenate([to_q[:half] + into_q, to_q[half:]], axis=0)
            return to_q, jnp.concatenate([to_p[:half], to_p[half:] + into_p], axis=0)

        to_q, to_p = rows_kernel(
            body, [term(near, 1), term(got, 1), term(near, 2), term(got, 2), term([into_q]), term([into_p])],
            [((2 * half, width), BF16)] * 2, "sum_next",
        )
        return [(near, 0), (got, 0)], [(to_q, "q"), (to_p, "p")], made
    if beside is not None:
        made = beside(last)
    last = jnp.concatenate(last, axis=0)
    pair = [both_cores(near, got, 0), both_cores(near, got, 1)]
    for k in range(1, np_):
        for side in range(2):
            item = last if 2 * k + side == 2 * np_ - 1 else both_cores(near, got, 2 * k + side).astype(BF16)
            pair[side] = pair[side] + xor_permute(item, "p", k).astype(F32)
    return [([pair[0]], None)], [(pair[1].astype(BF16), "q")], made


def scatter_first(far, near, beside=None):
    return scatter_diagonal(*scatter_core(far, near), beside)


def sent(state):
    return [item for item, _ in state[1]]


def received(state, sends):
    return [xor_permute(item, axis, 1) for item, (_, axis) in zip(sends, state[1])]


def sum_terms(parts, arrived):
    return [term(*part) for part in parts] + [term([item]) for item in arrived]


def normed_rows(x):
    return x * lax.rsqrt(jnp.mean(x * x, axis=-1, keepdims=True) + EPS)


def add_and_norm(parts, arrived, own, gain):
    terms = sum_terms(parts, arrived)

    def body(own, gain, *values):
        total = own + sum(values)
        return total, normed_rows(total) * gain

    return rows_kernel(body, [term([own]), term([gain])] + terms, [(own.shape, F32), (own.shape, BF16)], "add_norm")


def norm_back(parts, arrived, above, x, gain, kinds):
    terms = sum_terms(parts, arrived)

    def body(above, x, gain, *values):
        r = lax.rsqrt(jnp.mean(x * x, axis=-1, keepdims=True) + EPS)
        unit, scaled = x * r, sum(values) * gain
        total = above + r * (scaled - unit * jnp.mean(scaled * unit, axis=-1, keepdims=True))
        return [total] * len(kinds)

    return rows_kernel(
        body, [term([above]), term([x]), term([gain])] + terms, [(x.shape, kind) for kind in kinds], "norm_back"
    )


def add_rows(parts, arrived, own):
    return rows_kernel(
        lambda *values: [sum(values)], [term([own])] + sum_terms(parts, arrived), [(own.shape, BF16)], "add_rows"
    )[0]


def total_over(axis, x, step=1):
    while step < lax.axis_size(axis):
        x = x + xor_permute(x, axis, step)
        step *= 2
    return x


def log_sigmoid(z):
    return jnp.minimum(z, 0.0) - jnp.log(1.0 + jnp.exp(-jnp.abs(z)))


def window_of(i, bq, window):
    first = max(0, i * bq - window)
    return first, (i + 1) * bq - first


def pieces(members, rows, chunk):
    per = rows // chunk
    return [(j * per + k, j, k * chunk) for j in range(members) for k in range(per)]


def natural_rows(table, number, chunk):
    return pl.ds(pl.multiple_of(table[number] * chunk, chunk), chunk)


def spread_rows(table, source, far_ref, near_ref, chunk):
    half = near_ref.shape[0]
    for number, j, at in pieces(2 * half, near_ref.shape[1], chunk):
        target = near_ref if j < half else far_ref
        target[j % half, at:at + chunk, :] = source[natural_rows(table, number, chunk), :]


def attend_kernel(heads, depth, chunk, members, table, *refs):
    x_refs, refs = refs[:members], refs[members:]
    w_ref, bias_ref, begin_ref = refs[:3]
    h_ref, qkv_ref, g_ref, z_ref, a_ref, total_ref, cumul_ref, b_ref, gain_ref = refs[-13:-4]
    ka, va, rows, part = refs[-4:]
    total = total_ref.shape[0]
    columns = heads * depth
    bq = min(BQ, total)
    window = total // 2
    scale = jnp.asarray(depth ** -0.5, BF16)
    for number, j, at in pieces(members, x_refs[0].shape[0], chunk):
        part[natural_rows(table, number, chunk), :] = x_refs[j][at:at + chunk, :]
    gains = jnp.transpose(w_ref[:, 0:128].astype(F32))[2 * heads:2 * heads + 2, :]
    gain_ref[...] = jnp.concatenate([gains, jnp.zeros((6, gains.shape[1]), F32)], axis=0)
    gain = gains[0:1, :]
    lower = (
        lax.broadcasted_iota(jnp.int32, (bq, bq), 0) >= lax.broadcasted_iota(jnp.int32, (bq, bq), 1)
    ).astype(F32).astype(BF16)
    carry = jnp.zeros((1, 128), F32)
    for i in range(total // bq):
        here = slice(i * bq, (i + 1) * bq)
        values = part[here, :].astype(F32)
        values = values * lax.rsqrt(jnp.mean(values * values, axis=1, keepdims=True) + EPS) * gain
        h_ref[here, :] = values.astype(BF16)
        tile = dot(h_ref[here, :], w_ref[...])
        logit = tile[:, 0:128] + bias_ref[...]
        z_ref[here, :] = logit
        cumul = dot(lower, log_sigmoid(logit).astype(BF16)) + carry
        cumul_ref[here, :] = cumul
        carry = cumul[bq - 1:bq, :]
        qkv_ref[here, :] = tile[:, 128:128 + 3 * columns].astype(BF16)
        g_ref[here, :] = tile[:, 128 + 3 * columns:]
        for h in range(heads):
            lo = 128 + columns + h * depth
            ka[h, here, :] = tile[:, lo:lo + depth].astype(BF16)
            lo += columns
            va[h, here, 0:depth] = tile[:, lo:lo + depth].astype(BF16)
            va[h, here, depth:] = jnp.ones((bq, 128 - depth), BF16)
    rows[...] = jnp.transpose(cumul_ref[...])
    lane = lax.broadcasted_iota(jnp.int32, (bq, 128), 1)
    for i in range(total // bq):
        first, span = window_of(i, bq, window)
        here = slice(i * bq, (i + 1) * bq)
        place = i * bq + lax.broadcasted_iota(jnp.int32, (bq, span), 0)
        other = first + lax.broadcasted_iota(jnp.int32, (bq, span), 1)
        mask = jnp.where((other <= place) & (other >= begin_ref[here, :]), 0.0, LOW)
        totals = jnp.zeros((bq, 128), F32)
        for h in range(heads):
            query = qkv_ref[here, h * depth:(h + 1) * depth] * scale
            score = dot(query, ka[h, first:first + span, :], ((1,), (1,)))
            score = score - rows[h:h + 1, first:first + span] + mask
            peak = jnp.max(score, axis=1, keepdims=True)
            weight = jnp.exp(score - peak)
            both = dot(weight.astype(BF16), va[h, first:first + span, :])
            a_ref[here, h * depth:(h + 1) * depth] = both[:, 0:depth] / both[:, depth:2 * depth]
            totals = jnp.where(lane == h, peak + jnp.log(both[:, depth:depth + 1]), totals)
        total_ref[here, :] = totals
        part[here, 0:columns] = (a_ref[here, :] * jax.nn.sigmoid(g_ref[here, :])).astype(BF16)
    for number, j, at in pieces(members, b_ref.shape[1], chunk):
        b_ref[j, at:at + chunk, :] = part[natural_rows(table, number, chunk), 0:columns]


def attend_back_kernel(heads, depth, chunk, members, streams, held, table, *refs):
    x_refs, refs = refs[:members], refs[members:]
    extra = members * max(0, streams - 1)
    other_refs, gated_refs, refs = refs[:extra], refs[extra:extra + streams], refs[extra + streams:]
    w_ref, o_ref, qkv_ref, g_ref, z_ref, a_ref, total_ref, cumul_ref, begin_ref = refs[:9]
    refs = refs[held:]
    right_ref, far_ref, near_ref, dbias_ref = refs[9:13]
    part, below_grad, qa, ka, va, da, dkn, dvn, rows, deltas, dcumul = refs[-11:]
    if streams:
        out_grad = jnp.zeros(refs[13].shape, F32)
        for number, ref in enumerate(x_refs + other_refs):
            out_grad = out_grad + dot(gated_refs[number // members][number % members], ref[...], ((0,), (0,)))
        refs[13][...] = out_grad.astype(BF16)
    total = total_ref.shape[0]
    columns = heads * depth
    bq = min(BQ, total)
    window = total // 2
    scale = jnp.asarray(depth ** -0.5, BF16)
    lane = lax.broadcasted_iota(jnp.int32, (bq, 128), 1)
    per = x_refs[0].shape[0] // chunk
    for j in range(members):
        grad = dot(x_refs[j][...], o_ref[...], ((1,), (1,)))
        for k in range(per):
            below_grad[natural_rows(table, j * per + k, chunk), :] = grad[k * chunk:(k + 1) * chunk, :]
    dkn[...] = jnp.zeros_like(dkn)
    dvn[...] = jnp.zeros_like(dvn)
    for i in range(total // bq):
        here = slice(i * bq, (i + 1) * bq)
        grad = below_grad[here, :]
        opened = jax.nn.sigmoid(g_ref[here, :])
        attended = a_ref[here, :]
        below = (grad * opened).astype(BF16)
        right_ref[here, 128 + 3 * columns:] = (grad * attended * opened * (1.0 - opened)).astype(BF16)
        product = below.astype(F32) * attended
        delta = jnp.zeros((bq, 128), F32)
        for h in range(heads):
            da[h, here, :] = below[:, h * depth:(h + 1) * depth]
            delta = jnp.where(
                lane == h, jnp.sum(product[:, h * depth:(h + 1) * depth], axis=1, keepdims=True), delta
            )
            qa[h, here, 0:depth] = qkv_ref[here, h * depth:(h + 1) * depth] * scale
            qa[h, here, depth:] = jnp.ones((bq, 128 - depth), BF16)
            lo = columns + h * depth
            ka[h, here, 0:depth] = qkv_ref[here, lo:lo + depth]
            ka[h, here, depth:] = jnp.ones((bq, 128 - depth), BF16)
            lo += columns
            va[h, here, :] = qkv_ref[here, lo:lo + depth]
        dcumul[here, :] = delta
    deltas[...] = jnp.transpose(dcumul[...])
    rows[...] = jnp.transpose(total_ref[...])
    dcumul[...] = jnp.zeros_like(dcumul)
    for i in range(total // bq):
        first, span = window_of(i, bq, window)
        here, there = slice(i * bq, (i + 1) * bq), slice(first, first + span)
        place = i * bq + lax.broadcasted_iota(jnp.int32, (span, bq), 1)
        other = first + lax.broadcasted_iota(jnp.int32, (span, bq), 0)
        mask = jnp.where((other <= place) & (other >= begin_ref[:, here]), 0.0, LOW)
        for h in range(heads):
            query, below = qa[h, here, :], da[h, here, :]
            score = dot(ka[h, there, 0:depth], query[:, 0:depth], ((1,), (1,)))
            score = score - rows[h:h + 1, here] - cumul_ref[there, h:h + 1] + mask
            weight = jnp.exp(score)
            weight_grad = dot(va[h, there, :], below, ((1,), (1,))) - deltas[h:h + 1, here]
            score_grad = (weight * weight_grad).astype(BF16)
            dvn[h, there, :] += dot(weight.astype(BF16), below)
            dkn[h, there, :] += dot(score_grad, query)
            dq = dot(score_grad, ka[h, there, :], ((0,), (0,)))
            right_ref[here, 128 + h * depth:128 + (h + 1) * depth] = (dq[:, 0:depth] * depth ** -0.5).astype(BF16)
            mine = (lane == h) | (lane == h + heads)
            dcumul[here, :] += jnp.where(mine, dq[:, depth:depth + 1], 0.0)
    upper = (
        lax.broadcasted_iota(jnp.int32, (bq, bq), 0) <= lax.broadcasted_iota(jnp.int32, (bq, bq), 1)
    ).astype(F32)
    carry = jnp.zeros((1, 128), F32)
    sums = jnp.zeros((1, 128), F32)
    for i in reversed(range(total // bq)):
        here = slice(i * bq, (i + 1) * bq)
        change = dcumul[here, :]
        for h in range(heads):
            lo = 128 + columns + h * depth
            right_ref[here, lo:lo + depth] = dkn[h, here, 0:depth].astype(BF16)
            lo += columns
            right_ref[here, lo:lo + depth] = dvn[h, here, :].astype(BF16)
            mine = (lane == h) | (lane == h + heads)
            change = change - jnp.where(mine, dkn[h, here, depth:depth + 1], 0.0)
        summed = carry + jnp.dot(upper, change, precision=lax.Precision.HIGHEST, preferred_element_type=F32)
        carry = summed[0:1, :]
        grad = summed * jax.nn.sigmoid(-z_ref[here, :])
        sums = sums + jnp.sum(grad, axis=0, keepdims=True)
        high = grad.astype(BF16).astype(F32)
        pair = jnp.where(lane < heads, high, jnp.where(lane < 2 * heads, grad - high, 0.0))
        right_ref[here, 0:128] = pair.astype(BF16)
        part[here, :] = dot(right_ref[here, :], w_ref[...], ((1,), (1,))).astype(BF16)
    dbias_ref[...] = jnp.broadcast_to(sums, dbias_ref.shape)
    spread_rows(table, part, far_ref, near_ref, chunk)


def one_stream(blocks, m, streams):
    arrays, specs = [], []
    for block in blocks:
        array, place = (block[m], 0) if isinstance(block, list) else (block, m)
        rows, width = (array.shape[0] if isinstance(block, list) else array.shape[0] // streams), array.shape[1]
        arrays.append(array)
        specs.append(pl.BlockSpec((rows, width), lambda i, t, place=place: (place, 0), pipeline_mode=pl.Buffered(1)))
    return arrays, specs


def fixed(array):
    return pl.BlockSpec(array.shape, lambda i, t: (0,) * array.ndim, pipeline_mode=pl.Buffered(1))


def own_part(shape, m):
    return pl.BlockSpec(shape, lambda i, t: (m, 0), pipeline_mode=pl.Buffered(1))


def attend(table, blocks, m, streams, weights, bias, begin, into, heads, depth, chunk):
    arrays, specs = one_stream(blocks, m, streams)
    members, (rows, width) = len(arrays), specs[0].block_shape
    total = begin.shape[0]
    columns = heads * depth
    begin = begin[:, None]
    into = [] if into is None else [into]
    outs = [
        ((streams * total, width), BF16), ((total, 3 * columns), BF16), ((total, columns), F32), ((total, 128), F32),
        ((total, columns), F32), ((total, 128), F32), ((total, 128), F32), ((members, rows, columns), BF16),
        ((8, width), F32),
    ]
    out_shape = [jax.ShapeDtypeStruct(shape, kind) for shape, kind in outs]
    return pl.pallas_call(
        functools.partial(attend_kernel, heads, depth, chunk, members),
        grid_spec=pltpu.PrefetchScalarGridSpec(
            num_scalar_prefetch=1,
            grid=(1,),
            in_specs=specs + [fixed(weights), fixed(bias), fixed(begin)] + [pl.BlockSpec(memory_space=pl.ANY)] * len(into),
            out_specs=[own_part((total, width), m)] + [fixed(item) for item in out_shape[1:]],
            scratch_shapes=[
                pltpu.VMEM((heads, total, depth), BF16),
                pltpu.VMEM((heads, total, 128), BF16),
                pltpu.VMEM((128, total), F32),
                pltpu.VMEM((total, width), BF16),
            ],
        ),
        out_shape=out_shape,
        compiler_params=pltpu.CompilerParams(vmem_limit_bytes=VMEM_LIMIT),
        input_output_aliases={1 + members + 3: 0} if into else {},
        cost_estimate=pl.CostEstimate(flops=14 * 10 ** 9, bytes_accessed=10 ** 7, transcendentals=0),
        name="attend",
    )(table, *arrays, weights, bias, begin, *into)


def attend_back(table, blocks, m, streams, weights, out_w, kept, begin, gated, into, heads, depth, chunk):
    arrays, specs = one_stream(blocks, m, streams)
    members, (rows, width) = len(arrays), specs[0].block_shape
    total = begin.shape[0]
    columns = heads * depth
    begin = begin[None, :]
    gated = [] if gated is None else gated
    into = [] if into is None else [into]
    for other in range(1, len(gated)):
        other_arrays, other_specs = one_stream(blocks, other, streams)
        arrays, specs = arrays + other_arrays, specs + other_specs
    outs = [
        ((streams * total, 128 + 4 * columns), BF16), ((members // 2, rows, width), BF16), ((members // 2, rows, width), BF16),
        ((8, 128), F32),
    ] + [((columns, width), BF16)] * (len(gated) > 0)
    out_shape = [jax.ShapeDtypeStruct(shape, kind) for shape, kind in outs]
    return pl.pallas_call(
        functools.partial(attend_back_kernel, heads, depth, chunk, members, len(gated), len(into)),
        grid_spec=pltpu.PrefetchScalarGridSpec(
            num_scalar_prefetch=1,
            grid=(1,),
            in_specs=specs + [fixed(item) for item in (*gated, weights, out_w, *kept, begin)]
            + [pl.BlockSpec(memory_space=pl.ANY)] * len(into),
            out_specs=[own_part((total, 128 + 4 * columns), m)] + [fixed(item) for item in out_shape[1:]],
            scratch_shapes=[
                pltpu.VMEM((total, width), BF16),
                pltpu.VMEM((total, columns), F32),
                pltpu.VMEM((heads, total, 128), BF16),
                pltpu.VMEM((heads, total, 128), BF16),
                pltpu.VMEM((heads, total, depth), BF16),
                pltpu.VMEM((heads, total, depth), BF16),
                pltpu.VMEM((heads, total, 128), F32),
                pltpu.VMEM((heads, total, depth), F32),
                pltpu.VMEM((128, total), F32),
                pltpu.VMEM((128, total), F32),
                pltpu.VMEM((total, 128), F32),
            ],
        ),
        out_shape=out_shape,
        compiler_params=pltpu.CompilerParams(vmem_limit_bytes=VMEM_LIMIT),
        input_output_aliases={1 + len(arrays) + len(gated) + 3 + len(kept): 0} if into else {},
        cost_estimate=pl.CostEstimate(flops=20 * 10 ** 9, bytes_accessed=10 ** 7, transcendentals=0),
        name="attend_back",
    )(table, *arrays, *gated, weights, out_w, *kept, begin, *into)


def out_kernel(b_ref, o_ref, far_ref, near_ref):
    half = near_ref.shape[0]
    for j in range(2 * half):
        target = near_ref if j < half else far_ref
        target[j % half] = dot(b_ref[j], o_ref[...]).astype(BF16)


def out_product(gated, weights):
    members, rows, _ = gated.shape
    shape = jax.ShapeDtypeStruct((members // 2, rows, weights.shape[1]), BF16)
    return pl.pallas_call(
        out_kernel,
        out_shape=[shape, shape],
        compiler_params=pltpu.CompilerParams(vmem_limit_bytes=VMEM_LIMIT),
        name="out_product",
    )(gated, weights)


def ffn_kernel(h_ref, e_ref, w_ref, d_ref, *refs):
    m_ref, g_ref, part_ref = refs[-3:]
    down = d_ref[...].reshape(-1, d_ref.shape[-1])
    share = down.shape[0]
    pre = dot(h_ref[...], w_ref[...])
    gate, up = pre[:, :share], pre[:, share:]
    grad = dot(e_ref[...], down, ((1,), (1,)))
    opened = jax.nn.sigmoid(gate)
    silu = gate * opened
    m_ref[...] = (silu * up).astype(BF16)
    g_ref[:, :share] = (grad * up * (opened * (1.0 + gate * (1.0 - opened)))).astype(BF16)
    g_ref[:, share:] = (grad * silu).astype(BF16)
    part_ref[...] = dot(g_ref[...], w_ref[...], ((1,), (1,))).astype(BF16)


def ffn(normed, upstream, weights, down, unit, first, count, into):
    rows, width = normed.shape
    share = down.shape[0] * unit

    def blocks(lanes, shift):
        return pl.BlockSpec((BQ, lanes), lambda i: (i + shift, 0))

    def fixed(shape):
        return pl.BlockSpec(shape, lambda i: (0,) * len(shape), pipeline_mode=pl.Buffered(1))

    kept = [] if into is None else list(into)
    return pl.pallas_call(
        ffn_kernel,
        grid=(count,),
        in_specs=[blocks(width, first), blocks(width, first), fixed(weights.shape), fixed((down.shape[0], unit, width))]
        + [pl.BlockSpec(memory_space=pl.ANY)] * len(kept),
        out_specs=[
            blocks(share, first), blocks(2 * share, first), pl.BlockSpec((None, BQ, width), lambda i: (i, 0, 0)),
        ],
        out_shape=[
            jax.ShapeDtypeStruct((rows, share), BF16),
            jax.ShapeDtypeStruct((rows, 2 * share), BF16),
            jax.ShapeDtypeStruct((count, BQ, width), BF16),
        ],
        input_output_aliases={4 + i: i for i in range(len(kept))},
        compiler_params=pltpu.CompilerParams(vmem_limit_bytes=VMEM_LIMIT),
        cost_estimate=pl.CostEstimate(
            flops=10 * count * BQ * width * share, bytes_accessed=count * BQ * width * 8, transcendentals=0
        ),
        name="ffn",
    )(normed, upstream, weights, down, *kept)


def layout(body, shapes, kind, *arrays):
    kinds = kind if isinstance(kind, list) else [kind] * len(shapes)
    out_shape = [jax.ShapeDtypeStruct(shape, own) for shape, own in zip(shapes, kinds)]
    return pl.pallas_call(body, out_shape=out_shape, name="layout")(*arrays)


def block_columns(block, columns, limit):
    return min(block * columns, limit), max(0, min((block + 1) * columns, limit) - min(block * columns, limit))


def pack_heads(forget, weights, nf, columns):
    slab, width = weights[0].shape
    plane = 2 * nf

    def body(f_ref, *refs):
        out = refs[-1]
        for t in range(plane):
            out[t, :, 0:128] = f_ref[:, t * 128:(t + 1) * 128]
            first, count = block_columns(t % nf * 2 + t // nf, columns, width)
            for number, ref in enumerate(refs[:-1]):
                lo = 128 + number * columns
                if count < columns:
                    out[t, :, lo:lo + columns] = jnp.zeros((slab, columns), BF16)
                if count:
                    out[t, :, lo:lo + count] = ref[:, first:first + count]

    return layout(body, [(plane, slab, 128 + 4 * columns)], BF16, forget, *weights)[0]


def unpack_heads(grads, weights, nf, columns):
    plane, slab, _ = grads.shape
    width = weights[0].shape[1]

    def body(x_ref, *refs):
        sums = jnp.zeros((slab, 1), F32)
        for number in range(4):
            weight, out = refs[number], refs[4 + number]
            for t in range(plane):
                first, count = block_columns(t % nf * 2 + t // nf, columns, width)
                lo = 128 + number * columns
                if count:
                    out[:, first:first + count] = x_ref[t, :, lo:lo + count].astype(F32)
            sums = sums + jnp.sum(weight[...].astype(F32) * out[...], axis=1, keepdims=True)
        refs[8][...] = sums

    return layout(body, [(slab, width)] * 4 + [(slab, 1)], F32, grads, *weights)


def pack_hidden(gate, up, nz, plane):
    slab, hidden = gate.shape
    unit = hidden // (nz * plane)

    def body(gate_ref, up_ref, out):
        for number, ref in enumerate((gate_ref, up_ref)):
            for t in range(plane):
                for z in range(nz):
                    lo = (number * nz + z) * unit
                    at = (z * plane + t) * unit
                    out[t, :, lo:lo + unit] = ref[:, at:at + unit]

    return layout(body, [(plane, slab, 2 * nz * unit)], BF16, gate, up)[0]


def unpack_hidden(grads, weights, nz):
    plane, slab, both = grads.shape
    unit = both // (2 * nz)

    def body(x_ref, *refs):
        sums = jnp.zeros((slab, 1), F32)
        for number in range(2):
            weight, out = refs[number], refs[2 + number]
            for t in range(plane):
                for z in range(nz):
                    lo = (number * nz + z) * unit
                    at = (z * plane + t) * unit
                    out[:, at:at + unit] = x_ref[t, :, lo:lo + unit].astype(F32)
            sums = sums + jnp.sum(weight[...].astype(F32) * out[...], axis=1, keepdims=True)
        refs[4][...] = sums

    return layout(body, [(slab, plane * nz * unit)] * 2 + [(slab, 1)], F32, grads, *weights)


def doc_begins(lengths_row, total):
    ends = jnp.cumsum(lengths_row)
    begins = ends - lengths_row
    place = jnp.arange(total, dtype=jnp.int32)
    inside = (place[:, None] >= begins[None, :]) & (place[:, None] < ends[None, :])
    return jnp.sum(jnp.where(inside, begins[None, :], 0), axis=1)


def all_to_all(x, axes):
    return lax.all_to_all(x, axes, split_axis=0, concat_axis=0, tiled=True)


def scatter_layers(grad):
    return lax.psum_scatter(grad, "z", scatter_dimension=0, tiled=True)


def join_grads(grad, down, nz):
    lanes, width = grad.shape[1], down.shape[1]
    grad, down = grad.reshape(nz, -1, lanes), down.reshape(nz, -1, width)
    parts = [grad] + [down[:, :, i * lanes:(i + 1) * lanes] for i in range(width // lanes)]
    rest = width % lanes
    if rest:
        count = lanes // rest
        rows = down.shape[1] // count
        over = down[:, :, width - rest:].reshape(nz, count, rows, rest)
        parts.append(jnp.concatenate([over[:, i] for i in range(count)], axis=2))
    return jnp.concatenate(parts, axis=1).reshape(-1, lanes)


def part_grads(joined, slabs, rows, width):
    lanes = joined.shape[1]
    grad, joined = joined[:slabs], joined[slabs:]
    whole = width // lanes
    parts = [joined[i * rows:(i + 1) * rows] for i in range(whole)]
    rest = width % lanes
    if rest:
        over = joined[whole * rows:]
        parts.append(jnp.concatenate([over[:, i * rest:(i + 1) * rest] for i in range(lanes // rest)], axis=0))
    return grad, jnp.concatenate(parts, axis=1)


def tie(*values):
    return lax.optimization_barrier(values)


def per_device(
    inputs, cotangent, lengths, deal, norm1_gain, w_query, w_key, w_value, w_outgate, w_out,
    forget_weight, forget_bias, norm2_gain, w_gate, w_up, w_down,
):
    nz, np_, nq = lax.axis_size("z"), lax.axis_size("p"), lax.axis_size("q")
    z, core, f = lax.axis_index("z"), lax.axis_index("core"), lax.axis_index(("p", "q"))
    nf = np_ * nq
    n_ctx = 2 * nz
    plane = 2 * nf
    devices = nz * plane
    everywhere, members = ("z", "core", "p", "q"), ("core", "p", "q")
    micro, _, tokens, width = inputs.shape
    heads = forget_bias.shape[0]
    depth = width // heads
    own_heads = -(-heads // plane)
    columns = own_heads * depth
    spare_heads = own_heads * plane - heads
    total = tokens * n_ctx
    chunk = tokens // nf
    block = tokens // 2
    hidden = w_gate.shape[1]
    slab = w_query.shape[0]
    unit = hidden // devices
    share = nz * unit
    own_block = f * 2 + core
    aligned = spare_heads == 0 and columns == nf * slab

    member_block = [t % nf * 2 + t // nf for t in range(plane)]
    head_of = jnp.arange(heads, dtype=jnp.int32)[:, None]
    lane_of = jnp.arange(plane * 128, dtype=jnp.int32)[None, :]
    lane_head = jnp.asarray(member_block, jnp.int32)[lane_of // 128] * own_heads + lane_of % 128 % own_heads
    select = ((lane_head == head_of) & (lane_of % 128 < 2 * own_heads)).astype(BF16)
    first_lanes = dot(forget_weight, select, out=BF16)
    for number, gain in enumerate((norm1_gain, norm2_gain)):
        first_lanes = jnp.where(lane_of % 128 == 2 * own_heads + number, gain[:, None], first_lanes)
    packed = pack_heads(first_lanes, (w_query, w_key, w_value, w_outgate), nf, columns)
    own, w_out = tie(rows_to_plane(inputs[:, 0]), w_out)
    own = rows_to_layer(own)
    packed, own[1] = tie(packed, own[1])
    packed = all_to_all(packed, members)
    if aligned:
        out_w = jnp.stack([w_out] + [xor_permute(w_out, "z", k) for k in range(1, nz)])
        out_w = jnp.stack([pick(out_w, z ^ c) for c in range(nz)])
    else:
        out_w = jnp.pad(lax.all_gather(w_out, everywhere, axis=0, tiled=True), ((0, spare_heads * depth), (0, 0)))
        out_w = lax.dynamic_slice_in_dim(out_w, own_block * columns, columns, 0)
    own = jnp.concatenate(own, axis=1).reshape(-1, width)
    packed, own, out_w = tie(packed, own, out_w)
    packed = lax.all_gather(packed, "z", axis=0).reshape(width, -1)
    gathered = gather_first(own)
    ffn_send, gathered = tie(pack_hidden(w_gate, w_up, nz, plane), gathered)
    gathered = gather_rest(gathered)
    if aligned:
        out_w = all_to_all(out_w, ("p", "q")).reshape(columns, width)
    ffn_w = all_to_all(ffn_send, members)
    out_w, ffn_w, gathered, cotangent = tie(out_w, ffn_w, gathered, cotangent)
    upstream_own = rows_to_plane(cotangent[:, 0])
    packed, upstream_own = tie(packed, upstream_own)
    upstream_own = jnp.concatenate(rows_to_layer(upstream_own), axis=1).reshape(-1, width)

    lengths_own = lax.ppermute(
        lengths[:, 0], everywhere,
        [
            (((f_to * 2 + c) * nf) + z_to, ((z_to * 2 + c) * nf) + f_to)
            for z_to in range(nz) for c in range(2) for f_to in range(nf)
        ],
    )
    begins = [doc_begins(lengths_own[m], total) for m in range(micro)]
    number = jnp.arange(total // chunk, dtype=jnp.int32)
    from_core = core ^ (number // (nf * nz))
    from_f = f ^ (number // nz % nf)
    from_z = z ^ (number % nz)
    inside = from_f * chunk

    def natural_table(deal_row):
        dealt = jnp.take(deal_row, from_z * 2 + from_core)
        start = jnp.where(inside < block, dealt, 2 * n_ctx - 1 - dealt) * block + inside % block
        return (start // chunk).astype(jnp.int32)

    tables = [natural_table(deal[m]) for m in range(micro)]
    all_bias = jnp.pad(forget_bias, (0, spare_heads))
    own_bias = lax.dynamic_slice_in_dim(all_bias, own_block * own_heads, own_heads, 0)[None]
    bias_row = jnp.concatenate([own_bias, own_bias, jnp.zeros((1, 128 - 2 * own_heads), F32)], axis=1)

    def attend_stream(m, table, into):
        return attend(table, gathered, m, micro, packed, bias_row, begins[m], into, own_heads, depth, chunk)

    attended = [attend_stream(0, tables[0], None)]
    gains = attended[0][8]
    gated = [attended[0][7]]
    parts = [out_product(gated[0], out_w)]
    table, upstream_own, gains, ffn_w, w_down = tie(tables[1], upstream_own, gains, ffn_w, w_down)
    ffn_w = lax.all_gather(ffn_w, "z", axis=0).reshape(width, 2 * share)
    down_w = lax.all_gather(w_down, "z", axis=0)
    attended.append(attend_stream(1, table, attended[0][0]))
    upstream = gather_first(upstream_own)
    last_gated, upstream = tie(attended[1][7], upstream)
    gated.append(last_gated)
    upstream, last_part = tie(gather_own_core(upstream), out_product(gated[1], out_w))
    parts.append(last_part)
    upstream = in_rows(gather_both_cores(upstream))
    gain_one, gain_two = gains[0:1], gains[1:2]
    state = scatter_first([item[0] for item in parts], [item[1] for item in parts])
    middle, normed_two = add_and_norm(state[0], received(state, sent(state)), own, gain_two)
    normed_two = in_rows(gather_plane(normed_two))

    half_blocks = normed_two.shape[0] // BQ // 2
    weights = (normed_two, upstream, ffn_w, down_w, unit)
    activ, ffn_grad, far = ffn(*weights, half_blocks, half_blocks, None)
    activ, ffn_grad, near = ffn(*weights, 0, half_blocks, (activ, ffn_grad))
    def grad_of_ffn(hold):
        kept, _ = tie(normed_two, hold)
        return dot(kept, ffn_grad, ((0,), (0,)), BF16)

    state = scatter_first([far], [near], grad_of_ffn)
    grad_ffn_w = state[2]
    sends, held = tie(sent(state), activ)
    grad_down = dot(held, upstream, ((0,), (0,)), BF16)
    arrived, grad_ffn = tie(received(state, sends), join_grads(grad_ffn_w, grad_down, nz))
    grad_ffn = scatter_layers(grad_ffn)
    middle_grad, branch_own = norm_back(state[0], arrived, upstream_own, middle, gain_two, (F32, BF16))
    branch_own, held = tie(branch_own, activ)
    half = activ.shape[0] // 2
    down_rows = down_w.reshape(share, width)
    part_out = [
        dot(item, down_rows, out=BF16).reshape(plane // 2, -1, width) for item in (held[half:], held[:half])
    ]
    branch_grad, part_out = tie(gather_first(branch_own), part_out)
    result = scatter_core(part_out[:1], part_out[1:])
    branch_grad = gather_rest(branch_grad)

    def back_stream(m, table, gated, into):
        return attend_back(
            table, branch_grad, m, micro, packed, out_w, attended[m][1:7], begins[m], gated, into, own_heads, depth, chunk
        )

    def first_back(hold):
        table, _ = tie(tables[0], hold)
        return back_stream(0, table, gated, None)

    result = scatter_diagonal(*result, first_back)
    backs = [result[2]]
    sends, table = tie(sent(result), tables[1])
    grad_out = backs[0][4]
    if aligned:
        grad_out = all_to_all(grad_out.reshape(nf, slab, width), ("p", "q"))
    arrived, grad_out, last_back = tie(received(result, sends), grad_out, back_stream(1, table, None, backs[0][0]))
    backs.append(last_back)
    grad_packed = dot(attended[1][0], backs[1][0], ((0,), (0,)), BF16)
    bias_sum = sum(item[3][0] for item in backs)
    bias_all = lax.dynamic_update_slice_in_dim(
        jnp.zeros((own_heads * plane,), F32), bias_sum[:own_heads], own_block * own_heads, 0
    )[:heads]

    def rows_of_output(hold):
        own_arrived, own_bias, _ = tie(arrived, bias_all, hold)
        rows = add_rows(result[0], own_arrived, middle)
        own_bias = total_over("core", own_bias)
        return rows, own_bias + xor_permute(own_bias, "z", 1)

    near, got, last = scatter_core([item[1] for item in backs], [item[2] for item in backs])
    grad_packed, last, grad_ffn = tie(grad_packed, last, grad_ffn)
    grad_packed = scatter_layers(grad_packed)
    state = scatter_diagonal(near, got, last, rows_of_output)
    output, bias_all = state[2]
    sends, grad_ffn, grad_out = tie(sent(state), grad_ffn, grad_out)
    grad_ffn_w, grad_down = part_grads(grad_ffn, plane * slab, unit, width)
    grad_ffn_w = all_to_all(grad_ffn_w.reshape(plane, slab, 2 * share), members)
    arrived, bias_all = tie(received(state, sends), total_over("z", bias_all, 2))
    (stream_grad,) = norm_back(state[0], arrived, middle_grad, own, gain_one, (BF16,))
    stream_grad, bias_all = tie(stream_grad, bias_all)
    returned = jnp.concatenate([output, stream_grad], axis=0).reshape(2 * micro, -1, width)
    returned = rows_from_layer(returned)
    grad_bias = total_over("q", total_over("p", bias_all))
    returned, grad_packed, grad_bias = tie(returned, grad_packed, grad_bias)
    if aligned:
        grad_out = scatter_layers(grad_out.reshape(nf * slab, width))
    grad_packed = all_to_all(grad_packed.reshape(plane, slab, -1), members)
    returned, grad_packed = tie(returned, grad_packed)
    returned, grad_out = tie(rows_from_plane(returned), grad_out)
    output, input_grad = returned[:micro], returned[micro:].astype(F32)

    grad_gate, grad_up, sums_two = unpack_hidden(grad_ffn_w, (w_gate, w_up), nz)
    if not aligned:
        spread = jnp.zeros((own_heads * depth * plane, width), BF16)
        spread = lax.dynamic_update_slice_in_dim(spread, grad_out, own_block * columns, 0)
        grad_out = lax.psum_scatter(spread[:width], everywhere, scatter_dimension=0, tiled=True)
    grad_out = grad_out.astype(F32)
    grad_down = grad_down.astype(F32)
    grad_query, grad_key, grad_value, grad_outgate, sums_one = unpack_heads(
        grad_packed, (w_query, w_key, w_value, w_outgate), nf, columns
    )
    grad_forget = lax.dot_general(
        grad_packed[:, :, :128], select.reshape(heads, plane, 128), (((0, 2), (1, 2)), ((), ())),
        preferred_element_type=F32,
    )
    sums_one = sums_one[:, 0] + jnp.sum(forget_weight.astype(F32) * grad_forget, axis=1)
    grad_gain_one = sums_one / norm1_gain.astype(F32)
    grad_gain_two = sums_two[:, 0] / norm2_gain.astype(F32)
    return (
        output[:, None], input_grad[:, None], grad_gain_one, grad_query, grad_key, grad_value, grad_outgate,
        grad_out, grad_forget, grad_bias, grad_gain_two, grad_gate, grad_up, grad_down,
    )


def solution(mesh):
    n_ctx, n_fsdp = mesh.shape["ctx"], mesh.shape["fsdp"]
    fine = Mesh(mesh.devices.reshape(n_ctx // 2, 2, n_fsdp // 2, 2), ("z", "core", "p", "q"))
    ctx, fsdp, every = ("z", "core"), ("p", "q"), ("z", "core", "p", "q")
    rows = P(None, fsdp, ctx, None)
    vector, matrix = P(every), P(every, None)
    return jax.shard_map(
        per_device,
        mesh=fine,
        in_specs=(
            rows, rows, P(None, fsdp, None), P(), vector, matrix, matrix, matrix, matrix, matrix, matrix, P(),
            vector, matrix, matrix, matrix,
        ),
        out_specs=(
            rows, rows, vector, matrix, matrix, matrix, matrix, matrix, matrix, P(), vector, matrix, matrix, matrix,
        ),
        check_vma=False,
    )
```
